32 devices in a mesh: dp: 4 (over y, x), seq: 2 (over core), head: 4 (over z).
Axes of the slice: x: 2, y: 2, z: 4, core: 2. Of those that a mesh axis runs over, the one named last changes fastest.
Arguments:
- tokens: bfloat16 [4, 1024, 1024], P('dp', 'seq'), may hold values from -6 to 6
- qkv_weight: bfloat16 [2, 1024, 3072], P(None, ('dp', 'seq'), 'head'), may hold values from -0.1875 to 0.1875
- dense_weight: bfloat16 [2, 1024, 1024], P(None, 'head', ('dp', 'seq')), may hold values from -0.75 to 0.75
- up_weight: bfloat16 [2, 1024, 4096], P(None, ('dp', 'seq'), 'head'), may hold values from -0.1875 to 0.1875
- down_weight: bfloat16 [2, 4096, 1024], P(None, 'head', ('dp', 'seq')), may hold values from -0.125 to 0.125
- first_gain: float32 [2, 1024], P(None, ('dp', 'seq')), may hold values from 0.25 to 1.75
- first_shift: float32 [2, 1024], P(None, ('dp', 'seq')), may hold values from -4 to 4
- query_bias: float32 [2, 16, 64], P(None, 'head', ('dp', 'seq')), may hold values from -6 to 6
- value_bias: float32 [2, 16, 64], P(None, 'head', ('dp', 'seq')), may hold values from -6 to 6
- dense_bias: float32 [2, 1024], P(None, ('dp', 'seq')), may hold values from -6 to 6
- second_gain: float32 [2, 1024], P(None, ('dp', 'seq')), may hold values from 0.25 to 1.75
- second_shift: float32 [2, 1024], P(None, ('dp', 'seq')), may hold values from -4 to 4
- up_bias: float32 [2, 16, 256], P(None, 'head', ('dp', 'seq')), may hold values from -6 to 6
- down_bias: float32 [2, 1024], P(None, ('dp', 'seq')), may hold values from -6 to 6
- cotangent: bfloat16 [4, 1024, 1024], P('dp', 'seq'), may hold values from -6 to 6
Outputs:
- output: bfloat16 [4, 1024, 1024], P('dp', 'seq')
- tokens_grad: float32 [4, 1024, 1024], P('dp', 'seq')
- qkv_weight_grad: float32 [2, 1024, 3072], P(None, ('dp', 'seq'), 'head')
- dense_weight_grad: float32 [2, 1024, 1024], P(None, 'head', ('dp', 'seq'))
- up_weight_grad: float32 [2, 1024, 4096], P(None, ('dp', 'seq'), 'head')
- down_weight_grad: float32 [2, 4096, 1024], P(None, 'head', ('dp', 'seq'))
- first_gain_grad: float32 [2, 1024], P(None, ('dp', 'seq'))
- first_shift_grad: float32 [2, 1024], P(None, ('dp', 'seq'))
- query_bias_grad: float32 [2, 16, 64], P(None, 'head', ('dp', 'seq'))
- value_bias_grad: float32 [2, 16, 64], P(None, 'head', ('dp', 'seq'))
- dense_bias_grad: float32 [2, 1024], P(None, ('dp', 'seq'))
- second_gain_grad: float32 [2, 1024], P(None, ('dp', 'seq'))
- second_shift_grad: float32 [2, 1024], P(None, ('dp', 'seq'))
- up_bias_grad: float32 [2, 16, 256], P(None, 'head', ('dp', 'seq'))
- down_bias_grad: float32 [2, 1024], P(None, ('dp', 'seq'))
The draws below stay inside these ranges and needn't reach their ends.
All inputs are finite; a program needn't handle non-finite values.
Results may differ from the reference program's by a relative error of at most 0.035.
Values may be sent and summed in bfloat16 or wider, within the bound.
No kernel may reach another device: no remote copies, remote signals or barrier semaphores. Data moves between devices by JAX's collectives and lax.ppermute only.
A program may use at most 192 MiB of HBM per device.

```python
import math
import jax
import jax.numpy as jnp
from jax import lax

D = 1024
H = 16
HD = 64
FF = 4096
LAYERS = 2
SEQ_LEN = 1024
NSEQ = 4


def level_of(rng, extent, pieces, low, high):
    loudness = 1.0
    for position, parts in pieces:
        steps = jax.random.uniform(jax.random.fold_in(jax.random.fold_in(rng, 6), position), (parts,), jnp.float32, low / len(pieces), high / len(pieces))
        loudness = loudness * jnp.repeat(jnp.exp(steps), extent[position] // parts).reshape((-1,) + (1,) * (len(extent) - 1 - position))
    return loudness


def gaussian(stream_key, extent, deviation, most, cuts=(), kind=jnp.bfloat16):
    array = jax.random.normal(stream_key, extent, jnp.float32) * deviation
    if len(cuts) > 0:
        array = level_of(stream_key, extent, cuts, -0.22, 0.18) * array
    return jnp.clip(array, min=-most, max=most).astype(kind)


def setup_inputs(seed: int = 0) -> dict:
    splits = jax.random.split(jax.random.key(seed), 16)
    return {
        "tokens": gaussian(splits[0], (NSEQ, SEQ_LEN, D), 1.0, 6.0, ((0, 4), (1, 2))),
        "qkv_weight": gaussian(splits[1], (LAYERS, D, 3 * D), D ** -0.5, 0.1875, ((1, 8), (2, 4))),
        "dense_weight": gaussian(splits[2], (LAYERS, D, D), (D // 16) ** -0.5, 0.75, ((1, 4), (2, 8))),
        "up_weight": gaussian(splits[3], (LAYERS, D, FF), D ** -0.5, 0.1875, ((1, 8), (2, 4))),
        "down_weight": gaussian(splits[4], (LAYERS, FF, D), (FF // 2) ** -0.5, 0.125, ((1, 4), (2, 8))),
        "first_gain": jnp.clip(1.0 + 0.15 * jax.random.normal(splits[5], (LAYERS, D), jnp.float32), 0.25, 1.75),
        "first_shift": gaussian(splits[6], (LAYERS, D), 0.3, 4.0, ((1, 8),), jnp.float32),
        "query_bias": gaussian(splits[7], (LAYERS, H, HD), 0.5, 6.0, ((1, 4), (2, 8)), jnp.float32),
        "value_bias": gaussian(splits[8], (LAYERS, H, HD), 0.5, 6.0, ((1, 4), (2, 8)), jnp.float32),
        "dense_bias": gaussian(splits[9], (LAYERS, D), 0.5, 6.0, ((1, 8),), jnp.float32),
        "second_gain": jnp.clip(1.0 + 0.15 * jax.random.normal(splits[10], (LAYERS, D), jnp.float32), 0.25, 1.75),
        "second_shift": gaussian(splits[11], (LAYERS, D), 0.3, 4.0, ((1, 8),), jnp.float32),
        "up_bias": gaussian(splits[12], (LAYERS, H, FF // H), 0.5, 6.0, ((1, 4), (2, 8)), jnp.float32),
        "down_bias": gaussian(splits[13], (LAYERS, D), 0.5, 6.0, ((1, 8),), jnp.float32),
        "cotangent": gaussian(splits[14], (NSEQ, SEQ_LEN, D), 1.0, 6.0, ((0, 4), (1, 2))),
    }


@jax.custom_vjp
def low(v):
    return lax.optimization_barrier(v.astype(jnp.bfloat16)).astype(jnp.float32)

@jax.custom_vjp
def low_back(v):
    return v

def low_keep(v):
    return (low(v), None)

def low_pass(kept, grad):
    return (grad,)

def back_keep(v):
    return (v, None)

def back_low(kept, grad):
    return (low(grad),)
low.defvjp(low_keep, low_pass)
low_back.defvjp(back_keep, back_low)
epsilon = 1e-05
masked_value = -1000000000.0

def layer_norm(values, gain_row, shift_row):
    row_mean = lax.optimization_barrier(jnp.mean(values, axis=-1, keepdims=True))
    centred = values - row_mean
    spread = lax.optimization_barrier(jnp.mean(centred * centred, axis=-1, keepdims=True))
    return centred * lax.rsqrt(spread + epsilon) * gain_row + shift_row

def gelu_tanh(values):
    argument = 0.7978845608028654 * (values + 0.044715 * values * values * values)
    return 0.5 * values * (1.0 + jnp.tanh(argument))

def matmul(left, right):
    return jnp.dot(left, right, precision=lax.Precision.HIGHEST)

def attend(queries, key_rows, value_rows):
    positions = jnp.arange(SEQ_LEN, dtype=jnp.int32)
    causal = positions[None, :] <= positions[:, None]
    offsets = (positions[None, :] - positions[:, None]).astype(jnp.float32)
    slope_vals = 2.0 ** (-8.0 * (jnp.arange(H, dtype=jnp.float32) + 1.0) / H)
    products = jnp.einsum('qhd,khd->hqk', queries, key_rows, precision=lax.Precision.HIGHEST)
    scores = low_back(products * (1.0 / math.sqrt(HD)) + slope_vals[:, None, None] * offsets[None])
    scores = jnp.where(causal[None], scores, masked_value)
    row_max = lax.optimization_barrier(jnp.max(scores, axis=-1, keepdims=True))
    shifted = jnp.exp(scores - row_max)
    attn_probs = low(shifted / lax.optimization_barrier(jnp.sum(shifted, axis=-1, keepdims=True)))
    return jnp.einsum('hqk,khd->qhd', attn_probs, value_rows, precision=lax.Precision.HIGHEST)

def attend_all(queries, key_rows, value_rows):
    grid_shape = (NSEQ, SEQ_LEN, H, HD)
    checked = jax.checkpoint(attend)
    context = lax.map(lambda triple: checked(triple[0], triple[1], triple[2]), (queries.reshape(grid_shape), key_rows.reshape(grid_shape), value_rows.reshape(grid_shape)))
    return context.reshape(NSEQ * SEQ_LEN, D)

def block_forward(hidden, weights):
    w_qkv, w_dense, w_up, w_down, gain_one, shift_one, bias_query, bias_value, bias_dense, gain_two, shift_two, bias_up, bias_down = weights
    row_count = hidden.shape[0]
    normed_one = low(layer_norm(hidden, gain_one, shift_one))
    projected = matmul(normed_one, w_qkv).reshape(row_count, H, 3, HD)
    queries = low(low_back(projected[:, :, 0] + bias_query))
    key_rows = low(low_back(projected[:, :, 1]))
    value_rows = low(low_back(projected[:, :, 2] + bias_value))
    context = low(low_back(attend_all(queries, key_rows, value_rows)))
    hidden_mid = hidden + low_back(matmul(context, w_dense)) + bias_dense
    normed_two = low(layer_norm(hidden_mid, gain_two, shift_two))
    pre_up = low_back(matmul(normed_two, w_up) + bias_up.reshape(FF))
    activation = low(gelu_tanh(pre_up))
    return hidden_mid + low_back(matmul(activation, w_down)) + bias_down

def reference(tokens, qkv_weight, dense_weight, up_weight, down_weight, first_gain, first_shift, query_bias, value_bias, dense_bias, second_gain, second_shift, up_bias, down_bias, cotangent):
    weights = tuple((stacked.astype(jnp.float32) for stacked in (qkv_weight, dense_weight, up_weight, down_weight, first_gain, first_shift, query_bias, value_bias, dense_bias, second_gain, second_shift, up_bias, down_bias)))

    def forward(hidden, params):
        for layer_index in range(LAYERS):
            hidden = block_forward(hidden, tuple((stacked[layer_index] for stacked in params)))
        return hidden
    start = tokens.reshape(NSEQ * SEQ_LEN, D).astype(jnp.float32)
    result, pullback = jax.vjp(forward, start, weights)
    input_grad, weight_grads = pullback(cotangent.reshape(NSEQ * SEQ_LEN, D).astype(jnp.float32))
    grid = (NSEQ, SEQ_LEN, D)
    return (result.reshape(grid).astype(jnp.bfloat16), input_grad.reshape(grid), weight_grads[0], weight_grads[1], weight_grads[2], weight_grads[3], weight_grads[4], weight_grads[5], weight_grads[6], weight_grads[7], weight_grads[8], weight_grads[9], weight_grads[10], weight_grads[11], weight_grads[12])
```

```python
import functools
import math

import jax
import jax.numpy as jnp
from jax import lax
from jax.sharding import PartitionSpec as P

H = 16
HD = 64
LAYERS = 2
DP, SEQ, HEAD = "dp", "seq", "head"

epsilon = 1e-05
masked_value = -1000000000.0
bf16 = jnp.bfloat16
f32 = jnp.float32


def flip(array, index, axis=0):
    size = array.shape[axis]
    bit = 1
    while bit < size:
        shape = array.shape[:axis] + (size // (2 * bit), 2, bit) + array.shape[axis + 1 :]
        cut = array.reshape(shape)
        turned = lax.rev(cut, (axis + 1,))
        array = jnp.where((index & bit) != 0, turned, cut).reshape(array.shape)
        bit *= 2
    return array


def swap(array, name, size, step):
    return lax.ppermute(array, name, [(i, i ^ step) for i in range(size)])


def gather(array, name, size):
    return [array] + [swap(array, name, size, step) for step in range(1, size)]


def deal(blocks, name, size):
    return [blocks[0]] + [swap(blocks[step], name, size, step) for step in range(1, size)]


def sum_blocks(blocks, name, size):
    total = blocks[0]
    for step in range(1, size):
        total = total + swap(blocks[step].astype(bf16), name, size, step).astype(f32)
    return total


def after(array, *others):
    return lax.optimization_barrier((array,) + others)[0]


def norm_parts(values):
    row_mean = jnp.mean(values, axis=-1, keepdims=True)
    centred = values - row_mean
    scale = lax.rsqrt(jnp.mean(centred * centred, axis=-1, keepdims=True) + epsilon)
    return centred * scale, scale


def norm_forward(values, gain, shift):
    xhat, _ = norm_parts(values)
    return (xhat * gain + shift).astype(bf16)


def norm_backward(values, gain, e):
    xhat, scale = norm_parts(values)
    eg = e * gain
    grad = scale * (
        eg
        - jnp.mean(eg, axis=-1, keepdims=True)
        - xhat * jnp.mean(eg * xhat, axis=-1, keepdims=True)
    )
    return grad, jnp.sum(e * xhat, axis=0), jnp.sum(e, axis=0)


def gelu_tanh(values):
    argument = 0.7978845608028654 * (values + 0.044715 * values * values * values)
    return 0.5 * values * (1.0 + jnp.tanh(argument))


def product(spec, left, right):
    return jnp.einsum(spec, left, right, preferred_element_type=f32)


def block_scores(queries, keys, query_pos, key_pos, slopes):
    causal = key_pos[None, :] <= query_pos[:, None]
    offsets = (key_pos[None, :] - query_pos[:, None]).astype(f32)
    scores = product("hqd,hkd->hqk", queries, keys) * (1.0 / math.sqrt(HD))
    scores = scores + slopes[:, None, None] * offsets[None]
    return jnp.where(causal[None], scores, masked_value)


def attend_forward(queries, keys, values, query_pos, key_pos, slopes):
    scores = block_scores(queries, keys, query_pos, key_pos, slopes)
    row_max = jnp.max(scores, axis=-1, keepdims=True)
    shifted = jnp.exp(scores - row_max)
    row_total = jnp.sum(shifted, axis=-1, keepdims=True)
    prob_low = (shifted / row_total).astype(bf16)
    context = product("hqk,hkd->hqd", prob_low, values)
    return context, (row_max + jnp.log(row_total))[..., 0]


def attend_backward(queries, keys, values, grads, log_total, query_pos, key_pos, slopes):
    scores = block_scores(queries, keys, query_pos, key_pos, slopes)
    probs = jnp.exp(scores - log_total[..., None])
    prob_grad = product("hqd,hkd->hqk", grads, values)
    row_inner = jnp.sum(probs * prob_grad, axis=-1, keepdims=True)
    score_grad = (probs * (prob_grad - row_inner)).astype(bf16)
    factor = 1.0 / math.sqrt(HD)
    query_grad = product("hqk,hkd->hqd", score_grad, keys) * factor
    key_grad = product("hqk,hqd->hkd", score_grad, queries) * factor
    value_grad = product("hqk,hqd->hkd", probs.astype(bf16), grads)
    return query_grad, key_grad, value_grad


def per_device(
    sizes,
    tokens,
    qkv_weight,
    dense_weight,
    up_weight,
    down_weight,
    first_gain,
    first_shift,
    query_bias,
    value_bias,
    dense_bias,
    second_gain,
    second_shift,
    up_bias,
    down_bias,
    cotangent,
):
    n_t, n_s, n_z = sizes
    seq_count, slice_len, width = tokens.shape
    assert seq_count == 1 and n_t == n_z
    d, c, z = (lax.axis_index(name) for name in (DP, SEQ, HEAD))
    rows = slice_len // n_t
    cut = qkv_weight.shape[1]
    part = cut * n_t
    heads = query_bias.shape[1]
    assert heads == n_t
    units = up_bias.shape[2] * n_t * n_s

    def to_inner(array):
        lead = array.shape[:-1]
        array = array.reshape(lead + (n_t, n_s, cut))
        array = jnp.moveaxis(array, -2, -3)
        return flip(array, c, len(lead)).reshape(lead + (width,))

    def to_outer(array):
        lead = array.shape[:-1]
        array = flip(array.reshape(lead + (n_s, n_t, cut)), c, len(lead))
        return jnp.moveaxis(array, -2, -3).reshape(lead + (width,))

    def own_rows(array):
        blocks = flip(array.reshape(n_t, rows, width), d)
        total = jnp.where(d == z, blocks[0], jnp.zeros_like(blocks[0]))
        for step in range(1, n_t):
            pairs = [(i * n_z + i, (i ^ step) * n_z + i) for i in range(n_t)]
            total = total + lax.ppermute(blocks[step], (DP, HEAD), pairs)
        return total

    def all_rows(array):
        return jnp.concatenate(gather(array, DP, n_t), axis=0)

    def sum_rows(partial):
        blocks = partial.reshape(n_t, rows, width)
        return sum_blocks([blocks[step] for step in range(n_t)], DP, n_t)

    def to_output(array):
        blocks = flip(jnp.stack(gather(array, HEAD, n_z)), z)
        blocks = flip(blocks, d)
        got = deal([blocks[step] for step in range(n_t)], DP, n_t)
        return flip(jnp.stack(got), d).reshape(1, slice_len, width)

    wide = jnp.stack(
        (first_gain, first_shift, dense_bias, second_gain, second_shift, down_bias), axis=1
    )
    small = jnp.concatenate(
        [
            wide.reshape(-1),
            query_bias.reshape(-1),
            value_bias.reshape(-1),
            up_bias.reshape(-1),
        ]
    )
    small = lax.all_gather(small, (DP, SEQ, HEAD), axis=0, tiled=False)
    small = small.reshape(n_t, n_s, n_z, -1)
    n_wide = LAYERS * 6 * cut
    wide = small[:, :, 0, :n_wide].reshape(n_t, n_s, LAYERS, 6, cut)
    wide = flip(wide, c, 1).transpose(2, 3, 1, 0, 4).reshape(LAYERS, 6, width)
    tall = []
    begin = n_wide
    for source in (query_bias, value_bias, up_bias):
        size = source.shape[2]
        count = LAYERS * heads * size
        piece = small[:, :, :, begin : begin + count].reshape(n_t, n_s, n_z, LAYERS, heads, size)
        begin += count
        piece = lax.dynamic_index_in_dim(piece, d, axis=4, keepdims=False)
        piece = flip(piece, z, 2).transpose(3, 2, 0, 1, 4)
        tall.append(piece.reshape(LAYERS, n_z, n_t * n_s * size))

    def packed(layer):
        qkv = qkv_weight[layer].reshape(cut, n_t, -1)
        dense = dense_weight[layer].T.reshape(cut, n_t, -1)
        up = up_weight[layer].reshape(cut, n_t, -1)
        down = down_weight[layer].T.reshape(cut, n_t, -1)
        return (jnp.concatenate((qkv, dense), axis=2), up, down)

    def to_planes(array):
        blocks = flip(array.transpose(1, 0, 2), d)
        got = deal([blocks[step] for step in range(n_t)], DP, n_t)
        return flip(jnp.stack(got), d).reshape(part, -1)

    def along_z(array):
        return gather(array, HEAD, n_z)

    def join(blocks):
        full = [jnp.concatenate(gather(block, SEQ, n_s), axis=0) for block in blocks]
        return jnp.stack(full, axis=1)

    hidden = to_inner(own_rows(tokens[0])).astype(f32)

    weights = []
    previous = None
    for layer in range(LAYERS):
        kinds = []
        for shard in packed(layer):
            shard = to_planes(shard)
            if previous is not None:
                shard = after(shard, *previous)
            blocks = along_z(shard)
            previous = blocks
            kinds.append(join(blocks))
        weights.append(kinds)

    qkv_columns = 3 * HD
    head_ids = (z ^ jnp.arange(n_z, dtype=jnp.int32)) * heads + d
    slopes = 2.0 ** (-8.0 * (head_ids + 1).astype(f32) / H)
    block_ids = (d ^ jnp.arange(n_t, dtype=jnp.int32)) * rows
    own_pos = (block_ids[:, None] + jnp.arange(rows, dtype=jnp.int32)[None]).reshape(-1)
    query_pos = c * slice_len + own_pos
    others = (c ^ jnp.arange(n_s, dtype=jnp.int32)) * slice_len
    key_pos = (others[:, None] + own_pos[None]).reshape(-1)

    records = []
    for layer in range(LAYERS):
        mixed, w_up, w_down = weights[layer]
        w_qkv = mixed[:, :, :qkv_columns].reshape(width, -1)
        w_dense = mixed[:, :, qkv_columns:].reshape(width, -1)
        w_up = w_up.reshape(width, -1)
        w_down = w_down.reshape(width, -1)
        gain_one, shift_one, bias_dense, gain_two, shift_two, bias_down = (
            wide[layer, i] for i in range(6)
        )
        bias_query, bias_value, bias_up = (piece[layer] for piece in tall)
        normed_one = all_rows(norm_forward(hidden, gain_one, shift_one))
        projected = product("rd,dn->rn", normed_one, w_qkv)
        projected = projected.reshape(slice_len, n_z, 3, HD)
        queries = (projected[:, :, 0] + bias_query[None]).astype(bf16).transpose(1, 0, 2)
        keys = projected[:, :, 1].astype(bf16)
        values = (projected[:, :, 2] + bias_value[None]).astype(bf16)
        both = jnp.concatenate((keys, values), axis=2).transpose(1, 0, 2)
        both = jnp.concatenate(gather(both, SEQ, n_s), axis=1)
        keys, values = both[..., :HD], both[..., HD:]
        context, log_total = attend_forward(queries, keys, values, query_pos, key_pos, slopes)
        context = context.astype(bf16).transpose(1, 0, 2).reshape(slice_len, -1)
        hidden_mid = hidden + sum_rows(product("rc,dc->rd", context, w_dense)) + bias_dense
        normed_two = all_rows(norm_forward(hidden_mid, gain_two, shift_two))
        pre_up = product("rd,df->rf", normed_two, w_up) + bias_up.reshape(-1)
        activation = gelu_tanh(pre_up).astype(bf16)
        hidden_next = hidden_mid + sum_rows(product("rf,df->rd", activation, w_down)) + bias_down
        records.append(
            (
                (w_qkv, w_dense, w_up, w_down, gain_one, gain_two),
                (hidden, hidden_mid, normed_one, normed_two),
                (queries, keys, values, log_total, context, pre_up, activation),
            )
        )
        hidden = hidden_next

    output = to_output(to_outer(hidden.astype(bf16)))

    start = to_inner(own_rows(cotangent[0]))
    gradient = start.astype(f32)
    weight_grads = [None] * LAYERS
    wide_grads = [None] * LAYERS
    tall_grads = [None] * LAYERS
    chain = [None]

    def give_back(grad):
        blocks = grad.reshape(n_s, part, n_z, -1)
        mine = sum_blocks([blocks[step] for step in range(n_s)], SEQ, n_s)
        if chain[0] is not None:
            mine = after(mine, chain[0])
        mine = sum_blocks([mine[:, step] for step in range(n_z)], HEAD, n_z).astype(bf16)
        chain[0] = mine
        mine = flip(mine.reshape(n_t, cut, -1), d)
        got = deal([mine[step] for step in range(n_t)], DP, n_t)
        return flip(jnp.stack(got, axis=1), d, 1).astype(f32)

    for layer in reversed(range(LAYERS)):
        (
            (w_qkv, w_dense, w_up, w_down, gain_one, gain_two),
            (hidden, hidden_mid, normed_one, normed_two),
            (queries, keys, values, log_total, context, pre_up, activation),
        ) = records[layer]
        down_bias_grad = jnp.sum(gradient, axis=0)
        grad_low = all_rows(gradient.astype(bf16))
        act_grad = product("rd,df->rf", grad_low, w_down)
        pre_grad = jax.vjp(gelu_tanh, pre_up)[1](act_grad)[0].astype(bf16)
        e = sum_rows(product("rf,df->rd", pre_grad, w_up))
        down_grad = product("rd,rf->df", grad_low, activation).reshape(width, n_z, -1)
        up_grad = product("rd,rf->df", normed_two, pre_grad).reshape(width, n_z, -1)
        up_bias_grad = jnp.sum(pre_grad, axis=0, dtype=f32).reshape(n_z, -1)
        down_share = give_back(down_grad)
        up_share = give_back(up_grad)
        part_mid, gain_two_grad, shift_two_grad = norm_backward(hidden_mid, gain_two, e)
        mid_grad = gradient + part_mid
        dense_bias_grad = jnp.sum(mid_grad, axis=0)
        mid_low = all_rows(mid_grad.astype(bf16))
        context_grad = product("rd,dc->rc", mid_low, w_dense).astype(bf16)
        context_grad = context_grad.reshape(slice_len, n_z, HD).transpose(1, 0, 2)
        dense_grad = product("rd,rc->dc", mid_low, context).reshape(width, n_z, -1)
        query_grad, key_grad, value_grad = attend_backward(
            queries, keys, values, context_grad, log_total, query_pos, key_pos, slopes
        )
        both = jnp.concatenate((key_grad, value_grad), axis=2)
        both = both.reshape(n_z, n_s, slice_len, 2 * HD)
        both = sum_blocks([both[:, step] for step in range(n_s)], SEQ, n_s).astype(bf16)
        query_grad = query_grad.astype(bf16)
        query_bias_grad = jnp.sum(query_grad, axis=1, dtype=f32)
        value_bias_grad = jnp.sum(both[..., HD:], axis=1, dtype=f32)
        joined = jnp.concatenate((query_grad, both), axis=2)
        joined = joined.transpose(1, 0, 2).reshape(slice_len, -1)
        qkv_grad = product("rd,rn->dn", normed_one, joined).reshape(width, n_z, -1)
        mixed_share = give_back(jnp.concatenate((qkv_grad, dense_grad), axis=2))
        e = sum_rows(product("rn,dn->rd", joined, w_qkv))
        part_in, gain_one_grad, shift_one_grad = norm_backward(hidden, gain_one, e)
        gradient = mid_grad + part_in
        weight_grads[layer] = (
            mixed_share[:, :, :qkv_columns].reshape(cut, -1),
            mixed_share[:, :, qkv_columns:].reshape(cut, -1).T,
            up_share.reshape(cut, -1),
            down_share.reshape(cut, -1).T,
        )
        wide_grads[layer] = jnp.stack(
            (
                gain_one_grad,
                shift_one_grad,
                dense_bias_grad,
                gain_two_grad,
                shift_two_grad,
                down_bias_grad,
            )
        )
        tall_grads[layer] = jnp.concatenate(
            (query_bias_grad, value_bias_grad, up_bias_grad), axis=1
        )

    tokens_grad = to_output(to_outer(gradient.astype(bf16))).astype(f32)

    def fold(arrays, name, size):
        total = arrays[0]
        for step in range(1, size):
            total = total + swap(arrays[step], name, size, step)
        return total

    wide = jnp.stack(wide_grads).reshape(LAYERS * 6, n_s, n_t, cut)
    sizes_tall = (HD, HD, units)
    pieces, begin = [], 0
    tall = jnp.stack(tall_grads)
    for size in sizes_tall:
        piece = tall[:, :, begin : begin + size]
        begin += size
        piece = piece.reshape(LAYERS, n_z, n_t, n_s, size // (n_t * n_s))
        pieces.append(flip(piece, c, 3))
    tall = jnp.concatenate(
        [piece.transpose(3, 1, 2, 0, 4).reshape(n_s, n_z, n_t, -1) for piece in pieces], axis=3
    )
    wide = wide.transpose(1, 2, 0, 3).reshape(n_s, n_t, -1)
    n_wide = wide.shape[2]
    wide = jnp.broadcast_to(wide[:, None], (n_s, n_z) + wide.shape[1:])
    joint = jnp.concatenate((wide, tall), axis=3)
    joint = fold([joint[step] for step in range(n_s)], SEQ, n_s)
    joint = fold([joint[step] for step in range(n_z)], HEAD, n_z)
    joint = flip(joint, d)
    got = deal([joint[step] for step in range(n_t)], DP, n_t)
    wide = functools.reduce(jnp.add, [item[:n_wide] for item in got])
    wide = wide.reshape(LAYERS, 6, cut)
    tall = flip(jnp.stack([item[n_wide:] for item in got]), d)
    outs, begin = [], 0
    for size in sizes_tall:
        size = size // (n_t * n_s)
        piece = tall[:, begin : begin + LAYERS * size].reshape(n_t, LAYERS, size)
        begin += LAYERS * size
        outs.append(piece.transpose(1, 0, 2))
    query_bias_grad, value_bias_grad, up_bias_grad = outs
    qkv_grad, dense_grad, up_grad, down_grad = (
        jnp.stack([weight_grads[layer][kind] for layer in range(LAYERS)]) for kind in range(4)
    )
    return (
        output,
        tokens_grad,
        qkv_grad,
        dense_grad,
        up_grad,
        down_grad,
        wide[:, 0],
        wide[:, 1],
        query_bias_grad,
        value_bias_grad,
        wide[:, 2],
        wide[:, 3],
        wide[:, 4],
        up_bias_grad,
        wide[:, 5],
    )


def solution(mesh):
    sizes = tuple(mesh.shape[name] for name in (DP, SEQ, HEAD))
    rows = P(DP, SEQ, None)
    tall = P(None, (DP, SEQ), HEAD)
    flat = P(None, HEAD, (DP, SEQ))
    vector = P(None, (DP, SEQ))
    params = (
        tall,
        flat,
        tall,
        flat,
        vector,
        vector,
        flat,
        flat,
        vector,
        vector,
        vector,
        flat,
        vector,
    )
    return jax.shard_map(
        functools.partial(per_device, sizes),
        mesh=mesh,
        in_specs=(rows,) + params + (rows,),
        out_specs=(rows, rows) + params,
        check_vma=False,
    )
```

```python
import functools
import math

import jax
import jax.numpy as jnp
from jax import lax
from jax.sharding import PartitionSpec as P

H = 16
HD = 64
LAYERS = 2
DP, SEQ, HEAD = "dp", "seq", "head"

epsilon = 1e-05
masked_value = -1000000000.0
bf16 = jnp.bfloat16
f32 = jnp.float32


def flip_list(blocks, index):
    bit = 1
    while bit < len(blocks):
        turn = (index & bit) != 0
        blocks = [jnp.where(turn, blocks[j ^ bit], blocks[j]) for j in range(len(blocks))]
        bit *= 2
    return blocks


def flip(array, index, axis=0):
    blocks = [lax.index_in_dim(array, j, axis, keepdims=True) for j in range(array.shape[axis])]
    return jnp.concatenate(flip_list(blocks, index), axis=axis)


def swap(array, name, size, step):
    return lax.ppermute(array, name, [(i, i ^ step) for i in range(size)])


def gather(array, name, size):
    return [array] + [swap(array, name, size, step) for step in range(1, size)]


def deal(blocks, name, size):
    return [blocks[0]] + [swap(blocks[step], name, size, step) for step in range(1, size)]


def sum_blocks(blocks, name, size):
    total = blocks[0].astype(f32)
    for step in range(1, size):
        total = total + swap(blocks[step].astype(bf16), name, size, step).astype(f32)
    return total


def after(array, *others):
    return lax.optimization_barrier((array,) + others)[0]


def norm_parts(values):
    row_mean = jnp.mean(values, axis=-1, keepdims=True)
    centred = values - row_mean
    scale = lax.rsqrt(jnp.mean(centred * centred, axis=-1, keepdims=True) + epsilon)
    return centred * scale, scale


def norm_forward(values, gain, shift):
    xhat, _ = norm_parts(values)
    return (xhat * gain + shift).astype(bf16)


def norm_backward(values, gain, e):
    xhat, scale = norm_parts(values)
    eg = e * gain
    grad = scale * (
        eg
        - jnp.mean(eg, axis=-1, keepdims=True)
        - xhat * jnp.mean(eg * xhat, axis=-1, keepdims=True)
    )
    return grad, jnp.sum(e * xhat, axis=0), jnp.sum(e, axis=0)


def gelu_tanh(values):
    argument = 0.7978845608028654 * (values + 0.044715 * values * values * values)
    return 0.5 * values * (1.0 + jnp.tanh(argument))


def product(spec, left, right):
    return jnp.einsum(spec, left, right, preferred_element_type=f32)


def block_scores(queries, keys, query_pos, key_pos, slopes):
    causal = key_pos[None, :] <= query_pos[:, None]
    offsets = (key_pos[None, :] - query_pos[:, None]).astype(f32)
    scores = product("hqd,hkd->hqk", queries, keys) * (1.0 / math.sqrt(HD))
    scores = scores + slopes[:, None, None] * offsets[None]
    return jnp.where(causal[None], scores, masked_value)


def attend_forward(queries, keys, values, query_pos, key_pos, slopes):
    scores = block_scores(queries, keys, query_pos, key_pos, slopes)
    row_max = jnp.max(scores, axis=-1, keepdims=True)
    shifted = jnp.exp(scores - row_max)
    row_total = jnp.sum(shifted, axis=-1, keepdims=True)
    prob_low = (shifted / row_total).astype(bf16)
    context = product("hqk,hkd->hqd", prob_low, values)
    return context, (row_max + jnp.log(row_total))[..., 0]


def attend_backward(queries, keys, values, grads, log_total, query_pos, key_pos, slopes):
    scores = block_scores(queries, keys, query_pos, key_pos, slopes)
    probs = jnp.exp(scores - log_total[..., None])
    prob_grad = product("hqd,hkd->hqk", grads, values)
    row_inner = jnp.sum(probs * prob_grad, axis=-1, keepdims=True)
    score_grad = (probs * (prob_grad - row_inner)).astype(bf16)
    factor = 1.0 / math.sqrt(HD)
    query_grad = product("hqk,hkd->hqd", score_grad, keys) * factor
    key_grad = product("hqk,hqd->hkd", score_grad, queries) * factor
    value_grad = product("hqk,hqd->hkd", probs.astype(bf16), grads)
    return query_grad, key_grad, value_grad


def per_device(
    sizes,
    tokens,
    qkv_weight,
    dense_weight,
    up_weight,
    down_weight,
    first_gain,
    first_shift,
    query_bias,
    value_bias,
    dense_bias,
    second_gain,
    second_shift,
    up_bias,
    down_bias,
    cotangent,
):
    n_t, n_s, n_z = sizes
    seq_count, slice_len, width = tokens.shape
    assert seq_count == 1 and n_t == n_z
    d, c, z = (lax.axis_index(name) for name in (DP, SEQ, HEAD))
    rows = slice_len // n_t
    cut = qkv_weight.shape[1]
    part = cut * n_t
    heads = query_bias.shape[1]
    assert heads == n_t
    units = up_bias.shape[2] * n_t * n_s

    def to_inner(array):
        lead = array.shape[:-1]
        array = array.reshape(lead + (n_t, n_s, cut))
        array = jnp.moveaxis(array, -2, -3)
        return flip(array, c, len(lead)).reshape(lead + (width,))

    def to_outer(array):
        lead = array.shape[:-1]
        array = flip(array.reshape(lead + (n_s, n_t, cut)), c, len(lead))
        return jnp.moveaxis(array, -2, -3).reshape(lead + (width,))

    def own_rows(array):
        cuts = array.reshape(n_t, rows, width)
        blocks = [lax.dynamic_index_in_dim(cuts, d ^ step, 0, False) for step in range(n_t)]
        total = jnp.where(d == z, blocks[0], jnp.zeros_like(blocks[0]))
        for step in range(1, n_t):
            pairs = [(i * n_z + i, (i ^ step) * n_z + i) for i in range(n_t)]
            total = total + lax.ppermute(blocks[step], (DP, HEAD), pairs)
        return total

    def all_rows(array):
        return jnp.concatenate(gather(array, DP, n_t), axis=0)

    def sum_rows(partial):
        blocks = partial.astype(bf16).reshape(n_t, rows, width)
        return sum_blocks([blocks[step] for step in range(n_t)], DP, n_t)

    def to_output(array):
        planes = lax.all_gather(array, HEAD, axis=0, tiled=False)
        blocks = [lax.dynamic_index_in_dim(planes, d ^ step, 0, False) for step in range(n_t)]
        got = deal(blocks, DP, n_t)
        return jnp.concatenate(flip_list(got, d), axis=0).reshape(1, slice_len, width)

    def packed(layer):
        qkv = qkv_weight[layer].reshape(cut, n_t, -1)
        dense = dense_weight[layer].T.reshape(cut, n_t, -1)
        up = up_weight[layer].reshape(cut, n_t, -1)
        down = down_weight[layer].T.reshape(cut, n_t, -1)
        return tuple(
            [jnp.concatenate((one[:, j], two[:, j]), axis=1) for j in range(n_t)]
            for one, two in ((qkv, dense), (up, down))
        )

    def to_planes(blocks):
        got = deal(flip_list(blocks, d), DP, n_t)
        return jnp.concatenate(flip_list(got, d), axis=0)

    def join(planes):
        return jnp.concatenate(gather(planes, SEQ, n_s), axis=1).transpose(1, 0, 2)

    shards = [packed(layer) for layer in range(LAYERS)]
    shards = [to_planes(shards[0][0]), shards[0][1], shards[1][0], shards[1][1]]
    hidden = to_inner(own_rows(tokens[0])).astype(f32)

    wide = jnp.stack(
        (first_gain, first_shift, dense_bias, second_gain, second_shift, down_bias), axis=1
    )
    small = jnp.concatenate(
        [
            wide.reshape(-1),
            query_bias.reshape(-1),
            value_bias.reshape(-1),
            up_bias.reshape(-1),
        ]
    )
    small = lax.all_gather(small, (DP, SEQ), axis=0, tiled=False).reshape(n_t, n_s, -1)
    n_wide = LAYERS * 6 * cut
    wide = small[:, :, :n_wide].reshape(n_t, n_s, LAYERS, 6, cut)
    wide = flip(wide, c, 1).transpose(2, 3, 1, 0, 4).reshape(LAYERS, 6, width)
    tall = []
    begin = n_wide
    tall_sizes = (HD, HD, units)
    for size in tall_sizes:
        size = size // (n_t * n_s)
        count = LAYERS * heads * size
        piece = small[:, :, begin : begin + count].reshape(n_t, n_s, LAYERS, heads, size)
        begin += count
        piece = lax.dynamic_index_in_dim(piece, d, axis=3, keepdims=False)
        tall.append(piece.transpose(2, 0, 1, 3).reshape(LAYERS, -1))
    tall = jnp.concatenate(tall, axis=1)
    tall = jnp.stack(flip_list(gather(tall, HEAD, n_z), z), axis=1)

    planes = lax.all_gather(shards[0], HEAD, axis=0, tiled=False)
    messages = [planes]
    previous = shards[0]
    for shard in shards[1:]:
        shard = to_planes([after(block, previous) for block in shard])
        messages.append(lax.all_gather(shard, HEAD, axis=0, tiled=False))
        previous = shard
    weights = [join(planes) for planes in messages]

    qkv_columns = 3 * HD
    head_ids = jnp.arange(n_z, dtype=jnp.int32) * heads + d
    slopes = 2.0 ** (-8.0 * (head_ids + 1).astype(f32) / H)
    block_ids = (d ^ jnp.arange(n_t, dtype=jnp.int32)) * rows
    own_pos = (block_ids[:, None] + jnp.arange(rows, dtype=jnp.int32)[None]).reshape(-1)
    query_pos = c * slice_len + own_pos
    others = (c ^ jnp.arange(n_s, dtype=jnp.int32)) * slice_len
    key_pos = (others[:, None] + own_pos[None]).reshape(-1)

    records = []
    for layer in range(LAYERS):
        mixed, feed = weights[2 * layer], weights[2 * layer + 1]
        w_qkv = mixed[:, :, :qkv_columns].reshape(width, -1)
        w_dense = mixed[:, :, qkv_columns:].reshape(width, -1)
        w_up = feed[:, :, :units].reshape(width, -1)
        w_down = feed[:, :, units:].reshape(width, -1)
        gain_one, shift_one, bias_dense, gain_two, shift_two, bias_down = (
            wide[layer, i] for i in range(6)
        )
        bias_query, bias_value, bias_up = (
            tall[layer, :, begin : begin + size]
            for begin, size in ((0, HD), (HD, HD), (2 * HD, units))
        )
        normed_one = all_rows(norm_forward(hidden, gain_one, shift_one))
        projected = product("rd,dn->rn", normed_one, w_qkv)
        projected = projected.reshape(slice_len, n_z, 3, HD)
        queries = (projected[:, :, 0] + bias_query[None]).astype(bf16).transpose(1, 0, 2)
        keys = projected[:, :, 1].astype(bf16)
        values = (projected[:, :, 2] + bias_value[None]).astype(bf16)
        both = jnp.concatenate((keys, values), axis=2).transpose(1, 0, 2)
        both = jnp.concatenate(gather(both, SEQ, n_s), axis=1)
        keys, values = both[..., :HD], both[..., HD:]
        context, log_total = attend_forward(queries, keys, values, query_pos, key_pos, slopes)
        context = context.astype(bf16).transpose(1, 0, 2).reshape(slice_len, -1)
        hidden_mid = hidden + sum_rows(product("rc,dc->rd", context, w_dense)) + bias_dense
        normed_two = all_rows(norm_forward(hidden_mid, gain_two, shift_two))
        pre_up = product("rd,df->rf", normed_two, w_up) + bias_up.reshape(-1)
        activation = gelu_tanh(pre_up).astype(bf16)
        hidden_next = hidden_mid + sum_rows(product("rf,df->rd", activation, w_down)) + bias_down
        records.append(
            (
                (w_qkv, w_dense, w_up, w_down, gain_one, gain_two),
                (hidden, hidden_mid, normed_one, normed_two),
                (queries, keys, values, log_total, context, pre_up, activation),
            )
        )
        hidden = hidden_next

    output = to_output(to_outer(hidden.astype(bf16)))

    start = to_inner(own_rows(cotangent[0]))
    gradient = start.astype(f32)
    weight_grads = [None] * LAYERS
    wide_grads = [None] * LAYERS
    tall_grads = [None] * LAYERS

    def give_back(grad):
        blocks = grad.reshape(n_s, part, n_z, -1)
        mine = sum_blocks([blocks[step] for step in range(n_s)], SEQ, n_s).astype(bf16)
        mine = mine.transpose(1, 0, 2)
        mine = lax.psum_scatter(mine, HEAD, scatter_dimension=0, tiled=False)
        mine = mine.reshape(n_t, cut, -1)
        blocks = [lax.dynamic_index_in_dim(mine, d ^ step, 0, False) for step in range(n_t)]
        got = deal(blocks, DP, n_t)
        return jnp.stack(flip_list(got, d), axis=1).astype(f32)

    for layer in reversed(range(LAYERS)):
        (
            (w_qkv, w_dense, w_up, w_down, gain_one, gain_two),
            (hidden, hidden_mid, normed_one, normed_two),
            (queries, keys, values, log_total, context, pre_up, activation),
        ) = records[layer]
        down_bias_grad = jnp.sum(gradient, axis=0)
        grad_low = all_rows(gradient.astype(bf16))
        act_grad = product("rd,df->rf", grad_low, w_down)
        pre_grad = jax.vjp(gelu_tanh, pre_up)[1](act_grad)[0].astype(bf16)
        e = sum_rows(product("rf,df->rd", pre_grad, w_up))
        down_grad = product("rd,rf->df", grad_low, activation).astype(bf16)
        up_grad = product("rd,rf->df", normed_two, pre_grad).astype(bf16)
        feed_grad = jnp.concatenate(
            (up_grad.reshape(width, n_z, -1), down_grad.reshape(width, n_z, -1)), axis=2
        )
        up_bias_grad = jnp.sum(pre_grad, axis=0, dtype=f32).reshape(n_z, -1)
        feed_share = give_back(feed_grad)
        part_mid, gain_two_grad, shift_two_grad = norm_backward(hidden_mid, gain_two, e)
        mid_grad = gradient + part_mid
        dense_bias_grad = jnp.sum(mid_grad, axis=0)
        mid_low = all_rows(mid_grad.astype(bf16))
        context_grad = product("rd,dc->rc", mid_low, w_dense).astype(bf16)
        context_grad = context_grad.reshape(slice_len, n_z, HD).transpose(1, 0, 2)
        dense_grad = product("rd,rc->dc", mid_low, context).astype(bf16).reshape(width, n_z, -1)
        query_grad, key_grad, value_grad = attend_backward(
            queries, keys, values, context_grad, log_total, query_pos, key_pos, slopes
        )
        both = jnp.concatenate((key_grad, value_grad), axis=2)
        both = both.reshape(n_z, n_s, slice_len, 2 * HD)
        both = sum_blocks([both[:, step] for step in range(n_s)], SEQ, n_s).astype(bf16)
        query_grad = query_grad.astype(bf16)
        query_bias_grad = jnp.sum(query_grad, axis=1, dtype=f32)
        value_bias_grad = jnp.sum(both[..., HD:], axis=1, dtype=f32)
        joined = jnp.concatenate((query_grad, both), axis=2)
        joined = joined.transpose(1, 0, 2).reshape(slice_len, -1)
        qkv_grad = product("rd,rn->dn", normed_one, joined).astype(bf16).reshape(width, n_z, -1)
        mixed_share = give_back(jnp.concatenate((qkv_grad, dense_grad), axis=2))
        e = sum_rows(product("rn,dn->rd", joined, w_qkv))
        part_in, gain_one_grad, shift_one_grad = norm_backward(hidden, gain_one, e)
        gradient = mid_grad + part_in
        weight_grads[layer] = (
            mixed_share[:, :, :qkv_columns].reshape(cut, -1),
            mixed_share[:, :, qkv_columns:].reshape(cut, -1).T,
            feed_share[:, :, :units].reshape(cut, -1),
            feed_share[:, :, units:].reshape(cut, -1).T,
        )
        wide_grads[layer] = jnp.stack(
            (
                gain_one_grad,
                shift_one_grad,
                dense_bias_grad,
                gain_two_grad,
                shift_two_grad,
                down_bias_grad,
            )
        )
        tall_grads[layer] = jnp.concatenate(
            (query_bias_grad, value_bias_grad, up_bias_grad), axis=1
        )

    tokens_grad = to_output(to_outer(gradient.astype(bf16))).astype(f32)

    def fold(arrays, name, size):
        total = arrays[0]
        for step in range(1, size):
            total = total + swap(arrays[step], name, size, step)
        return total

    wide = jnp.stack(wide_grads).reshape(LAYERS * 6, n_s, n_t, cut)
    pieces, begin = [], 0
    tall = jnp.stack(tall_grads)
    for size in tall_sizes:
        piece = tall[:, :, begin : begin + size]
        begin += size
        piece = piece.reshape(LAYERS, n_z, n_t, n_s, size // (n_t * n_s))
        pieces.append(flip(flip(piece, c, 3), z, 1))
    tall = jnp.concatenate(
        [piece.transpose(3, 1, 2, 0, 4).reshape(n_s, n_z, n_t, -1) for piece in pieces], axis=3
    )
    wide = wide.transpose(1, 2, 0, 3).reshape(n_s, n_t, -1)
    n_wide = wide.shape[2]
    wide = jnp.broadcast_to(wide[:, None], (n_s, n_z) + wide.shape[1:])
    joint = jnp.concatenate((wide, tall), axis=3)
    joint = fold([joint[step] for step in range(n_s)], SEQ, n_s)
    joint = fold([joint[step] for step in range(n_z)], HEAD, n_z)
    joint = flip(joint, d)
    got = deal([joint[step] for step in range(n_t)], DP, n_t)
    wide = functools.reduce(jnp.add, [item[:n_wide] for item in got])
    wide = wide.reshape(LAYERS, 6, cut)
    tall = flip(jnp.stack([item[n_wide:] for item in got]), d)
    outs, begin = [], 0
    for size in tall_sizes:
        size = size // (n_t * n_s)
        piece = tall[:, begin : begin + LAYERS * size].reshape(n_t, LAYERS, size)
        begin += LAYERS * size
        outs.append(piece.transpose(1, 0, 2))
    query_bias_grad, value_bias_grad, up_bias_grad = outs
    qkv_grad, dense_grad, up_grad, down_grad = (
        jnp.stack([weight_grads[layer][kind] for layer in range(LAYERS)]) for kind in range(4)
    )
    return (
        output,
        tokens_grad,
        qkv_grad,
        dense_grad,
        up_grad,
        down_grad,
        wide[:, 0],
        wide[:, 1],
        query_bias_grad,
        value_bias_grad,
        wide[:, 2],
        wide[:, 3],
        wide[:, 4],
        up_bias_grad,
        wide[:, 5],
    )


def solution(mesh):
    sizes = tuple(mesh.shape[name] for name in (DP, SEQ, HEAD))
    rows = P(DP, SEQ, None)
    tall = P(None, (DP, SEQ), HEAD)
    flat = P(None, HEAD, (DP, SEQ))
    vector = P(None, (DP, SEQ))
    params = (
        tall,
        flat,
        tall,
        flat,
        vector,
        vector,
        flat,
        flat,
        vector,
        vector,
        vector,
        flat,
        vector,
    )
    return jax.shard_map(
        functools.partial(per_device, sizes),
        mesh=mesh,
        in_specs=(rows,) + params + (rows,),
        out_specs=(rows, rows) + params,
        check_vma=False,
    )
```

```python
import functools
import math

import jax
import jax.numpy as jnp
from jax import lax
from jax.sharding import PartitionSpec as P

H = 16
HD = 64
LAYERS = 2
DP, SEQ, HEAD = "dp", "seq", "head"

epsilon = 1e-05
masked_value = -1000000000.0
bf16 = jnp.bfloat16
f32 = jnp.float32


def flip_list(blocks, index):
    bit = 1
    while bit < len(blocks):
        turn = (index & bit) != 0
        blocks = [jnp.where(turn, blocks[j ^ bit], blocks[j]) for j in range(len(blocks))]
        bit *= 2
    return blocks


def flip(array, index, axis=0):
    blocks = [lax.index_in_dim(array, j, axis, keepdims=True) for j in range(array.shape[axis])]
    return jnp.concatenate(flip_list(blocks, index), axis=axis)


def swap(array, name, size, step):
    return lax.ppermute(array, name, [(i, i ^ step) for i in range(size)])


def gather(array, name, size):
    return [array] + [swap(array, name, size, step) for step in range(1, size)]


def deal(blocks, name, size):
    return [blocks[0]] + [swap(blocks[step], name, size, step) for step in range(1, size)]


def meet(*groups):
    return lax.optimization_barrier(groups)


def add_all(blocks):
    return functools.reduce(jnp.add, [block.astype(f32) for block in blocks])


def sum_blocks(blocks, name, size):
    total = blocks[0].astype(f32)
    for step in range(1, size):
        total = total + swap(blocks[step].astype(bf16), name, size, step).astype(f32)
    return total


def after(array, *others):
    return lax.optimization_barrier((array,) + others)[0]


def norm_parts(values):
    row_mean = jnp.mean(values, axis=-1, keepdims=True)
    centred = values - row_mean
    scale = lax.rsqrt(jnp.mean(centred * centred, axis=-1, keepdims=True) + epsilon)
    return centred * scale, scale


def norm_forward(values, gain, shift):
    xhat, _ = norm_parts(values)
    return (xhat * gain + shift).astype(bf16)


def norm_backward(values, gain, e):
    xhat, scale = norm_parts(values)
    eg = e * gain
    grad = scale * (
        eg
        - jnp.mean(eg, axis=-1, keepdims=True)
        - xhat * jnp.mean(eg * xhat, axis=-1, keepdims=True)
    )
    return grad, jnp.sum(e * xhat, axis=0), jnp.sum(e, axis=0)


def gelu_tanh(values):
    argument = 0.7978845608028654 * (values + 0.044715 * values * values * values)
    return 0.5 * values * (1.0 + jnp.tanh(argument))


def product(spec, left, right):
    return jnp.einsum(spec, left, right, preferred_element_type=f32)


def block_scores(queries, keys, query_pos, key_pos, slopes):
    causal = key_pos[None, :] <= query_pos[:, None]
    offsets = (key_pos[None, :] - query_pos[:, None]).astype(f32)
    scores = product("hqd,hkd->hqk", queries, keys) * (1.0 / math.sqrt(HD))
    scores = scores + slopes[:, None, None] * offsets[None]
    return jnp.where(causal[None], scores, masked_value)


def attend_forward(queries, keys, values, query_pos, key_pos, slopes):
    scores = block_scores(queries, keys, query_pos, key_pos, slopes)
    row_max = jnp.max(scores, axis=-1, keepdims=True)
    shifted = jnp.exp(scores - row_max)
    row_total = jnp.sum(shifted, axis=-1, keepdims=True)
    prob_low = (shifted / row_total).astype(bf16)
    context = product("hqk,hkd->hqd", prob_low, values)
    return context, (row_max + jnp.log(row_total))[..., 0]


def attend_backward(queries, keys, values, grads, log_total, query_pos, key_pos, slopes):
    scores = block_scores(queries, keys, query_pos, key_pos, slopes)
    probs = jnp.exp(scores - log_total[..., None])
    prob_grad = product("hqd,hkd->hqk", grads, values)
    row_inner = jnp.sum(probs * prob_grad, axis=-1, keepdims=True)
    score_grad = (probs * (prob_grad - row_inner)).astype(bf16)
    factor = 1.0 / math.sqrt(HD)
    query_grad = product("hqk,hkd->hqd", score_grad, keys) * factor
    key_grad = product("hqk,hqd->hkd", score_grad, queries) * factor
    value_grad = product("hqk,hqd->hkd", probs.astype(bf16), grads)
    return query_grad, key_grad, value_grad


def per_device(
    sizes,
    tokens,
    qkv_weight,
    dense_weight,
    up_weight,
    down_weight,
    first_gain,
    first_shift,
    query_bias,
    value_bias,
    dense_bias,
    second_gain,
    second_shift,
    up_bias,
    down_bias,
    cotangent,
):
    n_t, n_s, n_z = sizes
    seq_count, slice_len, width = tokens.shape
    assert seq_count == 1 and n_t == n_z
    d, c, z = (lax.axis_index(name) for name in (DP, SEQ, HEAD))
    rows = slice_len // n_t
    cut = qkv_weight.shape[1]
    part = cut * n_t
    heads = query_bias.shape[1]
    assert heads == n_t
    units = up_bias.shape[2] * n_t * n_s

    def to_inner(array):
        lead = array.shape[:-1]
        array = array.reshape(lead + (n_t, n_s, cut))
        array = jnp.moveaxis(array, -2, -3)
        return flip(array, c, len(lead)).reshape(lead + (width,))

    def to_outer(array):
        lead = array.shape[:-1]
        array = flip(array.reshape(lead + (n_s, n_t, cut)), c, len(lead))
        return jnp.moveaxis(array, -2, -3).reshape(lead + (width,))

    def own_rows(array):
        cuts = array.reshape(n_t, rows, width)
        blocks = [lax.dynamic_index_in_dim(cuts, d ^ step, 0, False) for step in range(n_t)]
        total = jnp.where(d == z, blocks[0], jnp.zeros_like(blocks[0]))
        for step in range(1, n_t):
            pairs = [(i * n_z + i, (i ^ step) * n_z + i) for i in range(n_t)]
            total = total + lax.ppermute(blocks[step], (DP, HEAD), pairs)
        return total

    def send_rows(array):
        return gather(array, DP, n_t)

    def send_sums(partial):
        blocks = partial.astype(bf16).reshape(n_t, rows, width)
        return deal([blocks[step] for step in range(n_t)], DP, n_t)

    def joined_rows(blocks):
        return jnp.concatenate(blocks, axis=0)

    def to_planes_of(array):
        return lax.all_gather(array, HEAD, axis=0, tiled=False)

    def send_output(planes):
        blocks = [lax.dynamic_index_in_dim(planes, d ^ step, 0, False) for step in range(n_t)]
        return deal(blocks, DP, n_t)

    def output_of(got):
        return jnp.concatenate(flip_list(got, d), axis=0).reshape(1, slice_len, width)

    def packed(layer):
        qkv = qkv_weight[layer].reshape(cut, n_t, -1)
        dense = dense_weight[layer].T.reshape(cut, n_t, -1)
        up = up_weight[layer].reshape(cut, n_t, -1)
        down = down_weight[layer].T.reshape(cut, n_t, -1)
        return tuple(
            [jnp.concatenate((one[:, j], two[:, j]), axis=1) for j in range(n_t)]
            for one, two in ((qkv, dense), (up, down))
        )

    def to_planes(blocks):
        got = deal(flip_list(blocks, d), DP, n_t)
        return jnp.concatenate(flip_list(got, d), axis=0)

    def join(planes):
        return jnp.concatenate(gather(planes, SEQ, n_s), axis=1).transpose(1, 0, 2)

    shards = [packed(layer) for layer in range(LAYERS)]
    first_shard = to_planes(shards[0][0])
    messages = [to_planes_of(first_shard)]
    start_rows = own_rows(tokens[0])

    wide = jnp.concatenate(
        (first_gain, first_shift, dense_bias, second_gain, second_shift, down_bias), axis=0
    )
    tall = jnp.concatenate((query_bias, value_bias, up_bias), axis=2)
    small = jnp.concatenate((wide, tall.reshape(-1, cut)), axis=0)
    small = after(small, first_shard)
    small = lax.all_gather(small, (DP, SEQ), axis=0, tiled=False)
    small = small.reshape((n_t, n_s) + small.shape[1:])
    wide = small[:, :, : 6 * LAYERS].transpose(2, 1, 0, 3)
    wide = flip(wide, c, 1).reshape(6, LAYERS, width)
    each = small[:, :, 6 * LAYERS :].reshape(n_t, n_s, LAYERS, heads, -1)
    each = lax.dynamic_index_in_dim(each, d, axis=3, keepdims=False)
    tall = []
    begin = 0
    tall_sizes = (HD, HD, units)
    for size in tall_sizes:
        size = size // (n_t * n_s)
        piece = each[:, :, :, begin : begin + size]
        begin += size
        tall.append(piece.transpose(2, 0, 1, 3).reshape(LAYERS, -1))
    tall = jnp.concatenate(tall, axis=1)
    tall = jnp.stack(flip_list(gather(tall, HEAD, n_z), z), axis=1)

    hidden = to_inner(start_rows).astype(f32)
    second_shard = to_planes([after(block, small) for block in shards[0][1]])
    messages.append(to_planes_of(second_shard))

    qkv_columns = 3 * HD
    head_ids = jnp.arange(n_z, dtype=jnp.int32) * heads + d
    slopes = 2.0 ** (-8.0 * (head_ids + 1).astype(f32) / H)
    block_ids = (d ^ jnp.arange(n_t, dtype=jnp.int32)) * rows
    own_pos = (block_ids[:, None] + jnp.arange(rows, dtype=jnp.int32)[None]).reshape(-1)
    query_pos = c * slice_len + own_pos
    others = (c ^ jnp.arange(n_s, dtype=jnp.int32)) * slice_len
    key_pos = (others[:, None] + own_pos[None]).reshape(-1)

    cot = cotangent[0]
    records = []
    for layer in range(LAYERS):
        mixed, feed = (join(planes) for planes in messages[2 * layer : 2 * layer + 2])
        w_qkv = mixed[:, :, :qkv_columns].reshape(width, -1)
        w_dense = mixed[:, :, qkv_columns:].reshape(width, -1)
        w_up = feed[:, :, :units].reshape(width, -1)
        w_down = feed[:, :, units:].reshape(width, -1)
        gain_one, shift_one, bias_dense, gain_two, shift_two, bias_down = (
            wide[i, layer] for i in range(6)
        )
        bias_query, bias_value, bias_up = (
            tall[layer, :, begin : begin + size]
            for begin, size in ((0, HD), (HD, HD), (2 * HD, units))
        )
        normed_one = joined_rows(send_rows(norm_forward(hidden, gain_one, shift_one)))
        projected = product("rd,dn->rn", normed_one, w_qkv)
        projected = projected.reshape(slice_len, n_z, 3, HD)
        queries = (projected[:, :, 0] + bias_query[None]).astype(bf16).transpose(1, 0, 2)
        keys = projected[:, :, 1].astype(bf16)
        values = (projected[:, :, 2] + bias_value[None]).astype(bf16)
        both = jnp.concatenate((keys, values), axis=2).transpose(1, 0, 2)
        both = gather(both, SEQ, n_s)
        if layer == 0:
            later = [to_planes([after(block, both[0]) for block in shards[1][0]])]
            later.append(to_planes([after(block, later[0]) for block in shards[1][1]]))
            cot_rows = own_rows(after(cot, both[0]))
        else:
            cot_rows = send_rows(after(cot_rows, both[0]))
        both = jnp.concatenate(both, axis=1)
        keys, values = both[..., :HD], both[..., HD:]
        context, log_total = attend_forward(queries, keys, values, query_pos, key_pos, slopes)
        context = context.astype(bf16).transpose(1, 0, 2).reshape(slice_len, -1)
        got = send_sums(product("rc,dc->rd", context, w_dense))
        if layer == 0:
            got, later, cot_rows = meet(got, later, cot_rows)
            messages.extend(to_planes_of(shard) for shard in later)
            cot_rows = to_inner(cot_rows)
        else:
            got, cot_rows = meet(got, cot_rows)
        hidden_mid = hidden + add_all(got) + bias_dense
        normed_two = joined_rows(send_rows(norm_forward(hidden_mid, gain_two, shift_two)))
        pre_up = product("rd,df->rf", normed_two, w_up) + bias_up.reshape(-1)
        activation = gelu_tanh(pre_up).astype(bf16)
        got = send_sums(product("rf,df->rd", activation, w_down))
        hidden_next = hidden_mid + add_all(got) + bias_down
        records.append(
            (
                (w_qkv, w_dense, w_up, w_down, gain_one, gain_two),
                (hidden, hidden_mid, normed_one, normed_two),
                (queries, keys, values, log_total, context, pre_up, activation),
            )
        )
        hidden = hidden_next

    output_low = to_outer(hidden.astype(bf16))

    gradient = cot_rows[0].astype(f32)
    grad_low = joined_rows(cot_rows)
    wide_grads = [None] * LAYERS
    tall_grads = [None] * LAYERS

    def core_sum(grad):
        blocks = grad.reshape(n_s, part, n_z, -1)
        mine = sum_blocks([blocks[step] for step in range(n_s)], SEQ, n_s).astype(bf16)
        return mine.transpose(1, 0, 2)

    def head_sum(mine):
        return lax.psum_scatter(mine, HEAD, scatter_dimension=0, tiled=False)

    def send_shares(mine):
        mine = mine.reshape(n_t, cut, -1)
        blocks = [lax.dynamic_index_in_dim(mine, d ^ step, 0, False) for step in range(n_t)]
        return deal(blocks, DP, n_t)

    def share_of(got):
        return jnp.stack(flip_list(got, d), axis=1).astype(f32)

    feed_shares = [None] * LAYERS
    mixed_shares = [None] * LAYERS
    feed_sums = [None] * LAYERS
    mixed_sums = [None] * LAYERS
    for layer in reversed(range(LAYERS)):
        (
            (w_qkv, w_dense, w_up, w_down, gain_one, gain_two),
            (hidden, hidden_mid, normed_one, normed_two),
            (queries, keys, values, log_total, context, pre_up, activation),
        ) = records[layer]
        last = layer == LAYERS - 1
        down_bias_grad = jnp.sum(gradient, axis=0)
        act_grad = product("rd,df->rf", grad_low, w_down)
        pre_grad = jax.vjp(gelu_tanh, pre_up)[1](act_grad)[0].astype(bf16)
        got = send_sums(product("rf,df->rd", pre_grad, w_up))
        down_grad = product("rd,rf->df", grad_low, activation).astype(bf16)
        up_grad = product("rd,rf->df", normed_two, pre_grad).astype(bf16)
        feed_grad = jnp.concatenate(
            (up_grad.reshape(width, n_z, -1), down_grad.reshape(width, n_z, -1)), axis=2
        )
        up_bias_grad = jnp.sum(pre_grad, axis=0, dtype=f32).reshape(n_z, -1)
        if last:
            got, feed_grad, output_low = meet(got, feed_grad, output_low)
            output_planes = to_planes_of(output_low)
        else:
            got, feed_grad, feed_got = meet(got, feed_grad, send_shares(feed_sums[layer + 1]))
            feed_shares[layer + 1] = share_of(feed_got)
        e = add_all(got)
        part_mid, gain_two_grad, shift_two_grad = norm_backward(hidden_mid, gain_two, e)
        mid_grad = gradient + part_mid
        dense_bias_grad = jnp.sum(mid_grad, axis=0)
        got, mine = meet(send_rows(mid_grad.astype(bf16)), core_sum(feed_grad))
        feed_sums[layer] = head_sum(mine)
        mid_low = joined_rows(got)
        context_grad = product("rd,dc->rc", mid_low, w_dense).astype(bf16)
        context_grad = context_grad.reshape(slice_len, n_z, HD).transpose(1, 0, 2)
        dense_grad = product("rd,rc->dc", mid_low, context).astype(bf16).reshape(width, n_z, -1)
        query_grad, key_grad, value_grad = attend_backward(
            queries, keys, values, context_grad, log_total, query_pos, key_pos, slopes
        )
        both = jnp.concatenate((key_grad, value_grad), axis=2).astype(bf16)
        both = both.reshape(n_z, n_s, slice_len, 2 * HD)
        got, dense_grad = meet(deal([both[:, step] for step in range(n_s)], SEQ, n_s), dense_grad)
        both = add_all(got).astype(bf16)
        query_grad = query_grad.astype(bf16)
        query_bias_grad = jnp.sum(query_grad, axis=1, dtype=f32)
        value_bias_grad = jnp.sum(both[..., HD:], axis=1, dtype=f32)
        joined = jnp.concatenate((query_grad, both), axis=2)
        joined = joined.transpose(1, 0, 2).reshape(slice_len, -1)
        got = send_sums(product("rn,dn->rd", joined, w_qkv))
        qkv_grad = product("rd,rn->dn", normed_one, joined).astype(bf16).reshape(width, n_z, -1)
        mixed_grad = jnp.concatenate((qkv_grad, dense_grad), axis=2)
        if last:
            got, mixed_grad, output_got = meet(got, mixed_grad, send_output(output_planes))
            output = output_of(output_got)
        else:
            mine = core_sum(mixed_grad)
            got, mine, mixed_got = meet(got, mine, send_shares(mixed_sums[layer + 1]))
            mixed_shares[layer + 1] = share_of(mixed_got)
            mixed_sums[layer] = head_sum(mine)
        e = add_all(got)
        part_in, gain_one_grad, shift_one_grad = norm_backward(hidden, gain_one, e)
        gradient = mid_grad + part_in
        if layer > 0:
            got, mine = meet(send_rows(gradient.astype(bf16)), core_sum(mixed_grad))
            mixed_sums[layer] = head_sum(mine)
            grad_low = joined_rows(got)
        wide_grads[layer] = jnp.stack(
            (
                gain_one_grad,
                shift_one_grad,
                dense_bias_grad,
                gain_two_grad,
                shift_two_grad,
                down_bias_grad,
            )
        )
        tall_grads[layer] = jnp.concatenate(
            (query_bias_grad, value_bias_grad, up_bias_grad), axis=1
        )

    tokens_planes = to_planes_of(to_outer(gradient.astype(bf16)))
    feed_shares[0] = share_of(send_shares(feed_sums[0]))
    mixed_shares[0] = share_of(send_shares(mixed_sums[0]))
    tokens_grad = output_of(send_output(tokens_planes)).astype(f32)

    def fold(arrays, name, size):
        total = arrays[0]
        for step in range(1, size):
            total = total + swap(arrays[step], name, size, step)
        return total

    wide = jnp.stack(wide_grads).reshape(LAYERS * 6, n_s, n_t, cut)
    pieces, begin = [], 0
    tall = jnp.stack(tall_grads)
    for size in tall_sizes:
        piece = tall[:, :, begin : begin + size]
        begin += size
        piece = piece.reshape(LAYERS, n_z, n_t, n_s, size // (n_t * n_s))
        pieces.append(flip(flip(piece, c, 3), z, 1))
    tall = jnp.concatenate(
        [piece.transpose(3, 1, 2, 0, 4).reshape(n_s, n_z, n_t, -1) for piece in pieces], axis=3
    )
    wide = wide.transpose(1, 2, 0, 3).reshape(n_s, n_t, -1)
    n_wide = wide.shape[2]
    wide = jnp.broadcast_to(wide[:, None], (n_s, n_z) + wide.shape[1:])
    joint = jnp.concatenate((wide, tall), axis=3)
    joint = fold([joint[step] for step in range(n_s)], SEQ, n_s)
    joint = fold([joint[step] for step in range(n_z)], HEAD, n_z)
    joint = flip(joint, d)
    got = deal([joint[step] for step in range(n_t)], DP, n_t)
    wide = functools.reduce(jnp.add, [item[:n_wide] for item in got])
    wide = wide.reshape(LAYERS, 6, cut)
    tall = flip(jnp.stack([item[n_wide:] for item in got]), d)
    outs, begin = [], 0
    for size in tall_sizes:
        size = size // (n_t * n_s)
        piece = tall[:, begin : begin + LAYERS * size].reshape(n_t, LAYERS, size)
        begin += LAYERS * size
        outs.append(piece.transpose(1, 0, 2))
    query_bias_grad, value_bias_grad, up_bias_grad = outs
    qkv_grad = jnp.stack([share[:, :, :qkv_columns].reshape(cut, -1) for share in mixed_shares])
    dense_grad = jnp.stack([share[:, :, qkv_columns:].reshape(cut, -1).T for share in mixed_shares])
    up_grad = jnp.stack([share[:, :, :units].reshape(cut, -1) for share in feed_shares])
    down_grad = jnp.stack([share[:, :, units:].reshape(cut, -1).T for share in feed_shares])
    return (
        output,
        tokens_grad,
        qkv_grad,
        dense_grad,
        up_grad,
        down_grad,
        wide[:, 0],
        wide[:, 1],
        query_bias_grad,
        value_bias_grad,
        wide[:, 2],
        wide[:, 3],
        wide[:, 4],
        up_bias_grad,
        wide[:, 5],
    )


def solution(mesh):
    sizes = tuple(mesh.shape[name] for name in (DP, SEQ, HEAD))
    rows = P(DP, SEQ, None)
    tall = P(None, (DP, SEQ), HEAD)
    flat = P(None, HEAD, (DP, SEQ))
    vector = P(None, (DP, SEQ))
    params = (
        tall,
        flat,
        tall,
        flat,
        vector,
        vector,
        flat,
        flat,
        vector,
        vector,
        vector,
        flat,
        vector,
    )
    return jax.shard_map(
        functools.partial(per_device, sizes),
        mesh=mesh,
        in_specs=(rows,) + params + (rows,),
        out_specs=(rows, rows) + params,
        check_vma=False,
    )
```

```python
import functools
import math

import jax
import jax.numpy as jnp
from jax import lax
from jax.experimental import pallas as pl
from jax.experimental.pallas import tpu as pltpu
from jax.sharding import PartitionSpec as P

H = 16
HD = 64
LAYERS = 2
DP, SEQ, HEAD = "dp", "seq", "head"

epsilon = 1e-05
masked_value = -1000000000.0
bf16 = jnp.bfloat16
f32 = jnp.float32


def flip_list(blocks, index):
    bit = 1
    while bit < len(blocks):
        turn = (index & bit) != 0
        blocks = [jnp.where(turn, blocks[j ^ bit], blocks[j]) for j in range(len(blocks))]
        bit *= 2
    return blocks


def flip(array, index, axis=0):
    blocks = [lax.index_in_dim(array, j, axis, keepdims=True) for j in range(array.shape[axis])]
    return jnp.concatenate(flip_list(blocks, index), axis=axis)


def swap(array, name, size, step):
    return lax.ppermute(array, name, [(i, i ^ step) for i in range(size)])


def gather(array, name, size):
    return [array] + [swap(array, name, size, step) for step in range(1, size)]


def deal(blocks, name, size):
    return [blocks[0]] + [swap(blocks[step], name, size, step) for step in range(1, size)]


def meet(*groups):
    return lax.optimization_barrier(groups)


def add_all(blocks):
    return functools.reduce(jnp.add, [block.astype(f32) for block in blocks])


def sum_blocks(blocks, name, size):
    total = blocks[0].astype(f32)
    for step in range(1, size):
        total = total + swap(blocks[step].astype(bf16), name, size, step).astype(f32)
    return total


def after(array, *others):
    return lax.optimization_barrier((array,) + others)[0]


def dot(left, right, left_dim, right_dim):
    dims = (((left_dim,), (right_dim,)), ((), ()))
    return lax.dot_general(left, right, dims, preferred_element_type=f32)


def gelu_tanh(values):
    argument = 0.7978845608028654 * (values + 0.044715 * values * values * values)
    return 0.5 * values * (1.0 + jnp.tanh(argument))


def gelu_slope(values):
    square = values * values
    bent = jnp.tanh(0.7978845608028654 * (values + 0.044715 * values * square))
    inner = 0.7978845608028654 * (1.0 + 3.0 * 0.044715 * square)
    return 0.5 * (1.0 + bent) + 0.5 * values * (1.0 - bent * bent) * inner


def norm_parts(values):
    row_mean = jnp.mean(values, axis=-1, keepdims=True)
    centred = values - row_mean
    scale = lax.rsqrt(jnp.mean(centred * centred, axis=-1, keepdims=True) + epsilon)
    return centred * scale, scale


def run(body, steps, each_in, whole_in, each_out, whole_out, scratch=(), flops=0):
    def each(array):
        zeros = (0,) * (len(array.shape) - 1)
        return pl.BlockSpec((None,) + tuple(array.shape[1:]), lambda z: (z,) + zeros)

    def whole(array):
        zeros = (0,) * len(array.shape)
        return pl.BlockSpec(tuple(array.shape), lambda z: zeros)

    counts = [len(part) for part in (each_in, whole_in, each_out, whole_out)]

    def kernel(*refs):
        parts, begin = [], 0
        for count in counts:
            parts.append(refs[begin : begin + count])
            begin += count
        body(pl.program_id(0), *parts, refs[begin:])

    arrays = list(each_in) + list(whole_in)
    shapes = list(each_out) + list(whole_out)
    moved = sum(math.prod(item.shape) * item.dtype.itemsize for item in arrays + shapes)
    return pl.pallas_call(
        kernel,
        grid=(steps,),
        in_specs=[each(item) for item in each_in] + [whole(item) for item in whole_in],
        out_specs=[each(item) for item in each_out] + [whole(item) for item in whole_out],
        out_shape=shapes,
        scratch_shapes=list(scratch),
        compiler_params=pltpu.CompilerParams(vmem_limit_bytes=48 * 1024 * 1024),
        cost_estimate=pl.CostEstimate(flops=flops, bytes_accessed=moved, transcendentals=0),
    )(*arrays)


def shape(dims, kind):
    return jax.ShapeDtypeStruct(tuple(dims), kind)


def lay(target, blocks):
    rows = blocks[0].shape[0]
    for index, block in enumerate(blocks):
        target[index * rows : (index + 1) * rows, :] = block[...]


def spread(blocks, source):
    rows = blocks[0].shape[0]
    for index, block in enumerate(blocks):
        block[...] = source[index * rows : (index + 1) * rows, :].astype(block.dtype)


def pieces(array, planes):
    part = planes[0].shape[0]
    return [array[:, s * part : (s + 1) * part] for s in range(len(planes))]


def times(array, planes, begin, end):
    total = None
    for piece, plane in zip(pieces(array, planes), planes):
        term = dot(piece, plane[:, begin:end], 1, 0)
        total = term if total is None else total + term
    return total


def add_back(acc, array, planes, begin, end):
    part = planes[0].shape[0]
    for s, plane in enumerate(planes):
        acc[:, s * part : (s + 1) * part] += dot(array, plane[:, begin:end], 1, 1)


def project(blocks, planes, bias):
    rows, width = blocks[0].shape
    length = rows * len(blocks)
    heads = planes[0].shape[0]
    n = len(planes)

    def body(z, each_in, whole_in, each_out, whole_out, scratch):
        @pl.when(z == 0)
        def _():
            lay(scratch[0], whole_in)

        got = times(scratch[0], each_in[:n], 0, 3 * HD) + each_in[n][...]
        low = got.astype(bf16)
        each_out[0][...] = low[:, :HD] * jnp.asarray(1.0 / math.sqrt(HD), bf16)
        each_out[1][...] = low[:, HD:]

    return run(
        body,
        heads,
        list(planes) + [bias],
        blocks,
        [shape((heads, length, HD), bf16), shape((heads, length, 2 * HD), bf16)],
        [],
        [pltpu.VMEM((length, width), bf16)],
        2 * heads * length * width * 3 * HD,
    )


def masked_scores(queries, both, slope, key_pos, query_pos):
    scores = dot(queries, both[:, :HD], 1, 1) + slope * key_pos
    return jnp.where(key_pos <= query_pos, scores, masked_value)


def attend(queries, both, planes, slopes, key_pos, query_pos, n_t):
    heads, length, _ = queries.shape
    n = len(planes)
    width = planes[0].shape[1] * n
    rows = length // n_t

    def body(z, each_in, whole_in, each_out, whole_out, scratch):
        kv, weights = each_in[1 : 1 + n], each_in[1 + n : 1 + 2 * n]
        slope = each_in[1 + 2 * n][:, :1]
        acc = scratch[0]

        @pl.when(z == 0)
        def _():
            acc[...] = jnp.zeros_like(acc)

        low_queries = each_in[0][...]
        scores = [
            masked_scores(low_queries, kv[s], slope, whole_in[0][s], whole_in[1][...])
            for s in range(n)
        ]
        top = functools.reduce(jnp.maximum, [jnp.max(x, axis=1, keepdims=True) for x in scores])
        shifted = [jnp.exp(x - top) for x in scores]
        total = sum(jnp.sum(x, axis=1, keepdims=True) for x in shifted)
        context = sum(dot(x.astype(bf16), kv[s][:, HD:], 1, 0) for s, x in enumerate(shifted))
        low = (context / total).astype(bf16)
        each_out[0][...] = low
        each_out[1][...] = top + jnp.log(total)
        add_back(acc, low, weights, 3 * HD, 4 * HD)

        @pl.when(z == heads - 1)
        def _():
            spread(whole_out, acc)

    out = run(
        body,
        heads,
        [queries] + list(both) + list(planes) + [slopes],
        [key_pos, query_pos],
        [shape((heads, length, HD), bf16), shape((heads, length, 1), f32)],
        [shape((rows, width), bf16)] * n_t,
        [pltpu.VMEM((length, width), f32)],
        2 * heads * length * (2 * HD * length * n + HD * width),
    )
    return out[0], out[1], out[2:]


def attend_back(blocks, queries, both, planes, context, logs, slopes, key_pos, query_pos):
    heads, length, _ = queries.shape
    n = len(planes)
    width = blocks[0].shape[1]

    def body(z, each_in, whole_in, each_out, whole_out, scratch):
        @pl.when(z == 0)
        def _():
            lay(scratch[0], whole_in[2:])

        kv, weights = each_in[1 : 1 + n], each_in[1 + n : 1 + 2 * n]
        context_ref, logs_ref, slope_ref = each_in[1 + 2 * n :]
        slope = slope_ref[:, :1]
        low_queries = each_in[0][...]
        grads = times(scratch[0], weights, 3 * HD, 4 * HD).astype(bf16)
        inner = jnp.sum(grads.astype(f32) * context_ref[...].astype(f32), axis=1, keepdims=True)
        query_grad = None
        for s in range(n):
            scores = masked_scores(low_queries, kv[s], slope, whole_in[0][s], whole_in[1][...])
            probs = jnp.exp(scores - logs_ref[...])
            prob_grad = dot(grads, kv[s][:, HD:], 1, 1)
            score_grad = (probs * (prob_grad - inner)).astype(bf16)
            term = dot(score_grad, kv[s][:, :HD], 1, 0)
            query_grad = term if query_grad is None else query_grad + term
            each_out[1 + s][:, :HD] = dot(score_grad, low_queries, 0, 0).astype(bf16)
            each_out[1 + s][:, HD:] = dot(probs.astype(bf16), grads, 0, 0).astype(bf16)
        each_out[0][...] = (query_grad * (1.0 / math.sqrt(HD))).astype(bf16)

    out = run(
        body,
        heads,
        [queries] + list(both) + list(planes) + [context, logs, slopes],
        [key_pos, query_pos] + list(blocks),
        [shape((heads, length, HD), bf16)] + [shape((heads, length, 2 * HD), bf16)] * n,
        [],
        [pltpu.VMEM((length, width), bf16)],
        2 * heads * length * (5 * HD * length * n + HD * width),
    )
    return out[0], out[1:]


def project_back(query_grad, both_grads, planes, n_t):
    heads, length, _ = query_grad.shape
    n = len(planes)
    width = planes[0].shape[1] * n
    rows = length // n_t

    def body(z, each_in, whole_in, each_out, whole_out, scratch):
        acc = scratch[0]

        @pl.when(z == 0)
        def _():
            acc[...] = jnp.zeros_like(acc)

        low = sum(item[...].astype(f32) for item in each_in[1 : 1 + n]).astype(bf16)
        joined, sums = each_out
        joined[:, :HD] = each_in[0][...]
        joined[:, HD:] = low
        sums[:, :HD] = jnp.sum(each_in[0][...].astype(f32), axis=0, keepdims=True)
        sums[:, HD:] = jnp.sum(low.astype(f32), axis=0, keepdims=True)
        add_back(acc, joined[...], each_in[1 + n :], 0, 3 * HD)

        @pl.when(z == heads - 1)
        def _():
            spread(whole_out, acc)

    out = run(
        body,
        heads,
        [query_grad] + list(both_grads) + list(planes),
        [],
        [shape((heads, length, 3 * HD), bf16), shape((heads, 1, 3 * HD), f32)],
        [shape((rows, width), bf16)] * n_t,
        [pltpu.VMEM((length, width), f32)],
        2 * heads * length * width * 3 * HD,
    )
    return out[0], out[1], out[2:]


def feed_forward(blocks, planes, bias):
    rows, width = blocks[0].shape
    length = rows * len(blocks)
    heads, _, units = bias.shape
    n = len(planes)

    def body(z, each_in, whole_in, each_out, whole_out, scratch):
        wide, acc = scratch

        @pl.when(z == 0)
        def _():
            lay(wide, whole_in)
            acc[...] = jnp.zeros_like(acc)

        pre_up = times(wide, each_in[:n], 0, units) + each_in[n][...]
        each_out[0][...] = pre_up
        low = gelu_tanh(pre_up).astype(bf16)
        each_out[1][...] = low
        add_back(acc, low, each_in[:n], units, 2 * units)

        @pl.when(z == heads - 1)
        def _():
            spread(whole_out, acc)

    out = run(
        body,
        heads,
        list(planes) + [bias],
        blocks,
        [shape((heads, length, units), f32), shape((heads, length, units), bf16)],
        [shape((rows, width), bf16)] * len(blocks),
        [pltpu.VMEM((length, width), bf16), pltpu.VMEM((length, width), f32)],
        4 * heads * length * width * units,
    )
    return out[0], out[1], out[2:]


def feed_back(blocks, planes, pre_up):
    rows, width = blocks[0].shape
    length = rows * len(blocks)
    heads, _, units = pre_up.shape
    n = len(planes)

    def body(z, each_in, whole_in, each_out, whole_out, scratch):
        wide, acc = scratch

        @pl.when(z == 0)
        def _():
            lay(wide, whole_in)
            acc[...] = jnp.zeros_like(acc)

        act_grad = times(wide, each_in[:n], units, 2 * units)
        low = (act_grad * gelu_slope(each_in[n][...])).astype(bf16)
        each_out[0][...] = low
        each_out[1][...] = jnp.sum(low.astype(f32), axis=0, keepdims=True)
        add_back(acc, low, each_in[:n], 0, units)

        @pl.when(z == heads - 1)
        def _():
            spread(whole_out, acc)

    out = run(
        body,
        heads,
        list(planes) + [pre_up],
        blocks,
        [shape((heads, length, units), bf16), shape((heads, 1, units), f32)],
        [shape((rows, width), bf16)] * len(blocks),
        [pltpu.VMEM((length, width), bf16), pltpu.VMEM((length, width), f32)],
        4 * heads * length * width * units,
    )
    return out[0], out[1], out[2:]


def weight_back(one_blocks, one, two_blocks, two, n):
    rows, width = one_blocks[0].shape
    length = rows * len(one_blocks)
    heads, _, first = one.shape
    second = two.shape[2]
    part = width // n
    half = len(one_blocks)

    def body(z, each_in, whole_in, each_out, whole_out, scratch):
        @pl.when(z == 0)
        def _():
            lay(scratch[0], whole_in[:half])
            lay(scratch[1], whole_in[half:])

        for s in range(n):
            cols = slice(s * part, (s + 1) * part)
            each_out[s][:, :first] = dot(scratch[0][:, cols], each_in[0][...], 0, 0).astype(bf16)
            each_out[s][:, first:] = dot(scratch[1][:, cols], each_in[1][...], 0, 0).astype(bf16)

    return run(
        body,
        heads,
        [one, two],
        list(one_blocks) + list(two_blocks),
        [shape((heads, part, first + second), bf16)] * n,
        [],
        [pltpu.VMEM((length, width), bf16)] * 2,
        2 * heads * length * width * (first + second),
    )


def norm_forward(values, got, bias, gain, shift):
    def body(z, each_in, whole_in, each_out, whole_out, scratch):
        start, bias_ref, gain_ref, shift_ref = whole_in[:4]
        total = start[...] + bias_ref[...]
        for item in whole_in[4:]:
            total = total + item[...].astype(f32)
        whole_out[0][...] = total
        xhat, _ = norm_parts(total)
        whole_out[1][...] = (xhat * gain_ref[...] + shift_ref[...]).astype(bf16)

    return run(
        body,
        1,
        [],
        [values, bias[None], gain[None], shift[None]] + list(got),
        [],
        [shape(values.shape, f32), shape(values.shape, bf16)],
    )


def norm_back(values, gradient, got, gain):
    width = values.shape[1]

    def body(z, each_in, whole_in, each_out, whole_out, scratch):
        e = sum(item[...].astype(f32) for item in whole_in[3:])
        xhat, scale = norm_parts(whole_in[0][...])
        eg = e * whole_in[2][...]
        back = scale * (
            eg
            - jnp.mean(eg, axis=-1, keepdims=True)
            - xhat * jnp.mean(eg * xhat, axis=-1, keepdims=True)
        )
        fresh = whole_in[1][...] + back
        whole_out[0][...] = fresh
        whole_out[1][...] = fresh.astype(bf16)
        whole_out[2][0:1, :] = jnp.sum(e * xhat, axis=0, keepdims=True)
        whole_out[2][1:2, :] = jnp.sum(e, axis=0, keepdims=True)
        whole_out[2][2:3, :] = jnp.sum(fresh, axis=0, keepdims=True)

    return run(
        body,
        1,
        [],
        [values, gradient, gain[None]] + list(got),
        [],
        [shape(values.shape, f32), shape(values.shape, bf16), shape((3, width), f32)],
    )


def per_device(
    sizes,
    tokens,
    qkv_weight,
    dense_weight,
    up_weight,
    down_weight,
    first_gain,
    first_shift,
    query_bias,
    value_bias,
    dense_bias,
    second_gain,
    second_shift,
    up_bias,
    down_bias,
    cotangent,
):
    n_t, n_s, n_z = sizes
    seq_count, slice_len, width = tokens.shape
    assert seq_count == 1 and n_t == n_z
    d, c, z = (lax.axis_index(name) for name in (DP, SEQ, HEAD))
    rows = slice_len // n_t
    cut = qkv_weight.shape[1]
    part = cut * n_t
    heads = query_bias.shape[1]
    assert heads == n_t
    units = up_bias.shape[2] * n_t * n_s

    def to_inner(array):
        lead = array.shape[:-1]
        array = array.reshape(lead + (n_t, n_s, cut))
        array = jnp.moveaxis(array, -2, -3)
        return flip(array, c, len(lead)).reshape(lead + (width,))

    def to_outer(array):
        lead = array.shape[:-1]
        array = flip(array.reshape(lead + (n_s, n_t, cut)), c, len(lead))
        return jnp.moveaxis(array, -2, -3).reshape(lead + (width,))

    def own_rows(array):
        cuts = array.reshape(n_t, rows, width)
        blocks = [lax.dynamic_index_in_dim(cuts, d ^ step, 0, False) for step in range(n_t)]
        total = jnp.where(d == z, blocks[0], jnp.zeros_like(blocks[0]))
        for step in range(1, n_t):
            pairs = [(i * n_z + i, (i ^ step) * n_z + i) for i in range(n_t)]
            total = total + lax.ppermute(blocks[step], (DP, HEAD), pairs)
        return total

    def send_rows(array):
        return gather(array, DP, n_t)

    def send_sums(blocks):
        return deal(blocks, DP, n_t)

    def to_planes_of(array):
        return lax.all_gather(array, HEAD, axis=0, tiled=False)

    def send_output(planes):
        blocks = [lax.dynamic_index_in_dim(planes, d ^ step, 0, False) for step in range(n_t)]
        return deal(blocks, DP, n_t)

    def output_of(got):
        return jnp.concatenate(flip_list(got, d), axis=0).reshape(1, slice_len, width)

    def packed(layer):
        qkv = qkv_weight[layer].reshape(cut, n_t, -1)
        dense = dense_weight[layer].T.reshape(cut, n_t, -1)
        up = up_weight[layer].reshape(cut, n_t, -1)
        down = down_weight[layer].T.reshape(cut, n_t, -1)
        return tuple(
            [jnp.concatenate((one[:, j], two[:, j]), axis=1) for j in range(n_t)]
            for one, two in ((qkv, dense), (up, down))
        )

    def to_planes(blocks):
        got = deal(flip_list(blocks, d), DP, n_t)
        return jnp.concatenate(flip_list(got, d), axis=0)

    def join(planes):
        return gather(planes, SEQ, n_s)

    shards = [packed(layer) for layer in range(LAYERS)]
    first_shard = to_planes(shards[0][0])
    messages = [to_planes_of(first_shard)]
    start_rows = own_rows(tokens[0])

    wide = jnp.concatenate(
        (first_gain, first_shift, dense_bias, second_gain, second_shift, down_bias), axis=0
    )
    tall = jnp.concatenate((query_bias, value_bias, up_bias), axis=2)
    small = jnp.concatenate((wide, tall.reshape(-1, cut)), axis=0)
    small = after(small, first_shard)
    small = lax.all_gather(small, (DP, SEQ), axis=0, tiled=False)
    small = small.reshape((n_t, n_s) + small.shape[1:])
    wide = small[:, :, : 6 * LAYERS].transpose(2, 1, 0, 3)
    wide = flip(wide, c, 1).reshape(6, LAYERS, width)
    each = small[:, :, 6 * LAYERS :].reshape(n_t, n_s, LAYERS, heads, -1)
    each = lax.dynamic_index_in_dim(each, d, axis=3, keepdims=False)
    tall = []
    begin = 0
    tall_sizes = (HD, HD, units)
    for size in tall_sizes:
        size = size // (n_t * n_s)
        piece = each[:, :, :, begin : begin + size]
        begin += size
        tall.append(piece.transpose(2, 0, 1, 3).reshape(LAYERS, -1))
    tall = jnp.concatenate(tall, axis=1)
    tall = jnp.stack(flip_list(gather(tall, HEAD, n_z), z), axis=1)

    hidden = to_inner(start_rows).astype(f32)
    second_shard = to_planes([after(block, small) for block in shards[0][1]])
    messages.append(to_planes_of(second_shard))

    qkv_columns = 3 * HD
    head_ids = jnp.arange(n_z, dtype=jnp.int32) * heads + d
    slopes = 2.0 ** (-8.0 * (head_ids + 1).astype(f32) / H)
    slopes = jnp.broadcast_to(slopes[:, None, None], (n_z, 1, 128))
    block_ids = (d ^ jnp.arange(n_t, dtype=jnp.int32)) * rows
    own_pos = (block_ids[:, None] + jnp.arange(rows, dtype=jnp.int32)[None]).reshape(-1)
    query_pos = (c * slice_len + own_pos).astype(f32)[:, None]
    others = (c ^ jnp.arange(n_s, dtype=jnp.int32)) * slice_len
    key_pos = (others[:, None] + own_pos[None]).astype(f32)[:, None, :]
    none = jnp.zeros((width,), f32)

    cot = cotangent[0]
    records = []
    _, low = norm_forward(hidden, [], none, wide[0, 0], wide[1, 0])
    for layer in range(LAYERS):
        mixed, feed = (join(planes) for planes in messages[2 * layer : 2 * layer + 2])
        gain_one, _, bias_dense, gain_two, shift_two, bias_down = (wide[i, layer] for i in range(6))
        zeros = jnp.zeros((n_z, HD), f32)
        bias_qkv = jnp.concatenate((tall[layer, :, :HD], zeros, tall[layer, :, HD : 2 * HD]), 1)
        bias_up = tall[layer, :, 2 * HD :][:, None]
        normed_one = send_rows(low)
        queries, both = project(normed_one, mixed, bias_qkv[:, None])
        both = gather(both, SEQ, n_s)
        if layer == 0:
            later = [to_planes([after(block, both[0]) for block in shards[1][0]])]
            later.append(to_planes([after(block, later[0]) for block in shards[1][1]]))
            cot_rows = own_rows(after(cot, both[0]))
        else:
            cot_rows = send_rows(after(cot_rows, both[0]))
        context, logs, out = attend(queries, both, mixed, slopes, key_pos, query_pos, n_t)
        got = send_sums(out)
        if layer == 0:
            got, later, cot_rows = meet(got, later, cot_rows)
            messages.extend(to_planes_of(shard) for shard in later)
            cot_rows = to_inner(cot_rows)
        else:
            got, cot_rows = meet(got, cot_rows)
        hidden_mid, low = norm_forward(hidden, got, bias_dense, gain_two, shift_two)
        normed_two = send_rows(low)
        pre_up, activation, out = feed_forward(normed_two, feed, bias_up)
        got = send_sums(out)
        records.append(
            (
                (mixed, feed, gain_one, gain_two),
                (hidden, hidden_mid, normed_one, normed_two),
                (queries, both, logs, context, pre_up, activation),
            )
        )
        if layer + 1 < LAYERS:
            hidden, low = norm_forward(
                hidden_mid, got, bias_down, wide[0, layer + 1], wide[1, layer + 1]
            )
        else:
            hidden = hidden_mid + add_all(got) + bias_down

    output_low = to_outer(hidden.astype(bf16))

    gradient = cot_rows[0].astype(f32)
    grad_low = cot_rows
    down_bias_grad = jnp.sum(gradient, axis=0, keepdims=True)
    wide_grads = [None] * LAYERS
    tall_grads = [None] * LAYERS

    def core_sum(blocks):
        return sum_blocks(blocks, SEQ, n_s).astype(bf16)

    def head_sum(mine):
        return lax.psum_scatter(mine, HEAD, scatter_dimension=0, tiled=False)

    def send_shares(mine):
        mine = mine.reshape(n_t, cut, -1)
        blocks = [lax.dynamic_index_in_dim(mine, d ^ step, 0, False) for step in range(n_t)]
        return deal(blocks, DP, n_t)

    def share_of(got):
        return jnp.stack(flip_list(got, d), axis=1).astype(f32)

    feed_shares = [None] * LAYERS
    mixed_shares = [None] * LAYERS
    feed_sums = [None] * LAYERS
    mixed_sums = [None] * LAYERS
    for layer in reversed(range(LAYERS)):
        (
            (mixed, feed, gain_one, gain_two),
            (hidden, hidden_mid, normed_one, normed_two),
            (queries, both, logs, context, pre_up, activation),
        ) = records[layer]
        last = layer == LAYERS - 1
        pre_grad, up_bias_grad, out = feed_back(grad_low, feed, pre_up)
        got = send_sums(out)
        feed_grad = weight_back(normed_two, pre_grad, grad_low, activation, n_s)
        if last:
            got, feed_grad, output_low = meet(got, feed_grad, output_low)
            output_planes = to_planes_of(output_low)
        else:
            got, feed_grad, feed_got = meet(got, feed_grad, send_shares(feed_sums[layer + 1]))
            feed_shares[layer + 1] = share_of(feed_got)
        mid_grad, low, sums_two = norm_back(hidden_mid, gradient, got, gain_two)
        mid_low = send_rows(low)
        mine = core_sum(feed_grad)
        if last:
            mid_low, mine = meet(mid_low, mine)
        else:
            mid_low, mine, mixed_got = meet(mid_low, mine, send_shares(mixed_sums[layer + 1]))
            mixed_shares[layer + 1] = share_of(mixed_got)
        feed_sums[layer] = head_sum(mine)
        query_grad, both_grads = attend_back(
            mid_low, queries, both, mixed, context, logs, slopes, key_pos, query_pos
        )
        got = deal(both_grads, SEQ, n_s)
        joined, qkv_sums, out = project_back(query_grad, got, mixed, n_t)
        got = send_sums(out)
        mixed_grad = weight_back(normed_one, joined, mid_low, context, n_s)
        if last:
            planes = after(output_planes, joined)
            got, mixed_grad, output_got = meet(got, mixed_grad, send_output(planes))
            output = output_of(output_got)
        else:
            mine = core_sum(mixed_grad)
            got, mine, feed_got = meet(got, mine, send_shares(after(feed_sums[layer], joined)))
            feed_shares[layer] = share_of(feed_got)
            mixed_sums[layer] = head_sum(mine)
        gradient, low, sums_one = norm_back(hidden, mid_grad, got, gain_one)
        if layer > 0:
            grad_low, mine = meet(send_rows(low), core_sum(mixed_grad))
            mixed_sums[layer] = head_sum(mine)
        wide_grads[layer] = jnp.stack(
            (
                sums_one[0],
                sums_one[1],
                sums_two[2],
                sums_two[0],
                sums_two[1],
                down_bias_grad[0],
            )
        )
        down_bias_grad = sums_one[2:3]
        tall_grads[layer] = jnp.concatenate(
            (qkv_sums[:, 0, :HD], qkv_sums[:, 0, 2 * HD :], up_bias_grad[:, 0]), axis=1
        )

    tokens_planes = to_planes_of(to_outer(low))
    mixed_shares[0] = share_of(send_shares(mixed_sums[0]))
    tokens_grad = output_of(send_output(tokens_planes)).astype(f32)

    def fold(arrays, name, size):
        total = arrays[0]
        for step in range(1, size):
            total = total + swap(arrays[step], name, size, step)
        return total

    wide = jnp.stack(wide_grads).reshape(LAYERS * 6, n_s, n_t, cut)
    pieces, begin = [], 0
    tall = jnp.stack(tall_grads)
    for size in tall_sizes:
        piece = tall[:, :, begin : begin + size]
        begin += size
        piece = piece.reshape(LAYERS, n_z, n_t, n_s, size // (n_t * n_s))
        pieces.append(flip(flip(piece, c, 3), z, 1))
    tall = jnp.concatenate(
        [piece.transpose(3, 1, 2, 0, 4).reshape(n_s, n_z, n_t, -1) for piece in pieces], axis=3
    )
    wide = wide.transpose(1, 2, 0, 3).reshape(n_s, n_t, -1)
    n_wide = wide.shape[2]
    wide = jnp.broadcast_to(wide[:, None], (n_s, n_z) + wide.shape[1:])
    joint = jnp.concatenate((wide, tall), axis=3)
    joint = fold([joint[step] for step in range(n_s)], SEQ, n_s)
    joint = fold([joint[step] for step in range(n_z)], HEAD, n_z)
    joint = flip(joint, d)
    got = deal([joint[step] for step in range(n_t)], DP, n_t)
    wide = functools.reduce(jnp.add, [item[:n_wide] for item in got])
    wide = wide.reshape(LAYERS, 6, cut)
    tall = flip(jnp.stack([item[n_wide:] for item in got]), d)
    outs, begin = [], 0
    for size in tall_sizes:
        size = size // (n_t * n_s)
        piece = tall[:, begin : begin + LAYERS * size].reshape(n_t, LAYERS, size)
        begin += LAYERS * size
        outs.append(piece.transpose(1, 0, 2))
    query_bias_grad, value_bias_grad, up_bias_grad = outs
    qkv_grad = jnp.stack([share[:, :, :qkv_columns].reshape(cut, -1) for share in mixed_shares])
    dense_grad = jnp.stack([share[:, :, qkv_columns:].reshape(cut, -1).T for share in mixed_shares])
    up_grad = jnp.stack([share[:, :, :units].reshape(cut, -1) for share in feed_shares])
    down_grad = jnp.stack([share[:, :, units:].reshape(cut, -1).T for share in feed_shares])
    return (
        output,
        tokens_grad,
        qkv_grad,
        dense_grad,
        up_grad,
        down_grad,
        wide[:, 0],
        wide[:, 1],
        query_bias_grad,
        value_bias_grad,
        wide[:, 2],
        wide[:, 3],
        wide[:, 4],
        up_bias_grad,
        wide[:, 5],
    )


def solution(mesh):
    sizes = tuple(mesh.shape[name] for name in (DP, SEQ, HEAD))
    rows = P(DP, SEQ, None)
    tall = P(None, (DP, SEQ), HEAD)
    flat = P(None, HEAD, (DP, SEQ))
    vector = P(None, (DP, SEQ))
    params = (
        tall,
        flat,
        tall,
        flat,
        vector,
        vector,
        flat,
        flat,
        vector,
        vector,
        vector,
        flat,
        vector,
    )
    return jax.shard_map(
        functools.partial(per_device, sizes),
        mesh=mesh,
        in_specs=(rows,) + params + (rows,),
        out_specs=(rows, rows) + params,
        check_vma=False,
    )
```

```python
import functools
import math

import jax
import jax.numpy as jnp
from jax import lax
from jax.experimental import pallas as pl
from jax.experimental.pallas import tpu as pltpu
from jax.sharding import PartitionSpec as P

H = 16
HD = 64
LAYERS = 2
DP, SEQ, HEAD = "dp", "seq", "head"

epsilon = 1e-05
masked_value = -1000000000.0
VMEM_LIMIT = 48 * 1024 * 1024
bf16 = jnp.bfloat16
f32 = jnp.float32


def flip_list(blocks, index):
    bit = 1
    while bit < len(blocks):
        turn = (index & bit) != 0
        blocks = [
            jax.tree.map(lambda x, y: jnp.where(turn, x, y), blocks[j ^ bit], blocks[j])
            for j in range(len(blocks))
        ]
        bit *= 2
    return blocks


def flip(array, index, axis=0):
    blocks = [lax.index_in_dim(array, j, axis, keepdims=True) for j in range(array.shape[axis])]
    return jnp.concatenate(flip_list(blocks, index), axis=axis)


def swap(array, name, size, step):
    return lax.ppermute(array, name, [(i, i ^ step) for i in range(size)])


def gather(array, name, size):
    return [array] + [swap(array, name, size, step) for step in range(1, size)]


def deal(blocks, name, size):
    return [blocks[0]] + [swap(blocks[step], name, size, step) for step in range(1, size)]


def exchange(array, name):
    return lax.all_to_all(array, name, 0, 0, tiled=True)


def meet(*groups):
    return lax.optimization_barrier(groups)


def add_all(blocks):
    return functools.reduce(jnp.add, [block.astype(f32) for block in blocks])


def sum_blocks(blocks, name, size):
    total = blocks[0].astype(f32)
    for step in range(1, size):
        total = total + swap(blocks[step].astype(bf16), name, size, step).astype(f32)
    return total


def after(array, *others):
    return lax.optimization_barrier((array,) + others)[0]


def dot(left, right, left_dim, right_dim):
    dims = (((left_dim,), (right_dim,)), ((), ()))
    return lax.dot_general(left, right, dims, preferred_element_type=f32)


def gelu_tanh(values):
    argument = 0.7978845608028654 * (values + 0.044715 * values * values * values)
    return 0.5 * values * (1.0 + jnp.tanh(argument))


def gelu_slope(values):
    square = values * values
    bent = jnp.tanh(0.7978845608028654 * (values + 0.044715 * values * square))
    inner = 0.7978845608028654 * (1.0 + 3.0 * 0.044715 * square)
    return 0.5 * (1.0 + bent) + 0.5 * values * (1.0 - bent * bent) * inner


def norm_parts(values):
    row_mean = jnp.mean(values, axis=-1, keepdims=True)
    centred = values - row_mean
    scale = lax.rsqrt(jnp.mean(centred * centred, axis=-1, keepdims=True) + epsilon)
    return centred * scale, scale


def run(body, steps, each_in, whole_in, each_out, whole_out, scratch=(), flops=0):
    def each(array):
        zeros = (0,) * (len(array.shape) - 1)
        return pl.BlockSpec((None,) + tuple(array.shape[1:]), lambda z: (z,) + zeros)

    def whole(array):
        zeros = (0,) * len(array.shape)
        return pl.BlockSpec(tuple(array.shape), lambda z: zeros)

    counts = [len(part) for part in (each_in, whole_in, each_out, whole_out)]

    def kernel(*refs):
        parts, begin = [], 0
        for count in counts:
            parts.append(refs[begin : begin + count])
            begin += count
        body(pl.program_id(0), *parts, refs[begin:])

    arrays = list(each_in) + list(whole_in)
    shapes = list(each_out) + list(whole_out)
    moved = sum(math.prod(item.shape) * item.dtype.itemsize for item in arrays + shapes)
    return pl.pallas_call(
        kernel,
        grid=(steps,),
        in_specs=[each(item) for item in each_in] + [whole(item) for item in whole_in],
        out_specs=[each(item) for item in each_out] + [whole(item) for item in whole_out],
        out_shape=shapes,
        scratch_shapes=list(scratch),
        compiler_params=pltpu.CompilerParams(vmem_limit_bytes=VMEM_LIMIT),
        cost_estimate=pl.CostEstimate(flops=flops, bytes_accessed=moved, transcendentals=0),
    )(*arrays)


def shape(dims, kind):
    return jax.ShapeDtypeStruct(tuple(dims), kind)


def lay(target, blocks):
    rows = blocks[0].shape[0]
    for index, block in enumerate(blocks):
        target[index * rows : (index + 1) * rows, :] = block[...]


def spread(blocks, source):
    rows = blocks[0].shape[0]
    for index, block in enumerate(blocks):
        block[...] = source[index * rows : (index + 1) * rows, :].astype(block.dtype)


def times(array, planes, begin, end):
    part = array.shape[1] // len(planes)
    total = None
    for s, plane in enumerate(planes):
        term = dot(array[:, s * part : (s + 1) * part], plane[:part, begin:end], 1, 0)
        total = term if total is None else total + term
    return total


def add_back(acc, array, planes, begin, end):
    part = acc.shape[1] // len(planes)
    for s, plane in enumerate(planes):
        acc[:, s * part : (s + 1) * part] += dot(array, plane[:part, begin:end], 1, 1)


def project(blocks, planes, bias, gain=None, shift=None):
    rows, width = blocks[0].shape
    length = rows * len(blocks)
    heads = planes[0].shape[0]
    n, n_blocks = len(planes), len(blocks)
    vectors = [] if gain is None else [gain[None], shift[None]]

    def body(z, each_in, whole_in, each_out, whole_out, scratch):
        wide = scratch[0]

        @pl.when(z == 0)
        def _():
            lay(wide, whole_in[:n_blocks])
            if vectors:
                gain_ref, shift_ref = whole_in[n_blocks:]
                normed = wide[...].astype(f32) * gain_ref[...] + shift_ref[...]
                wide[...] = normed.astype(bf16)
                spread(whole_out, wide)

        got = times(wide, each_in[:n], 0, 3 * HD) + each_in[n][...]
        low = got.astype(bf16)
        each_out[0][...] = low[:, :HD] * jnp.asarray(1.0 / math.sqrt(HD), bf16)
        each_out[1][...] = low[:, HD:]

    out = run(
        body,
        heads,
        list(planes) + [bias],
        list(blocks) + vectors,
        [shape((heads, length, HD), bf16), shape((heads, length, 2 * HD), bf16)],
        [shape((rows, width), bf16)] * n_blocks if vectors else [],
        [pltpu.VMEM((length, width), bf16)],
        2 * heads * length * width * 3 * HD,
    )
    return out[0], out[1], out[2:] or blocks


def masked_scores(queries, both, slope, key_pos, query_pos):
    scores = dot(queries, both[:, :HD], 1, 1) + slope * key_pos
    return jnp.where(key_pos <= query_pos, scores, masked_value)


def attend(queries, both, planes, slopes, key_pos, query_pos, n_t, width):
    heads, length, _ = queries.shape
    n = len(planes)
    rows = length // n_t

    def body(z, each_in, whole_in, each_out, whole_out, scratch):
        kv, weights = each_in[1 : 1 + n], each_in[1 + n : 1 + 2 * n]
        slope = each_in[1 + 2 * n][:, :1]
        acc = scratch[0]

        @pl.when(z == 0)
        def _():
            acc[...] = jnp.zeros_like(acc)

        low_queries = each_in[0][...]
        scores = [
            masked_scores(low_queries, kv[s], slope, whole_in[0][s], whole_in[1][...])
            for s in range(n)
        ]
        top = functools.reduce(jnp.maximum, [jnp.max(x, axis=1, keepdims=True) for x in scores])
        shifted = [jnp.exp(x - top) for x in scores]
        total = sum(jnp.sum(x, axis=1, keepdims=True) for x in shifted)
        context = sum(dot(x.astype(bf16), kv[s][:, HD:], 1, 0) for s, x in enumerate(shifted))
        low = (context / total).astype(bf16)
        each_out[0][...] = low
        each_out[1][...] = top + jnp.log(total)
        add_back(acc, low, weights, 3 * HD, 4 * HD)

        @pl.when(z == heads - 1)
        def _():
            spread(whole_out, acc)

    out = run(
        body,
        heads,
        [queries] + list(both) + list(planes) + [slopes],
        [key_pos, query_pos],
        [shape((heads, length, HD), bf16), shape((heads, length, 1), f32)],
        [shape((rows, width), bf16)] * n_t,
        [pltpu.VMEM((length, width), f32)],
        2 * heads * length * (2 * HD * length * n + HD * width),
    )
    return out[0], out[1], out[2:]


def attend_back(blocks, queries, both, planes, context, logs, slopes, key_pos, query_pos):
    heads, length, _ = queries.shape
    n = len(planes)
    width = blocks[0].shape[1]

    def body(z, each_in, whole_in, each_out, whole_out, scratch):
        @pl.when(z == 0)
        def _():
            lay(scratch[0], whole_in[2:])

        kv, weights = each_in[1 : 1 + n], each_in[1 + n : 1 + 2 * n]
        context_ref, logs_ref, slope_ref = each_in[1 + 2 * n :]
        slope = slope_ref[:, :1]
        low_queries = each_in[0][...]
        grads = times(scratch[0], weights, 3 * HD, 4 * HD).astype(bf16)
        inner = jnp.sum(grads.astype(f32) * context_ref[...].astype(f32), axis=1, keepdims=True)
        query_grad = None
        for s in range(n):
            scores = masked_scores(low_queries, kv[s], slope, whole_in[0][s], whole_in[1][...])
            probs = jnp.exp(scores - logs_ref[...])
            prob_grad = dot(grads, kv[s][:, HD:], 1, 1)
            score_grad = (probs * (prob_grad - inner)).astype(bf16)
            term = dot(score_grad, kv[s][:, :HD], 1, 0)
            query_grad = term if query_grad is None else query_grad + term
            each_out[1 + s][:, :HD] = dot(score_grad, low_queries, 0, 0).astype(bf16)
            each_out[1 + s][:, HD:] = dot(probs.astype(bf16), grads, 0, 0).astype(bf16)
        each_out[0][...] = (query_grad * (1.0 / math.sqrt(HD))).astype(bf16)

    out = run(
        body,
        heads,
        [queries] + list(both) + list(planes) + [context, logs, slopes],
        [key_pos, query_pos] + list(blocks),
        [shape((heads, length, HD), bf16)] + [shape((heads, length, 2 * HD), bf16)] * n,
        [],
        [pltpu.VMEM((length, width), bf16)],
        2 * heads * length * (5 * HD * length * n + HD * width),
    )
    return out[0], out[1:]


def project_back(query_grad, both_grads, planes, n_t, width):
    heads, length, _ = query_grad.shape
    n = len(planes)
    rows = length // n_t

    def body(z, each_in, whole_in, each_out, whole_out, scratch):
        acc = scratch[0]

        @pl.when(z == 0)
        def _():
            acc[...] = jnp.zeros_like(acc)

        low = sum(item[...].astype(f32) for item in each_in[1 : 1 + n]).astype(bf16)
        joined, sums = each_out
        joined[:, :HD] = each_in[0][...]
        joined[:, HD:] = low
        sums[:, :HD] = jnp.sum(each_in[0][...].astype(f32), axis=0, keepdims=True)
        sums[:, HD:] = jnp.sum(low.astype(f32), axis=0, keepdims=True)
        add_back(acc, joined[...], each_in[1 + n :], 0, 3 * HD)

        @pl.when(z == heads - 1)
        def _():
            spread(whole_out, acc)

    out = run(
        body,
        heads,
        [query_grad] + list(both_grads) + list(planes),
        [],
        [shape((heads, length, 3 * HD), bf16), shape((heads, 1, 3 * HD), f32)],
        [shape((rows, width), bf16)] * n_t,
        [pltpu.VMEM((length, width), f32)],
        2 * heads * length * width * 3 * HD,
    )
    return out[0], out[1], out[2:]


def feed_forward(blocks, planes, bias):
    rows, width = blocks[0].shape
    length = rows * len(blocks)
    heads, _, units = bias.shape
    n = len(planes)

    def body(z, each_in, whole_in, each_out, whole_out, scratch):
        wide, acc = scratch

        @pl.when(z == 0)
        def _():
            lay(wide, whole_in)
            acc[...] = jnp.zeros_like(acc)

        pre_up = times(wide, each_in[:n], 0, units) + each_in[n][...]
        each_out[0][...] = pre_up
        low = gelu_tanh(pre_up).astype(bf16)
        each_out[1][...] = low
        add_back(acc, low, each_in[:n], units, 2 * units)

        @pl.when(z == heads - 1)
        def _():
            spread(whole_out, acc)

    out = run(
        body,
        heads,
        list(planes) + [bias],
        blocks,
        [shape((heads, length, units), f32), shape((heads, length, units), bf16)],
        [shape((rows, width), bf16)] * len(blocks),
        [pltpu.VMEM((length, width), bf16), pltpu.VMEM((length, width), f32)],
        4 * heads * length * width * units,
    )
    return out[0], out[1], out[2:]


def feed_back(blocks, planes, pre_up):
    rows, width = blocks[0].shape
    length = rows * len(blocks)
    heads, _, units = pre_up.shape
    n = len(planes)

    def body(z, each_in, whole_in, each_out, whole_out, scratch):
        wide, acc = scratch

        @pl.when(z == 0)
        def _():
            lay(wide, whole_in)
            acc[...] = jnp.zeros_like(acc)

        act_grad = times(wide, each_in[:n], units, 2 * units)
        low = (act_grad * gelu_slope(each_in[n][...])).astype(bf16)
        each_out[0][...] = low
        each_out[1][...] = jnp.sum(low.astype(f32), axis=0, keepdims=True)
        add_back(acc, low, each_in[:n], 0, units)

        @pl.when(z == heads - 1)
        def _():
            spread(whole_out, acc)

    out = run(
        body,
        heads,
        list(planes) + [pre_up],
        blocks,
        [shape((heads, length, units), bf16), shape((heads, 1, units), f32)],
        [shape((rows, width), bf16)] * len(blocks),
        [pltpu.VMEM((length, width), bf16), pltpu.VMEM((length, width), f32)],
        4 * heads * length * width * units,
    )
    return out[0], out[1], out[2:]


def weight_back(one_blocks, one, two_blocks, two, n):
    rows, width = one_blocks[0].shape
    length = rows * len(one_blocks)
    heads, _, first = one.shape
    second = two.shape[2]
    part = width // n
    half = len(one_blocks)

    def body(z, each_in, whole_in, each_out, whole_out, scratch):
        @pl.when(z == 0)
        def _():
            lay(scratch[0], whole_in[:half])
            lay(scratch[1], whole_in[half:])

        for s in range(n):
            cols = slice(s * part, (s + 1) * part)
            each_out[s][:, :first] = dot(scratch[0][:, cols], each_in[0][...], 0, 0).astype(bf16)
            each_out[s][:, first:] = dot(scratch[1][:, cols], each_in[1][...], 0, 0).astype(bf16)

    return run(
        body,
        heads,
        [one, two],
        list(one_blocks) + list(two_blocks),
        [shape((heads, part, first + second), bf16)] * n,
        [],
        [pltpu.VMEM((length, width), bf16)] * 2,
        2 * heads * length * width * (first + second),
    )


def norm_forward(values, got, bias, gain, shift):
    def body(z, each_in, whole_in, each_out, whole_out, scratch):
        start, bias_ref, gain_ref, shift_ref = whole_in[:4]
        total = start[...] + bias_ref[...]
        for item in whole_in[4:]:
            total = total + item[...].astype(f32)
        whole_out[0][...] = total
        xhat, _ = norm_parts(total)
        whole_out[1][...] = (xhat * gain_ref[...] + shift_ref[...]).astype(bf16)

    return run(
        body,
        1,
        [],
        [values, bias[None], gain[None], shift[None]] + list(got),
        [],
        [shape(values.shape, f32), shape(values.shape, bf16)],
    )


def norm_back(values, gradient, got, gain):
    width = values.shape[1]

    def body(z, each_in, whole_in, each_out, whole_out, scratch):
        e = sum(item[...].astype(f32) for item in whole_in[3:])
        xhat, scale = norm_parts(whole_in[0][...])
        eg = e * whole_in[2][...]
        back = scale * (
            eg
            - jnp.mean(eg, axis=-1, keepdims=True)
            - xhat * jnp.mean(eg * xhat, axis=-1, keepdims=True)
        )
        fresh = whole_in[1][...] + back
        whole_out[0][...] = fresh
        whole_out[1][...] = fresh.astype(bf16)
        whole_out[2][0:1, :] = jnp.sum(e * xhat, axis=0, keepdims=True)
        whole_out[2][1:2, :] = jnp.sum(e, axis=0, keepdims=True)
        whole_out[2][2:3, :] = jnp.sum(fresh, axis=0, keepdims=True)

    return run(
        body,
        1,
        [],
        [values, gradient, gain[None]] + list(got),
        [],
        [shape(values.shape, f32), shape(values.shape, bf16), shape((3, width), f32)],
    )


def per_device(
    sizes,
    tokens,
    qkv_weight,
    dense_weight,
    up_weight,
    down_weight,
    first_gain,
    first_shift,
    query_bias,
    value_bias,
    dense_bias,
    second_gain,
    second_shift,
    up_bias,
    down_bias,
    cotangent,
):
    n_t, n_s, n_z = sizes
    seq_count, slice_len, width = tokens.shape
    assert seq_count == 1 and n_t == n_z
    d, c, z = (lax.axis_index(name) for name in (DP, SEQ, HEAD))
    rows = slice_len // n_t
    cut = qkv_weight.shape[1]
    part = cut * n_t
    heads = query_bias.shape[1]
    assert heads == n_t
    units = up_bias.shape[2] * n_t * n_s

    def chunks(array):
        return [array[..., j * cut : (j + 1) * cut] for j in range(n_t * n_s)]

    def to_inner(array):
        parts = chunks(array)
        by_seq = flip_list([parts[s::n_s] for s in range(n_s)], c)
        return jnp.concatenate([part for group in by_seq for part in group], axis=-1)

    def to_outer(array):
        parts = chunks(array)
        by_seq = flip_list([parts[k * n_t : (k + 1) * n_t] for k in range(n_s)], c)
        return jnp.concatenate([by_seq[s][t] for t in range(n_t) for s in range(n_s)], axis=-1)

    def own_rows(array):
        cuts = array.reshape(n_t, rows, width)
        blocks = [lax.dynamic_index_in_dim(cuts, d ^ step, 0, False) for step in range(n_t)]
        total = jnp.where(d == z, blocks[0], jnp.zeros_like(blocks[0]))
        for step in range(1, n_t):
            pairs = [(i * n_z + i, (i ^ step) * n_z + i) for i in range(n_t)]
            total = total + lax.ppermute(blocks[step], (DP, HEAD), pairs)
        return total

    def send_rows(array):
        return gather(array, DP, n_t)

    def send_sums(blocks):
        return deal(blocks, DP, n_t)

    def to_planes_of(array):
        return lax.all_gather(array, HEAD, axis=0, tiled=False)

    def send_output(planes):
        return exchange(planes, DP).reshape(1, slice_len, width)

    def packed_mixed(layer):
        qkv = qkv_weight[layer].reshape(cut, n_t, -1).transpose(1, 0, 2)
        dense = dense_weight[layer].reshape(n_t, -1, cut).transpose(0, 2, 1)
        return jnp.concatenate((qkv, dense), axis=2)

    def packed_feed(layer):
        up = up_weight[layer].reshape(cut, n_t, -1).transpose(1, 0, 2)
        down = down_weight[layer].reshape(n_t, -1, cut).transpose(0, 2, 1)
        return jnp.concatenate((up, down), axis=2)

    def to_planes(blocks):
        return exchange(blocks, DP).reshape(part, -1)

    def join(planes):
        return gather(planes, SEQ, n_s)

    wide = jnp.concatenate(
        (first_gain, first_shift, dense_bias, second_gain, second_shift, down_bias), axis=0
    )
    tall = jnp.concatenate((query_bias, value_bias, up_bias), axis=2).transpose(1, 0, 2)
    n_wide, n_tall = 6 * LAYERS * cut, LAYERS * tall.shape[2]
    columns = 4 * HD
    extra = -(-(n_wide + n_tall) // (16 * columns)) * 16
    small = jnp.concatenate(
        (
            jnp.broadcast_to(wide.reshape(1, -1), (n_t, n_wide)),
            tall.reshape(n_t, -1),
            jnp.zeros((n_t, extra * columns - n_wide - n_tall), f32),
        ),
        axis=1,
    )
    small = small.astype(bf16).reshape(n_t, extra, columns)
    first = exchange(jnp.concatenate((packed_mixed(0), small), axis=1), DP)
    first_shard = jnp.concatenate(
        (first[:, :cut].reshape(part, columns), first[:, cut:].reshape(-1, columns)), axis=0
    )
    messages = [to_planes_of(first_shard)]
    hidden = to_inner(own_rows(tokens[0])).astype(f32)
    second_shard = to_planes(after(packed_feed(0), first_shard))
    messages.append(to_planes_of(second_shard))
    mixed = join(messages[0])
    small = jnp.stack([plane[:, part:].reshape(n_z, n_t, -1) for plane in mixed]).astype(f32)
    wide = small[:, 0, :, :n_wide].reshape(n_s, n_t, 6 * LAYERS, cut)
    wide = wide.transpose(2, 0, 1, 3).reshape(6, LAYERS, width)
    each = small[:, :, :, n_wide : n_wide + n_tall].reshape(n_s, n_z, n_t, LAYERS, -1)
    each = jnp.stack(flip_list([each[k] for k in range(n_s)], c)).transpose(3, 1, 2, 0, 4)
    tall = []
    begin = 0
    tall_sizes = (HD, HD, units)
    for size in tall_sizes:
        size = size // (n_t * n_s)
        tall.append(each[..., begin : begin + size].reshape(LAYERS, n_z, -1))
        begin += size
    tall = jnp.concatenate(tall, axis=2)

    qkv_columns = 3 * HD
    head_ids = jnp.arange(n_z, dtype=jnp.int32) * heads + d
    slopes = 2.0 ** (-8.0 * (head_ids + 1).astype(f32) / H)
    slopes = jnp.broadcast_to(slopes[:, None, None], (n_z, 1, 128))
    block_ids = (d ^ jnp.arange(n_t, dtype=jnp.int32)) * rows
    own_pos = (block_ids[:, None] + jnp.arange(rows, dtype=jnp.int32)[None]).reshape(-1)
    query_pos = (c * slice_len + own_pos).astype(f32)[:, None]
    others = (c ^ jnp.arange(n_s, dtype=jnp.int32)) * slice_len
    key_pos = (others[:, None] + own_pos[None]).astype(f32)[:, None, :]
    cot = cotangent[0]
    records = []
    low = norm_parts(hidden)[0].astype(bf16)
    for layer in range(LAYERS):
        gain_one, shift_one, bias_dense, gain_two, shift_two, bias_down = (wide[i, layer] for i in range(6))
        zeros = jnp.zeros((n_z, HD), f32)
        bias_qkv = jnp.concatenate((tall[layer, :, :HD], zeros, tall[layer, :, HD : 2 * HD]), 1)
        bias_up = tall[layer, :, 2 * HD :][:, None]
        normed_one = send_rows(low)
        if layer > 0:
            mixed = join(after(messages[2 * layer], out[0]))
        affine = (gain_one, shift_one) if layer == 0 else ()
        queries, both, normed_one = project(normed_one, mixed, bias_qkv[:, None], *affine)
        both = gather(both, SEQ, n_s)
        if layer == 0:
            later = [to_planes(after(packed_mixed(1), both[0]))]
            later.append(to_planes(after(packed_feed(1), later[0])))
            cot_rows = own_rows(after(cot, both[0]))
        else:
            cot_rows = send_rows(after(cot_rows, both[0]))
        context, logs, out = attend(queries, both, mixed, slopes, key_pos, query_pos, n_t, width)
        got = send_sums(out)
        feed = join(after(messages[2 * layer + 1], out[0]))
        if layer == 0:
            got, later, cot_rows = meet(got, later, cot_rows)
            messages.extend(to_planes_of(shard) for shard in later)
            cot_rows = to_inner(cot_rows)
        else:
            got, cot_rows = meet(got, cot_rows)
        hidden_mid, low = norm_forward(hidden, got, bias_dense, gain_two, shift_two)
        normed_two = send_rows(low)
        pre_up, activation, out = feed_forward(normed_two, feed, bias_up)
        got = send_sums(out)
        records.append(
            (
                (mixed, feed, gain_one, gain_two),
                (hidden, hidden_mid, normed_one, normed_two),
                (queries, both, logs, context, pre_up, activation),
            )
        )
        if layer + 1 < LAYERS:
            hidden, low = norm_forward(
                hidden_mid, got, bias_down, wide[0, layer + 1], wide[1, layer + 1]
            )
        else:
            hidden = hidden_mid + add_all(got) + bias_down

    output_low = to_outer(hidden.astype(bf16))

    gradient = cot_rows[0].astype(f32)
    grad_low = cot_rows
    down_bias_grad = jnp.sum(gradient, axis=0, keepdims=True)
    wide_grads = [None] * LAYERS
    tall_grads = [None] * LAYERS

    def core_sum(blocks):
        return sum_blocks(blocks, SEQ, n_s).astype(bf16)

    def head_sum(mine):
        return lax.psum_scatter(mine, HEAD, scatter_dimension=0, tiled=False)

    def send_shares(mine):
        return exchange(mine.reshape(n_t, cut, -1), DP)

    feed_shares = [None] * LAYERS
    mixed_shares = [None] * LAYERS
    feed_sums = [None] * LAYERS
    mixed_sums = [None] * LAYERS
    for layer in reversed(range(LAYERS)):
        (
            (mixed, feed, gain_one, gain_two),
            (hidden, hidden_mid, normed_one, normed_two),
            (queries, both, logs, context, pre_up, activation),
        ) = records[layer]
        last = layer == LAYERS - 1
        pre_grad, up_bias_grad, out = feed_back(grad_low, feed, pre_up)
        got = send_sums(out)
        feed_grad = weight_back(normed_two, pre_grad, grad_low, activation, n_s)
        if last:
            got, feed_grad, output_low = meet(got, feed_grad, output_low)
            output_planes = to_planes_of(output_low)
        else:
            got, feed_grad = meet(got, feed_grad)
        mid_grad, low, sums_two = norm_back(hidden_mid, gradient, got, gain_two)
        mid_low = send_rows(low)
        mine = core_sum(feed_grad)
        if last:
            mid_low, mine = meet(mid_low, mine)
        else:
            feed_share = send_shares(after(feed_sums[layer + 1], low))
            mid_low, mine, feed_shares[layer + 1] = meet(mid_low, mine, feed_share)
        feed_sums[layer] = head_sum(mine)
        query_grad, both_grads = attend_back(
            mid_low, queries, both, mixed, context, logs, slopes, key_pos, query_pos
        )
        got = deal(both_grads, SEQ, n_s)
        joined, qkv_sums, out = project_back(query_grad, got, mixed, n_t, width)
        got = send_sums(out)
        mixed_grad = weight_back(normed_one, joined, mid_low, context, n_s)
        if last:
            planes = after(output_planes, joined)
            got, mixed_grad, output = meet(got, mixed_grad, send_output(planes))
        else:
            mixed_sums[layer] = head_sum(after(core_sum(mixed_grad), feed_sums[layer]))
        gradient, low, sums_one = norm_back(hidden, mid_grad, got, gain_one)
        if layer > 0:
            grad_low, mine = meet(send_rows(low), core_sum(mixed_grad))
            mixed_sums[layer] = head_sum(mine)
        wide_grads[layer] = jnp.stack(
            (
                sums_one[0],
                sums_one[1],
                sums_two[2],
                sums_two[0],
                sums_two[1],
                down_bias_grad[0],
            )
        )
        down_bias_grad = sums_one[2:3]
        tall_grads[layer] = jnp.concatenate(
            (qkv_sums[:, 0, :HD], qkv_sums[:, 0, 2 * HD :], up_bias_grad[:, 0]), axis=1
        )

    tokens_planes = to_planes_of(to_outer(low))
    mixed_shares[1] = send_shares(after(mixed_sums[1], low))
    feed_shares[0] = send_shares(after(feed_sums[0], low))
    mixed_shares[0] = send_shares(mixed_sums[0])
    tokens_grad = send_output(tokens_planes).astype(f32)
    feed_shares = [after(share, low) for share in feed_shares]

    def fold(arrays, name, size):
        total = arrays[0]
        for step in range(1, size):
            total = total + swap(arrays[step], name, size, step)
        return total

    wide = jnp.stack(wide_grads).reshape(LAYERS * 6, n_s, n_t, cut)
    pieces, begin = [], 0
    tall = jnp.stack(tall_grads)
    for size in tall_sizes:
        piece = tall[:, :, begin : begin + size]
        begin += size
        piece = piece.reshape(LAYERS, n_z, n_t, n_s, size // (n_t * n_s))
        pieces.append(flip(flip(piece, c, 3), z, 1))
    tall = jnp.concatenate(
        [piece.transpose(3, 1, 2, 0, 4).reshape(n_s, n_z, n_t, -1) for piece in pieces], axis=3
    )
    wide = wide.transpose(1, 2, 0, 3).reshape(n_s, n_t, -1)
    n_wide = wide.shape[2]
    wide = jnp.broadcast_to(wide[:, None], (n_s, n_z) + wide.shape[1:])
    joint = jnp.concatenate((wide, tall), axis=3)
    joint = fold([joint[step] for step in range(n_s)], SEQ, n_s)
    joint = fold([joint[step] for step in range(n_z)], HEAD, n_z)
    joint = flip(joint, d)
    got = deal([joint[step] for step in range(n_t)], DP, n_t)
    wide = functools.reduce(jnp.add, [item[:n_wide] for item in got])
    wide = wide.reshape(LAYERS, 6, cut)
    tall = flip(jnp.stack([item[n_wide:] for item in got]), d)
    outs, begin = [], 0
    for size in tall_sizes:
        size = size // (n_t * n_s)
        piece = tall[:, begin : begin + LAYERS * size].reshape(n_t, LAYERS, size)
        begin += LAYERS * size
        outs.append(piece.transpose(1, 0, 2))
    query_bias_grad, value_bias_grad, up_bias_grad = outs
    def rows_first(shares, begin, end):
        parts = [share[:, :, begin:end].transpose(1, 0, 2).reshape(cut, -1) for share in shares]
        return jnp.stack(parts).astype(f32)

    def columns_first(shares, begin, end):
        parts = [share[:, :, begin:end].transpose(0, 2, 1).reshape(-1, cut) for share in shares]
        return jnp.stack(parts).astype(f32)

    qkv_grad = rows_first(mixed_shares, 0, qkv_columns)
    dense_grad = columns_first(mixed_shares, qkv_columns, columns)
    up_grad = rows_first(feed_shares, 0, units)
    down_grad = columns_first(feed_shares, units, 2 * units)
    return (
        output,
        tokens_grad,
        qkv_grad,
        dense_grad,
        up_grad,
        down_grad,
        wide[:, 0],
        wide[:, 1],
        query_bias_grad,
        value_bias_grad,
        wide[:, 2],
        wide[:, 3],
        wide[:, 4],
        up_bias_grad,
        wide[:, 5],
    )


def solution(mesh):
    sizes = tuple(mesh.shape[name] for name in (DP, SEQ, HEAD))
    rows = P(DP, SEQ, None)
    tall = P(None, (DP, SEQ), HEAD)
    flat = P(None, HEAD, (DP, SEQ))
    vector = P(None, (DP, SEQ))
    params = (
        tall,
        flat,
        tall,
        flat,
        vector,
        vector,
        flat,
        flat,
        vector,
        vector,
        vector,
        flat,
        vector,
    )
    return jax.shard_map(
        functools.partial(per_device, sizes),
        mesh=mesh,
        in_specs=(rows,) + params + (rows,),
        out_specs=(rows, rows) + params,
        check_vma=False,
    )
```

```python
import functools
import math

import jax
import jax.numpy as jnp
from jax import lax
from jax.experimental import pallas as pl
from jax.experimental.pallas import tpu as pltpu
from jax.sharding import PartitionSpec as P

H = 16
HD = 64
LAYERS = 2
DP, SEQ, HEAD = "dp", "seq", "head"

epsilon = 1e-05
masked_value = -1000000000.0
VMEM_LIMIT = 60 * 1024 * 1024
bf16 = jnp.bfloat16
f32 = jnp.float32


def flip_list(blocks, index):
    bit = 1
    while bit < len(blocks):
        turn = (index & bit) != 0
        blocks = [
            jax.tree.map(lambda x, y: jnp.where(turn, x, y), blocks[j ^ bit], blocks[j])
            for j in range(len(blocks))
        ]
        bit *= 2
    return blocks


def flip(array, index, axis=0):
    blocks = [lax.index_in_dim(array, j, axis, keepdims=True) for j in range(array.shape[axis])]
    return jnp.concatenate(flip_list(blocks, index), axis=axis)


def swap(array, name, size, step):
    return lax.ppermute(array, name, [(i, i ^ step) for i in range(size)])


def gather(array, name, size):
    return [array] + [swap(array, name, size, step) for step in range(1, size)]


def deal(blocks, name, size):
    return [blocks[0]] + [swap(blocks[step], name, size, step) for step in range(1, size)]


def exchange(array, name):
    return lax.all_to_all(array, name, 0, 0, tiled=True)


def meet(*groups):
    return lax.optimization_barrier(groups)


def add_all(blocks):
    return functools.reduce(jnp.add, [block.astype(f32) for block in blocks])


def sum_blocks(blocks, name, size):
    total = blocks[0].astype(f32)
    for step in range(1, size):
        total = total + swap(blocks[step].astype(bf16), name, size, step).astype(f32)
    return total


def after(array, *others):
    return lax.optimization_barrier((array,) + others)[0]


def dot(left, right, left_dim, right_dim):
    dims = (((left_dim,), (right_dim,)), ((), ()))
    return lax.dot_general(left, right, dims, preferred_element_type=f32)


def gelu_tanh(values):
    argument = 0.7978845608028654 * (values + 0.044715 * values * values * values)
    return 0.5 * values * (1.0 + jnp.tanh(argument))


def gelu_slope(values):
    square = values * values
    bent = jnp.tanh(0.7978845608028654 * (values + 0.044715 * values * square))
    inner = 0.7978845608028654 * (1.0 + 3.0 * 0.044715 * square)
    return 0.5 * (1.0 + bent) + 0.5 * values * (1.0 - bent * bent) * inner


def norm_parts(values):
    row_mean = jnp.mean(values, axis=-1, keepdims=True)
    centred = values - row_mean
    scale = lax.rsqrt(jnp.mean(centred * centred, axis=-1, keepdims=True) + epsilon)
    return centred * scale, scale


def run(body, steps, each_in, whole_in, each_out, whole_out, scratch=(), flops=0):
    def each(array):
        zeros = (0,) * (len(array.shape) - 1)
        return pl.BlockSpec((None,) + tuple(array.shape[1:]), lambda z: (z,) + zeros)

    def whole(array):
        zeros = (0,) * len(array.shape)
        return pl.BlockSpec(tuple(array.shape), lambda z: zeros)

    counts = [len(part) for part in (each_in, whole_in, each_out, whole_out)]

    def kernel(*refs):
        parts, begin = [], 0
        for count in counts:
            parts.append(refs[begin : begin + count])
            begin += count
        body(pl.program_id(0), *parts, refs[begin:])

    arrays = list(each_in) + list(whole_in)
    shapes = list(each_out) + list(whole_out)
    moved = sum(math.prod(item.shape) * item.dtype.itemsize for item in arrays + shapes)
    return pl.pallas_call(
        kernel,
        grid=(steps,),
        in_specs=[each(item) for item in each_in] + [whole(item) for item in whole_in],
        out_specs=[each(item) for item in each_out] + [whole(item) for item in whole_out],
        out_shape=shapes,
        scratch_shapes=list(scratch),
        compiler_params=pltpu.CompilerParams(vmem_limit_bytes=VMEM_LIMIT),
        cost_estimate=pl.CostEstimate(flops=flops, bytes_accessed=moved, transcendentals=0),
    )(*arrays)


def shape(dims, kind):
    return jax.ShapeDtypeStruct(tuple(dims), kind)


def lay(target, blocks):
    rows = blocks[0].shape[0]
    for index, block in enumerate(blocks):
        target[index * rows : (index + 1) * rows, :] = block[...]


def spread(blocks, source):
    rows = blocks[0].shape[0]
    for index, block in enumerate(blocks):
        block[...] = source[index * rows : (index + 1) * rows, :].astype(block.dtype)


def times(array, planes, begin, end):
    part = array.shape[1] // len(planes)
    total = None
    for s, plane in enumerate(planes):
        term = dot(array[:, s * part : (s + 1) * part], plane[:part, begin:end], 1, 0)
        total = term if total is None else total + term
    return total


def add_back(acc, array, planes, begin, end):
    part = acc.shape[1] // len(planes)
    for s, plane in enumerate(planes):
        acc[:, s * part : (s + 1) * part] += dot(array, plane[:part, begin:end], 1, 1)


def project(blocks, planes, bias, vectors=None, gain=None, shift=None):
    rows, width = blocks[0].shape
    length = rows * len(blocks)
    heads = planes[0].shape[0]
    n, n_blocks = len(planes), len(blocks)
    vectors = [] if gain is None else [vectors]

    def body(z, each_in, whole_in, each_out, whole_out, scratch):
        wide = scratch[0]

        @pl.when(z == 0)
        def _():
            lay(wide, whole_in[:n_blocks])
            if vectors:
                lines = whole_in[n_blocks]
                normed = wide[...].astype(f32) * lines[gain : gain + 1, :]
                normed = normed + lines[shift : shift + 1, :]
                wide[...] = normed.astype(bf16)
                spread(whole_out, wide)

        got = times(wide, each_in[:n], 0, 3 * HD) + each_in[n][...]
        low = got.astype(bf16)
        each_out[0][...] = low[:, :HD] * jnp.asarray(1.0 / math.sqrt(HD), bf16)
        each_out[1][...] = low[:, HD:]

    out = run(
        body,
        heads,
        list(planes) + [bias],
        list(blocks) + vectors,
        [shape((heads, length, HD), bf16), shape((heads, length, 2 * HD), bf16)],
        [shape((rows, width), bf16)] * n_blocks if vectors else [],
        [pltpu.VMEM((length, width), bf16)],
        2 * heads * length * width * 3 * HD,
    )
    return out[0], out[1], out[2:] or blocks


def masked_scores(queries, both, slope, key_pos, query_pos):
    scores = dot(queries, both[:, :HD], 1, 1) + slope * key_pos
    return jnp.where(key_pos <= query_pos, scores, masked_value)


def attend(queries, both, planes, slopes, key_pos, query_pos, n_t, width):
    heads, length, _ = queries.shape
    n = len(planes)
    rows = length // n_t

    def body(z, each_in, whole_in, each_out, whole_out, scratch):
        kv, weights = each_in[1 : 1 + n], each_in[1 + n : 1 + 2 * n]
        slope = each_in[1 + 2 * n][:, :1]
        acc = scratch[0]

        @pl.when(z == 0)
        def _():
            acc[...] = jnp.zeros_like(acc)

        low_queries = each_in[0][...]
        scores = [
            masked_scores(low_queries, kv[s], slope, whole_in[0][s], whole_in[1][...])
            for s in range(n)
        ]
        top = functools.reduce(jnp.maximum, [jnp.max(x, axis=1, keepdims=True) for x in scores])
        shifted = [jnp.exp(x - top) for x in scores]
        total = sum(jnp.sum(x, axis=1, keepdims=True) for x in shifted)
        context = sum(dot(x.astype(bf16), kv[s][:, HD:], 1, 0) for s, x in enumerate(shifted))
        low = (context / total).astype(bf16)
        each_out[0][...] = low
        each_out[1][...] = top + jnp.log(total)
        add_back(acc, low, weights, 3 * HD, 4 * HD)

        @pl.when(z == heads - 1)
        def _():
            spread(whole_out, acc)

    out = run(
        body,
        heads,
        [queries] + list(both) + list(planes) + [slopes],
        [key_pos, query_pos],
        [shape((heads, length, HD), bf16), shape((heads, length, 1), f32)],
        [shape((rows, width), bf16)] * n_t,
        [pltpu.VMEM((length, width), f32)],
        2 * heads * length * (2 * HD * length * n + HD * width),
    )
    return out[0], out[1], out[2:]


def attend_back(blocks, queries, both, planes, context, logs, slopes, key_pos, query_pos):
    heads, length, _ = queries.shape
    n = len(planes)
    width = blocks[0].shape[1]

    def body(z, each_in, whole_in, each_out, whole_out, scratch):
        @pl.when(z == 0)
        def _():
            lay(scratch[0], whole_in[2:])

        kv, weights = each_in[1 : 1 + n], each_in[1 + n : 1 + 2 * n]
        context_ref, logs_ref, slope_ref = each_in[1 + 2 * n :]
        slope = slope_ref[:, :1]
        low_queries = each_in[0][...]
        grads = times(scratch[0], weights, 3 * HD, 4 * HD).astype(bf16)
        inner = jnp.sum(grads.astype(f32) * context_ref[...].astype(f32), axis=1, keepdims=True)
        query_grad = None
        for s in range(n):
            scores = masked_scores(low_queries, kv[s], slope, whole_in[0][s], whole_in[1][...])
            probs = jnp.exp(scores - logs_ref[...])
            prob_grad = dot(grads, kv[s][:, HD:], 1, 1)
            score_grad = (probs * (prob_grad - inner)).astype(bf16)
            term = dot(score_grad, kv[s][:, :HD], 1, 0)
            query_grad = term if query_grad is None else query_grad + term
            each_out[1 + s][:, :HD] = dot(score_grad, low_queries, 0, 0).astype(bf16)
            each_out[1 + s][:, HD:] = dot(probs.astype(bf16), grads, 0, 0).astype(bf16)
        each_out[0][...] = (query_grad * (1.0 / math.sqrt(HD))).astype(bf16)

    out = run(
        body,
        heads,
        [queries] + list(both) + list(planes) + [context, logs, slopes],
        [key_pos, query_pos] + list(blocks),
        [shape((heads, length, HD), bf16)] + [shape((heads, length, 2 * HD), bf16)] * n,
        [],
        [pltpu.VMEM((length, width), bf16)],
        2 * heads * length * (5 * HD * length * n + HD * width),
    )
    return out[0], out[1:]


def project_back(query_grad, both_grads, planes, n_t, width):
    heads, length, _ = query_grad.shape
    n = len(planes)
    rows = length // n_t

    def body(z, each_in, whole_in, each_out, whole_out, scratch):
        acc = scratch[0]

        @pl.when(z == 0)
        def _():
            acc[...] = jnp.zeros_like(acc)

        low = sum(item[...].astype(f32) for item in each_in[1 : 1 + n]).astype(bf16)
        joined, sums = each_out
        joined[:, :HD] = each_in[0][...]
        joined[:, HD:] = low
        sums[:, :HD] = jnp.sum(each_in[0][...].astype(f32), axis=0, keepdims=True)
        sums[:, HD:] = jnp.sum(low.astype(f32), axis=0, keepdims=True)
        add_back(acc, joined[...], each_in[1 + n :], 0, 3 * HD)

        @pl.when(z == heads - 1)
        def _():
            spread(whole_out, acc)

    out = run(
        body,
        heads,
        [query_grad] + list(both_grads) + list(planes),
        [],
        [shape((heads, length, 3 * HD), bf16), shape((heads, 1, 3 * HD), f32)],
        [shape((rows, width), bf16)] * n_t,
        [pltpu.VMEM((length, width), f32)],
        2 * heads * length * width * 3 * HD,
    )
    return out[0], out[1], out[2:]


def feed_forward(blocks, planes, bias):
    rows, width = blocks[0].shape
    length = rows * len(blocks)
    heads, _, units = bias.shape
    n = len(planes)

    def body(z, each_in, whole_in, each_out, whole_out, scratch):
        wide, acc = scratch

        @pl.when(z == 0)
        def _():
            lay(wide, whole_in)
            acc[...] = jnp.zeros_like(acc)

        pre_up = times(wide, each_in[:n], 0, units) + each_in[n][...]
        each_out[0][...] = pre_up
        low = gelu_tanh(pre_up).astype(bf16)
        each_out[1][...] = low
        add_back(acc, low, each_in[:n], units, 2 * units)

        @pl.when(z == heads - 1)
        def _():
            spread(whole_out, acc)

    out = run(
        body,
        heads,
        list(planes) + [bias],
        blocks,
        [shape((heads, length, units), f32), shape((heads, length, units), bf16)],
        [shape((rows, width), bf16)] * len(blocks),
        [pltpu.VMEM((length, width), bf16), pltpu.VMEM((length, width), f32)],
        4 * heads * length * width * units,
    )
    return out[0], out[1], out[2:]


def feed_back(blocks, planes, pre_up):
    rows, width = blocks[0].shape
    length = rows * len(blocks)
    heads, _, units = pre_up.shape
    n = len(planes)

    def body(z, each_in, whole_in, each_out, whole_out, scratch):
        wide, acc = scratch

        @pl.when(z == 0)
        def _():
            lay(wide, whole_in)
            acc[...] = jnp.zeros_like(acc)

        act_grad = times(wide, each_in[:n], units, 2 * units)
        low = (act_grad * gelu_slope(each_in[n][...])).astype(bf16)
        each_out[0][...] = low
        each_out[1][...] = jnp.sum(low.astype(f32), axis=0, keepdims=True)
        add_back(acc, low, each_in[:n], 0, units)

        @pl.when(z == heads - 1)
        def _():
            spread(whole_out, acc)

    out = run(
        body,
        heads,
        list(planes) + [pre_up],
        blocks,
        [shape((heads, length, units), bf16), shape((heads, 1, units), f32)],
        [shape((rows, width), bf16)] * len(blocks),
        [pltpu.VMEM((length, width), bf16), pltpu.VMEM((length, width), f32)],
        4 * heads * length * width * units,
    )
    return out[0], out[1], out[2:]


def weight_back(one_blocks, one, two_blocks, two, n):
    rows, width = one_blocks[0].shape
    length = rows * len(one_blocks)
    heads, _, first = one.shape
    second = two.shape[2]
    part = width // n
    half = len(one_blocks)

    def body(z, each_in, whole_in, each_out, whole_out, scratch):
        @pl.when(z == 0)
        def _():
            lay(scratch[0], whole_in[:half])
            lay(scratch[1], whole_in[half:])

        for s in range(n):
            cols = slice(s * part, (s + 1) * part)
            each_out[s][:, :first] = dot(scratch[0][:, cols], each_in[0][...], 0, 0).astype(bf16)
            each_out[s][:, first:] = dot(scratch[1][:, cols], each_in[1][...], 0, 0).astype(bf16)

    return run(
        body,
        heads,
        [one, two],
        list(one_blocks) + list(two_blocks),
        [shape((heads, part, first + second), bf16)] * n,
        [],
        [pltpu.VMEM((length, width), bf16)] * 2,
        2 * heads * length * width * (first + second),
    )


def norm_forward(values, got, vectors, bias, gain, shift):
    def body(z, each_in, whole_in, each_out, whole_out, scratch):
        start, rows = whole_in[:2]
        total = start[...] + rows[bias : bias + 1, :]
        for item in whole_in[2:]:
            total = total + item[...].astype(f32)
        whole_out[0][...] = total
        xhat, _ = norm_parts(total)
        normed = xhat * rows[gain : gain + 1, :] + rows[shift : shift + 1, :]
        whole_out[1][...] = normed.astype(bf16)

    shapes = [shape(values.shape, f32), shape(values.shape, bf16)]
    return run(body, 1, [], [values, vectors] + list(got), [], shapes)


def norm_back(values, gradient, got, vectors, gain):
    width = values.shape[1]

    def body(z, each_in, whole_in, each_out, whole_out, scratch):
        e = sum(item[...].astype(f32) for item in whole_in[3:])
        xhat, scale = norm_parts(whole_in[0][...])
        eg = e * whole_in[2][gain : gain + 1, :]
        back = scale * (
            eg
            - jnp.mean(eg, axis=-1, keepdims=True)
            - xhat * jnp.mean(eg * xhat, axis=-1, keepdims=True)
        )
        fresh = whole_in[1][...].astype(f32) + back
        whole_out[0][...] = fresh
        whole_out[1][...] = fresh.astype(bf16)
        whole_out[2][0:1, :] = jnp.sum(e * xhat, axis=0, keepdims=True)
        whole_out[2][1:2, :] = jnp.sum(e, axis=0, keepdims=True)
        whole_out[2][2:3, :] = jnp.sum(fresh, axis=0, keepdims=True)

    shapes = [shape(values.shape, f32), shape(values.shape, bf16), shape((3, width), f32)]
    return run(body, 1, [], [values, gradient, vectors] + list(got), [], shapes)


def turn_columns(array, turn, counts, inward):
    n_t, n_s = counts
    cut = array.shape[1] // (n_t * n_s)
    parts = [array[:, j * cut : (j + 1) * cut] for j in range(n_t * n_s)]
    index = turn[:, :cut]
    if inward:
        groups = flip_list([parts[s::n_s] for s in range(n_s)], index)
        return [part for group in groups for part in group]
    groups = flip_list([parts[k * n_t : (k + 1) * n_t] for k in range(n_s)], index)
    return [groups[s][t] for t in range(n_t) for s in range(n_s)]


def store_columns(target, parts):
    cut = parts[0].shape[1]
    for j, part in enumerate(parts):
        target[:, j * cut : (j + 1) * cut] = part.astype(target.dtype)


def first_norm(items, turn, counts):
    dims = items[0].shape

    def body(z, each_in, whole_in, each_out, whole_out, scratch):
        total = sum(item[...].astype(f32) for item in whole_in[1:])
        store_columns(whole_out[0], turn_columns(total, whole_in[0][...], counts, True))
        whole_out[1][...] = norm_parts(whole_out[0][...])[0].astype(bf16)

    return run(body, 1, [], [turn] + list(items), [], [shape(dims, f32), shape(dims, bf16)])


def turned_sum(items, turn, counts, inward, bias=None):
    dims = items[0].shape

    def body(z, each_in, whole_in, each_out, whole_out, scratch):
        count = len(whole_in) - (0 if bias is None else 1)
        total = sum(item[...].astype(f32) for item in whole_in[1:count])
        if bias is not None:
            total = total + whole_in[count][bias : bias + 1, :]
        store_columns(whole_out[0], turn_columns(total, whole_in[0][...], counts, inward))

    return run(body, 1, [], [turn] + list(items), [], [shape(dims, bf16)])[0]


def unpack(planes, turn, counts, width, layers, spare):
    n_t, n_s = counts
    heads, _, columns = planes[0].shape
    part, cut = width // n_s, width // (n_s * n_t)
    small = HD // (n_t * n_s)
    units = columns
    unit = units // (n_t * n_s)
    half = columns // 2

    def kernel(*refs):
        ex, index, outs = refs[:n_s], refs[n_s], refs[n_s + 1 :]
        vectors, qkv, up = outs[0], outs[1 : 1 + layers], outs[1 + layers :]
        for layer in range(layers):
            qkv[layer][...] = jnp.zeros_like(qkv[layer])
        for t in range(n_t):
            rows = slice(t * spare, (t + 1) * spare)
            for k in range(n_s):
                place = (k * n_t + t) * cut
                vectors[:, place : place + cut] = ex[k][0, rows, :cut].astype(f32)
            for head in range(heads):
                blocks = [ex[k][head, rows, half:].astype(f32) for k in range(n_s)]
                blocks = flip_list(blocks, index[:, :half])
                for s in range(n_s):
                    place = t * n_s + s
                    for layer in range(layers):
                        row = blocks[s][layer : layer + 1, :]
                        at = place * small
                        qkv[layer][head, :, at : at + small] = row[:, :small]
                        at += 2 * HD
                        qkv[layer][head, :, at : at + small] = row[:, small : 2 * small]
                        at = place * unit
                        up[layer][head, :, at : at + unit] = row[:, 2 * small : 2 * small + unit]

    block = pl.BlockSpec((heads, n_t * spare, columns), lambda i: (0, part // (n_t * spare), 0))
    shapes = [shape((spare, width), f32)]
    shapes += [shape((heads, 1, 3 * HD), f32)] * layers
    shapes += [shape((heads, 1, units), f32)] * layers

    def whole(dims):
        return pl.BlockSpec(dims, lambda i: (0,) * len(dims))

    out = pl.pallas_call(
        kernel,
        grid=(1,),
        in_specs=[block] * n_s + [whole(turn.shape)],
        out_specs=[whole(item.shape) for item in shapes],
        out_shape=shapes,
        compiler_params=pltpu.CompilerParams(vmem_limit_bytes=VMEM_LIMIT),
    )(*planes, turn)
    return out[0], out[1 : 1 + layers], out[1 + layers :]


def per_device(
    sizes,
    tokens,
    qkv_weight,
    dense_weight,
    up_weight,
    down_weight,
    first_gain,
    first_shift,
    query_bias,
    value_bias,
    dense_bias,
    second_gain,
    second_shift,
    up_bias,
    down_bias,
    cotangent,
):
    n_t, n_s, n_z = sizes
    seq_count, slice_len, width = tokens.shape
    assert seq_count == 1 and n_t == n_z
    d, c, z = (lax.axis_index(name) for name in (DP, SEQ, HEAD))
    rows = slice_len // n_t
    cut = qkv_weight.shape[1]
    part = cut * n_t
    heads = query_bias.shape[1]
    assert heads == n_t
    units = up_bias.shape[2] * n_t * n_s

    def spread_rows(array):
        return exchange(array.reshape(n_t, rows, width), DP)

    def own_rows(blocks):
        return lax.dynamic_index_in_dim(blocks, z, 0, False)

    def send_rows(array):
        return gather(array, DP, n_t)

    def send_sums(blocks):
        return deal(blocks, DP, n_t)

    def to_planes_of(array):
        return lax.all_gather(array, HEAD, axis=0, tiled=False)

    def send_output(planes):
        return exchange(planes, DP).reshape(1, slice_len, width)

    def packed_mixed(layer):
        qkv = qkv_weight[layer].reshape(cut, n_t, -1).transpose(1, 0, 2)
        dense = dense_weight[layer].reshape(n_t, -1, cut).transpose(0, 2, 1)
        return jnp.concatenate((qkv, dense), axis=2)

    def packed_feed(layer):
        up = up_weight[layer].reshape(cut, n_t, -1).transpose(1, 0, 2)
        down = down_weight[layer].reshape(n_t, -1, cut).transpose(0, 2, 1)
        return jnp.concatenate((up, down), axis=2)

    def to_planes(blocks):
        return exchange(blocks, DP).reshape(part, -1)

    def join(planes):
        return gather(planes, SEQ, n_s)

    counts = (n_t, n_s)
    turn = jnp.full((1, 128), c, jnp.int32)
    wide = jnp.concatenate(
        (first_gain, first_shift, dense_bias, second_gain, second_shift, down_bias), axis=0
    )
    tall = jnp.concatenate((query_bias, value_bias, up_bias), axis=2).transpose(1, 0, 2)
    columns, spare = 4 * HD, 16
    half = columns // 2
    wide = jnp.pad(wide, ((0, spare - 6 * LAYERS), (0, half - cut)))
    tall = jnp.pad(tall, ((0, 0), (0, spare - LAYERS), (0, half - tall.shape[2])))
    small = jnp.concatenate((jnp.broadcast_to(wide[None], (n_t, spare, half)), tall), axis=2)
    first = jnp.concatenate((packed_mixed(0), small.astype(bf16)), axis=1)
    first = exchange(first, DP)
    first_shard = jnp.concatenate(
        (first[:, :cut].reshape(part, columns), first[:, cut:].reshape(-1, columns)), axis=0
    )
    messages = [to_planes_of(first_shard)]
    hidden, low = first_norm([own_rows(spread_rows(tokens[0]))], turn, counts)
    normed_one = send_rows(low)
    rest = jnp.concatenate((packed_feed(0), packed_mixed(1), packed_feed(1)), axis=2)
    rest = to_planes(after(rest, low))
    messages.append(to_planes_of(rest[:, : 2 * units]))
    later = [rest[:, 2 * units : 2 * units + columns], rest[:, 2 * units + columns :]]
    mixed = join(after(messages[0], normed_one[-1]))
    vectors, biases_qkv, biases_up = unpack(mixed, turn, counts, width, LAYERS, spare)
    tall_sizes = (HD, HD, units)

    def vector(kind, layer):
        return kind * LAYERS + layer

    qkv_columns = 3 * HD
    head_ids = jnp.arange(n_z, dtype=jnp.int32) * heads + d
    slopes = 2.0 ** (-8.0 * (head_ids + 1).astype(f32) / H)
    slopes = jnp.broadcast_to(slopes[:, None, None], (n_z, 1, 128))
    block_ids = (d ^ jnp.arange(n_t, dtype=jnp.int32)) * rows
    own_pos = (block_ids[:, None] + jnp.arange(rows, dtype=jnp.int32)[None]).reshape(-1)
    query_pos = (c * slice_len + own_pos).astype(f32)[:, None]
    others = (c ^ jnp.arange(n_s, dtype=jnp.int32)) * slice_len
    key_pos = (others[:, None] + own_pos[None]).astype(f32)[:, None, :]
    cot = cotangent[0]
    records = []
    for layer in range(LAYERS):
        if layer > 0:
            normed_one = send_rows(low)
            mixed = join(after(messages[2 * layer], out[0]))
        affine = (vectors, vector(0, 0), vector(1, 0)) if layer == 0 else ()
        queries, both, normed_one = project(normed_one, mixed, biases_qkv[layer], *affine)
        both = gather(both, SEQ, n_s)
        if layer == 0:
            cot_rows = spread_rows(after(cot, both[0]))
        else:
            cot_rows = send_rows(after(cot_rows, both[0]))
        context, logs, out = attend(queries, both, mixed, slopes, key_pos, query_pos, n_t, width)
        if layer == 0:
            out, cot_rows = meet(out, cot_rows)
        got = send_sums(out)
        feed = join(after(messages[2 * layer + 1], out[0]))
        if layer == 0:
            got, later = meet(got, later)
            messages.extend(to_planes_of(shard) for shard in later)
            cot_rows = turned_sum([own_rows(cot_rows)], turn, counts, True)
        else:
            got, cot_rows = meet(got, cot_rows)
        hidden_mid, low = norm_forward(
            hidden, got, vectors, vector(2, layer), vector(3, layer), vector(4, layer)
        )
        normed_two = send_rows(low)
        pre_up, activation, out = feed_forward(normed_two, feed, biases_up[layer])
        got = send_sums(out)
        records.append(
            (
                (mixed, feed),
                (hidden, hidden_mid, normed_one, normed_two),
                (queries, both, logs, context, pre_up, activation),
            )
        )
        if layer + 1 < LAYERS:
            hidden, low = norm_forward(
                hidden_mid,
                got,
                vectors,
                vector(5, layer),
                vector(0, layer + 1),
                vector(1, layer + 1),
            )

    last_bias = vector(5, LAYERS - 1)
    output_low = turned_sum([hidden_mid] + list(got) + [vectors], turn, counts, False, last_bias)

    gradient = cot_rows[0]
    grad_low = cot_rows
    down_bias_grad = jnp.sum(gradient, axis=0, keepdims=True, dtype=f32)
    wide_grads = [None] * LAYERS
    tall_grads = [None] * LAYERS

    def core_sum(blocks):
        return sum_blocks(blocks, SEQ, n_s).astype(bf16)

    def head_sum(mine):
        return lax.psum_scatter(mine, HEAD, scatter_dimension=0, tiled=False)

    def send_shares(mine):
        return exchange(mine.reshape(n_t, cut, -1), DP)

    feed_shares = [None] * LAYERS
    mixed_shares = [None] * LAYERS
    feed_sums = [None] * LAYERS
    mixed_sums = [None] * LAYERS
    for layer in reversed(range(LAYERS)):
        (
            (mixed, feed),
            (hidden, hidden_mid, normed_one, normed_two),
            (queries, both, logs, context, pre_up, activation),
        ) = records[layer]
        last = layer == LAYERS - 1
        pre_grad, up_bias_grad, out = feed_back(grad_low, feed, pre_up)
        got = send_sums(out)
        feed_grad = weight_back(normed_two, pre_grad, grad_low, activation, n_s)
        if last:
            got, feed_grad, output_low = meet(got, feed_grad, output_low)
            output_planes = to_planes_of(output_low)
        else:
            got, feed_grad = meet(got, feed_grad)
        mid_grad, low, sums_two = norm_back(
            hidden_mid, gradient, got, vectors, vector(3, layer)
        )
        mid_low = send_rows(low)
        mine = core_sum(feed_grad)
        if last:
            mid_low, mine = meet(mid_low, mine)
        else:
            mid_low, mine = meet(mid_low, mine)
        feed_sums[layer] = head_sum(mine)
        query_grad, both_grads = attend_back(
            mid_low, queries, both, mixed, context, logs, slopes, key_pos, query_pos
        )
        if not last:
            feed_share = send_shares(after(feed_sums[layer + 1], mid_low[-1]))
            both_grads, feed_shares[layer + 1] = meet(both_grads, feed_share)
        got = deal(both_grads, SEQ, n_s)
        joined, qkv_sums, out = project_back(query_grad, got, mixed, n_t, width)
        got = send_sums(out)
        mixed_grad = weight_back(normed_one, joined, mid_low, context, n_s)
        if last:
            planes = after(output_planes, joined)
            got, mixed_grad, output = meet(got, mixed_grad, send_output(planes))
        else:
            mixed_sums[layer] = head_sum(after(core_sum(mixed_grad), feed_sums[layer]))
        gradient, low, sums_one = norm_back(
            hidden, mid_grad, got, vectors, vector(0, layer)
        )
        if layer > 0:
            grad_low, mine = meet(send_rows(low), core_sum(mixed_grad))
            mixed_sums[layer] = head_sum(mine)
        wide_grads[layer] = jnp.stack(
            (
                sums_one[0],
                sums_one[1],
                sums_two[2],
                sums_two[0],
                sums_two[1],
                down_bias_grad[0],
            )
        )
        down_bias_grad = sums_one[2:3]
        tall_grads[layer] = jnp.concatenate(
            (qkv_sums[:, 0, :HD], qkv_sums[:, 0, 2 * HD :], up_bias_grad[:, 0]), axis=1
        )

    low_outer = turned_sum([low], turn, counts, False)
    tokens_planes = to_planes_of(after(low_outer, mixed_sums[0]))
    mixed_shares[1] = send_shares(after(mixed_sums[1], low))
    feed_shares[0] = send_shares(after(feed_sums[0], low))
    mixed_shares[0] = send_shares(mixed_sums[0])
    tokens_grad = send_output(tokens_planes).astype(f32)
    feed_shares = [after(share, low) for share in feed_shares]

    def fold(arrays, name, size):
        total = arrays[0]
        for step in range(1, size):
            total = total + swap(arrays[step], name, size, step)
        return total

    wide = jnp.stack(wide_grads).reshape(LAYERS * 6, n_s, n_t, cut)
    pieces, begin = [], 0
    tall = jnp.stack(tall_grads)
    for size in tall_sizes:
        piece = tall[:, :, begin : begin + size]
        begin += size
        piece = piece.reshape(LAYERS, n_z, n_t, n_s, size // (n_t * n_s))
        pieces.append(flip(flip(piece, c, 3), z, 1))
    tall = jnp.concatenate(
        [piece.transpose(3, 1, 2, 0, 4).reshape(n_s, n_z, n_t, -1) for piece in pieces], axis=3
    )
    wide = wide.transpose(1, 2, 0, 3).reshape(n_s, n_t, -1)
    n_wide = wide.shape[2]
    wide = jnp.broadcast_to(wide[:, None], (n_s, n_z) + wide.shape[1:])
    joint = jnp.concatenate((wide, tall), axis=3)
    joint = fold([joint[step] for step in range(n_s)], SEQ, n_s)
    joint = fold([joint[step] for step in range(n_z)], HEAD, n_z)
    joint = flip(joint, d)
    got = deal([joint[step] for step in range(n_t)], DP, n_t)
    wide = functools.reduce(jnp.add, [item[:n_wide] for item in got])
    wide = wide.reshape(LAYERS, 6, cut)
    tall = flip(jnp.stack([item[n_wide:] for item in got]), d)
    outs, begin = [], 0
    for size in tall_sizes:
        size = size // (n_t * n_s)
        piece = tall[:, begin : begin + LAYERS * size].reshape(n_t, LAYERS, size)
        begin += LAYERS * size
        outs.append(piece.transpose(1, 0, 2))
    query_bias_grad, value_bias_grad, up_bias_grad = outs
    def rows_first(shares, begin, end):
        parts = [share[:, :, begin:end].transpose(1, 0, 2).reshape(cut, -1) for share in shares]
        return jnp.stack(parts).astype(f32)

    def columns_first(shares, begin, end):
        parts = [share[:, :, begin:end].transpose(0, 2, 1).reshape(-1, cut) for share in shares]
        return jnp.stack(parts).astype(f32)

    qkv_grad = rows_first(mixed_shares, 0, qkv_columns)
    dense_grad = columns_first(mixed_shares, qkv_columns, columns)
    up_grad = rows_first(feed_shares, 0, units)
    down_grad = columns_first(feed_shares, units, 2 * units)
    return (
        output,
        tokens_grad,
        qkv_grad,
        dense_grad,
        up_grad,
        down_grad,
        wide[:, 0],
        wide[:, 1],
        query_bias_grad,
        value_bias_grad,
        wide[:, 2],
        wide[:, 3],
        wide[:, 4],
        up_bias_grad,
        wide[:, 5],
    )


def solution(mesh):
    sizes = tuple(mesh.shape[name] for name in (DP, SEQ, HEAD))
    rows = P(DP, SEQ, None)
    tall = P(None, (DP, SEQ), HEAD)
    flat = P(None, HEAD, (DP, SEQ))
    vector = P(None, (DP, SEQ))
    params = (
        tall,
        flat,
        tall,
        flat,
        vector,
        vector,
        flat,
        flat,
        vector,
        vector,
        vector,
        flat,
        vector,
    )
    return jax.shard_map(
        functools.partial(per_device, sizes),
        mesh=mesh,
        in_specs=(rows,) + params + (rows,),
        out_specs=(rows, rows) + params,
        check_vma=False,
    )
```

```python
import functools
import math

import jax
import jax.numpy as jnp
from jax import lax
from jax.experimental import pallas as pl
from jax.experimental.pallas import tpu as pltpu
from jax.sharding import PartitionSpec as P

H = 16
HD = 64
LAYERS = 2
DP, SEQ, HEAD = "dp", "seq", "head"

epsilon = 1e-05
masked_value = -1000000000.0
VMEM_LIMIT = 60 * 1024 * 1024
bf16 = jnp.bfloat16
f32 = jnp.float32


def flip_list(blocks, index):
    bit = 1
    while bit < len(blocks):
        turn = (index & bit) != 0
        blocks = [
            jax.tree.map(lambda x, y: jnp.where(turn, x, y), blocks[j ^ bit], blocks[j])
            for j in range(len(blocks))
        ]
        bit *= 2
    return blocks


def flip(array, index, axis=0):
    blocks = [lax.index_in_dim(array, j, axis, keepdims=True) for j in range(array.shape[axis])]
    return jnp.concatenate(flip_list(blocks, index), axis=axis)


def swap(array, name, size, step):
    return lax.ppermute(array, name, [(i, i ^ step) for i in range(size)])


def gather(array, name, size):
    return [array] + [swap(array, name, size, step) for step in range(1, size)]


def deal(blocks, name, size):
    return [blocks[0]] + [swap(blocks[step], name, size, step) for step in range(1, size)]


def exchange(array, name):
    return lax.all_to_all(array, name, 0, 0, tiled=True)


def meet(*groups):
    return lax.optimization_barrier(groups)


def add_all(blocks):
    return functools.reduce(jnp.add, [block.astype(f32) for block in blocks])


def sum_blocks(blocks, name, size):
    total = blocks[0].astype(f32)
    for step in range(1, size):
        total = total + swap(blocks[step].astype(bf16), name, size, step).astype(f32)
    return total


def after(array, *others):
    return lax.optimization_barrier((array,) + others)[0]


def dot(left, right, left_dim, right_dim):
    dims = (((left_dim,), (right_dim,)), ((), ()))
    return lax.dot_general(left, right, dims, preferred_element_type=f32)


def gelu_tanh(values):
    argument = 0.7978845608028654 * (values + 0.044715 * values * values * values)
    return 0.5 * values * (1.0 + jnp.tanh(argument))


def gelu_slope(values):
    square = values * values
    bent = jnp.tanh(0.7978845608028654 * (values + 0.044715 * values * square))
    inner = 0.7978845608028654 * (1.0 + 3.0 * 0.044715 * square)
    return 0.5 * (1.0 + bent) + 0.5 * values * (1.0 - bent * bent) * inner


def norm_parts(values):
    row_mean = jnp.mean(values, axis=-1, keepdims=True)
    centred = values - row_mean
    scale = lax.rsqrt(jnp.mean(centred * centred, axis=-1, keepdims=True) + epsilon)
    return centred * scale, scale


def run(body, steps, each_in, whole_in, each_out, whole_out, scratch=(), flops=0):
    def each(array):
        zeros = (0,) * (len(array.shape) - 1)
        return pl.BlockSpec((None,) + tuple(array.shape[1:]), lambda z: (z,) + zeros)

    def whole(array):
        zeros = (0,) * len(array.shape)
        return pl.BlockSpec(tuple(array.shape), lambda z: zeros)

    counts = [len(part) for part in (each_in, whole_in, each_out, whole_out)]

    def kernel(*refs):
        parts, begin = [], 0
        for count in counts:
            parts.append(refs[begin : begin + count])
            begin += count
        body(pl.program_id(0), *parts, refs[begin:])

    arrays = list(each_in) + list(whole_in)
    shapes = list(each_out) + list(whole_out)
    moved = sum(math.prod(item.shape) * item.dtype.itemsize for item in arrays + shapes)
    return pl.pallas_call(
        kernel,
        grid=(steps,),
        in_specs=[each(item) for item in each_in] + [whole(item) for item in whole_in],
        out_specs=[each(item) for item in each_out] + [whole(item) for item in whole_out],
        out_shape=shapes,
        scratch_shapes=list(scratch),
        compiler_params=pltpu.CompilerParams(vmem_limit_bytes=VMEM_LIMIT),
        cost_estimate=pl.CostEstimate(flops=flops, bytes_accessed=moved, transcendentals=0),
    )(*arrays)


def shape(dims, kind):
    return jax.ShapeDtypeStruct(tuple(dims), kind)


def lay(target, blocks):
    rows = blocks[0].shape[0]
    for index, block in enumerate(blocks):
        target[index * rows : (index + 1) * rows, :] = block[...]


def spread(blocks, source):
    rows = blocks[0].shape[0]
    for index, block in enumerate(blocks):
        block[...] = source[index * rows : (index + 1) * rows, :].astype(block.dtype)


def times(array, planes, begin, end):
    part = array.shape[1] // len(planes)
    total = None
    for s, plane in enumerate(planes):
        term = dot(array[:, s * part : (s + 1) * part], plane[:part, begin:end], 1, 0)
        total = term if total is None else total + term
    return total


def add_back(acc, array, planes, begin, end):
    part = acc.shape[1] // len(planes)
    for s, plane in enumerate(planes):
        acc[:, s * part : (s + 1) * part] += dot(array, plane[:part, begin:end], 1, 1)


def project(blocks, planes, bias, vectors=None, gain=None, shift=None):
    rows, width = blocks[0].shape
    length = rows * len(blocks)
    heads = planes[0].shape[0]
    n, n_blocks = len(planes), len(blocks)
    vectors = [] if gain is None else [vectors]

    def body(z, each_in, whole_in, each_out, whole_out, scratch):
        wide = scratch[0]

        @pl.when(z == 0)
        def _():
            lay(wide, whole_in[:n_blocks])
            if vectors:
                lines = whole_in[n_blocks]
                normed = wide[...].astype(f32) * lines[gain : gain + 1, :]
                normed = normed + lines[shift : shift + 1, :]
                wide[...] = normed.astype(bf16)
                spread(whole_out, wide)

        got = times(wide, each_in[:n], 0, 3 * HD) + each_in[n][...]
        low = got.astype(bf16)
        each_out[0][...] = low[:, :HD] * jnp.asarray(1.0 / math.sqrt(HD), bf16)
        each_out[1][...] = low[:, HD:]

    out = run(
        body,
        heads,
        list(planes) + [bias],
        list(blocks) + vectors,
        [shape((heads, length, HD), bf16), shape((heads, length, 2 * HD), bf16)],
        [shape((rows, width), bf16)] * n_blocks if vectors else [],
        [pltpu.VMEM((length, width), bf16)],
        2 * heads * length * width * 3 * HD,
    )
    return out[0], out[1], out[2:] or blocks


def masked_scores(queries, both, slope, key_pos, query_pos):
    scores = dot(queries, both[:, :HD], 1, 1) + slope * key_pos
    return jnp.where(key_pos <= query_pos, scores, masked_value)


def attend(queries, both, planes, slopes, key_pos, query_pos, n_t, width):
    heads, length, _ = queries.shape
    n = len(planes)
    rows = length // n_t

    def body(z, each_in, whole_in, each_out, whole_out, scratch):
        kv, weights = each_in[1 : 1 + n], each_in[1 + n : 1 + 2 * n]
        slope = each_in[1 + 2 * n][:, :1]
        acc = scratch[0]

        @pl.when(z == 0)
        def _():
            acc[...] = jnp.zeros_like(acc)

        low_queries = each_in[0][...]
        scores = [
            masked_scores(low_queries, kv[s], slope, whole_in[0][s], whole_in[1][...])
            for s in range(n)
        ]
        top = functools.reduce(jnp.maximum, [jnp.max(x, axis=1, keepdims=True) for x in scores])
        shifted = [jnp.exp(x - top) for x in scores]
        total = sum(jnp.sum(x, axis=1, keepdims=True) for x in shifted)
        context = sum(dot(x.astype(bf16), kv[s][:, HD:], 1, 0) for s, x in enumerate(shifted))
        low = (context / total).astype(bf16)
        each_out[0][...] = low
        each_out[1][...] = top + jnp.log(total)
        add_back(acc, low, weights, 3 * HD, 4 * HD)

        @pl.when(z == heads - 1)
        def _():
            spread(whole_out, acc)

    out = run(
        body,
        heads,
        [queries] + list(both) + list(planes) + [slopes],
        [key_pos, query_pos],
        [shape((heads, length, HD), bf16), shape((heads, length, 1), f32)],
        [shape((rows, width), bf16)] * n_t,
        [pltpu.VMEM((length, width), f32)],
        2 * heads * length * (2 * HD * length * n + HD * width),
    )
    return out[0], out[1], out[2:]


def attend_back(blocks, queries, both, planes, context, logs, slopes, key_pos, query_pos):
    heads, length, _ = queries.shape
    n = len(planes)
    width = blocks[0].shape[1]

    def body(z, each_in, whole_in, each_out, whole_out, scratch):
        @pl.when(z == 0)
        def _():
            lay(scratch[0], whole_in[2:])

        kv, weights = each_in[1 : 1 + n], each_in[1 + n : 1 + 2 * n]
        context_ref, logs_ref, slope_ref = each_in[1 + 2 * n :]
        slope = slope_ref[:, :1]
        low_queries = each_in[0][...]
        grads = times(scratch[0], weights, 3 * HD, 4 * HD).astype(bf16)
        inner = jnp.sum(grads.astype(f32) * context_ref[...].astype(f32), axis=1, keepdims=True)
        query_grad = None
        for s in range(n):
            scores = masked_scores(low_queries, kv[s], slope, whole_in[0][s], whole_in[1][...])
            probs = jnp.exp(scores - logs_ref[...])
            prob_grad = dot(grads, kv[s][:, HD:], 1, 1)
            score_grad = (probs * (prob_grad - inner)).astype(bf16)
            term = dot(score_grad, kv[s][:, :HD], 1, 0)
            query_grad = term if query_grad is None else query_grad + term
            each_out[1 + s][:, :HD] = dot(score_grad, low_queries, 0, 0).astype(bf16)
            each_out[1 + s][:, HD:] = dot(probs.astype(bf16), grads, 0, 0).astype(bf16)
        each_out[0][...] = (query_grad * (1.0 / math.sqrt(HD))).astype(bf16)

    out = run(
        body,
        heads,
        [queries] + list(both) + list(planes) + [context, logs, slopes],
        [key_pos, query_pos] + list(blocks),
        [shape((heads, length, HD), bf16)] + [shape((heads, length, 2 * HD), bf16)] * n,
        [],
        [pltpu.VMEM((length, width), bf16)],
        2 * heads * length * (5 * HD * length * n + HD * width),
    )
    return out[0], out[1:]


def project_back(query_grad, both_grads, planes, n_t, width):
    heads, length, _ = query_grad.shape
    n = len(planes)
    rows = length // n_t

    def body(z, each_in, whole_in, each_out, whole_out, scratch):
        acc = scratch[0]

        @pl.when(z == 0)
        def _():
            acc[...] = jnp.zeros_like(acc)

        low = sum(item[...].astype(f32) for item in each_in[1 : 1 + n]).astype(bf16)
        joined, sums = each_out
        joined[:, :HD] = each_in[0][...]
        joined[:, HD:] = low
        sums[:, :HD] = jnp.sum(each_in[0][...].astype(f32), axis=0, keepdims=True)
        sums[:, HD:] = jnp.sum(low.astype(f32), axis=0, keepdims=True)
        add_back(acc, joined[...], each_in[1 + n :], 0, 3 * HD)

        @pl.when(z == heads - 1)
        def _():
            spread(whole_out, acc)

    out = run(
        body,
        heads,
        [query_grad] + list(both_grads) + list(planes),
        [],
        [shape((heads, length, 3 * HD), bf16), shape((heads, 1, 3 * HD), f32)],
        [shape((rows, width), bf16)] * n_t,
        [pltpu.VMEM((length, width), f32)],
        2 * heads * length * width * 3 * HD,
    )
    return out[0], out[1], out[2:]


def feed_forward(blocks, planes, bias):
    rows, width = blocks[0].shape
    length = rows * len(blocks)
    heads, _, units = bias.shape
    n = len(planes)

    def body(z, each_in, whole_in, each_out, whole_out, scratch):
        wide, acc = scratch

        @pl.when(z == 0)
        def _():
            lay(wide, whole_in)
            acc[...] = jnp.zeros_like(acc)

        pre_up = times(wide, each_in[:n], 0, units) + each_in[n][...]
        each_out[0][...] = pre_up
        low = gelu_tanh(pre_up).astype(bf16)
        each_out[1][...] = low
        add_back(acc, low, each_in[:n], units, 2 * units)

        @pl.when(z == heads - 1)
        def _():
            spread(whole_out, acc)

    out = run(
        body,
        heads,
        list(planes) + [bias],
        blocks,
        [shape((heads, length, units), f32), shape((heads, length, units), bf16)],
        [shape((rows, width), bf16)] * len(blocks),
        [pltpu.VMEM((length, width), bf16), pltpu.VMEM((length, width), f32)],
        4 * heads * length * width * units,
    )
    return out[0], out[1], out[2:]


def feed_back(blocks, planes, pre_up):
    rows, width = blocks[0].shape
    length = rows * len(blocks)
    heads, _, units = pre_up.shape
    n = len(planes)

    def body(z, each_in, whole_in, each_out, whole_out, scratch):
        wide, acc = scratch

        @pl.when(z == 0)
        def _():
            lay(wide, whole_in)
            acc[...] = jnp.zeros_like(acc)

        act_grad = times(wide, each_in[:n], units, 2 * units)
        low = (act_grad * gelu_slope(each_in[n][...])).astype(bf16)
        each_out[0][...] = low
        each_out[1][...] = jnp.sum(low.astype(f32), axis=0, keepdims=True)
        add_back(acc, low, each_in[:n], 0, units)

        @pl.when(z == heads - 1)
        def _():
            spread(whole_out, acc)

    out = run(
        body,
        heads,
        list(planes) + [pre_up],
        blocks,
        [shape((heads, length, units), bf16), shape((heads, 1, units), f32)],
        [shape((rows, width), bf16)] * len(blocks),
        [pltpu.VMEM((length, width), bf16), pltpu.VMEM((length, width), f32)],
        4 * heads * length * width * units,
    )
    return out[0], out[1], out[2:]


def weight_back(one_blocks, one, two_blocks, two, n):
    rows, width = one_blocks[0].shape
    length = rows * len(one_blocks)
    heads, _, first = one[0].shape
    second = two[0].shape[2]
    part = width // n
    half = len(one_blocks)

    def summed(wide, cols, items):
        total, begin = None, 0
        for item in items:
            end = begin + item.shape[0]
            term = dot(wide[begin:end, cols], item[...], 0, 0)
            total = term if total is None else total + term
            begin = end
        return total.astype(bf16)

    def body(z, each_in, whole_in, each_out, whole_out, scratch):
        @pl.when(z == 0)
        def _():
            lay(scratch[0], whole_in[:half])
            lay(scratch[1], whole_in[half:])

        for s in range(n):
            cols = slice(s * part, (s + 1) * part)
            each_out[s][:, :first] = summed(scratch[0], cols, each_in[: len(one)])
            each_out[s][:, first:] = summed(scratch[1], cols, each_in[len(one) :])

    return run(
        body,
        heads,
        list(one) + list(two),
        list(one_blocks) + list(two_blocks),
        [shape((heads, part, first + second), bf16)] * n,
        [],
        [pltpu.VMEM((length, width), bf16)] * 2,
        2 * heads * length * width * (first + second),
    )


def norm_forward(values, got, vectors, bias, gain, shift):
    def body(z, each_in, whole_in, each_out, whole_out, scratch):
        start, rows = whole_in[:2]
        total = start[...] + rows[bias : bias + 1, :]
        for item in whole_in[2:]:
            total = total + item[...].astype(f32)
        whole_out[0][...] = total
        xhat, _ = norm_parts(total)
        normed = xhat * rows[gain : gain + 1, :] + rows[shift : shift + 1, :]
        whole_out[1][...] = normed.astype(bf16)

    shapes = [shape(values.shape, f32), shape(values.shape, bf16)]
    return run(body, 1, [], [values, vectors] + list(got), [], shapes)


def norm_back(values, gradient, got, vectors, gain):
    width = values.shape[1]

    def body(z, each_in, whole_in, each_out, whole_out, scratch):
        e = sum(item[...].astype(f32) for item in whole_in[3:])
        xhat, scale = norm_parts(whole_in[0][...])
        eg = e * whole_in[2][gain : gain + 1, :]
        back = scale * (
            eg
            - jnp.mean(eg, axis=-1, keepdims=True)
            - xhat * jnp.mean(eg * xhat, axis=-1, keepdims=True)
        )
        fresh = whole_in[1][...].astype(f32) + back
        whole_out[0][...] = fresh
        whole_out[1][...] = fresh.astype(bf16)
        whole_out[2][0:1, :] = jnp.sum(e * xhat, axis=0, keepdims=True)
        whole_out[2][1:2, :] = jnp.sum(e, axis=0, keepdims=True)
        whole_out[2][2:3, :] = jnp.sum(fresh, axis=0, keepdims=True)

    shapes = [shape(values.shape, f32), shape(values.shape, bf16), shape((3, width), f32)]
    return run(body, 1, [], [values, gradient, vectors] + list(got), [], shapes)


def turn_columns(array, turn, counts, inward):
    n_t, n_s = counts
    cut = array.shape[1] // (n_t * n_s)
    parts = [array[:, j * cut : (j + 1) * cut] for j in range(n_t * n_s)]
    index = turn[:, :cut]
    if inward:
        groups = flip_list([parts[s::n_s] for s in range(n_s)], index)
        return [part for group in groups for part in group]
    groups = flip_list([parts[k * n_t : (k + 1) * n_t] for k in range(n_s)], index)
    return [groups[s][t] for t in range(n_t) for s in range(n_s)]


def store_columns(target, parts):
    cut = parts[0].shape[1]
    for j, part in enumerate(parts):
        target[:, j * cut : (j + 1) * cut] = part.astype(target.dtype)


def first_norm(items, turn, counts):
    dims = items[0].shape

    def body(z, each_in, whole_in, each_out, whole_out, scratch):
        total = sum(item[...].astype(f32) for item in whole_in[1:])
        store_columns(whole_out[0], turn_columns(total, whole_in[0][...], counts, True))
        whole_out[1][...] = norm_parts(whole_out[0][...])[0].astype(bf16)

    return run(body, 1, [], [turn] + list(items), [], [shape(dims, f32), shape(dims, bf16)])


def turned_sum(items, turn, counts, inward, bias=None):
    dims = items[0].shape

    def body(z, each_in, whole_in, each_out, whole_out, scratch):
        count = len(whole_in) - (0 if bias is None else 1)
        total = sum(item[...].astype(f32) for item in whole_in[1:count])
        if bias is not None:
            total = total + whole_in[count][bias : bias + 1, :]
        store_columns(whole_out[0], turn_columns(total, whole_in[0][...], counts, inward))

    return run(body, 1, [], [turn] + list(items), [], [shape(dims, bf16)])[0]


def unpack(planes, turn, counts, width, layers, spare):
    n_t, n_s = counts
    heads, _, columns = planes[0].shape
    part, cut = width // n_s, width // (n_s * n_t)
    small = HD // (n_t * n_s)
    units = columns
    unit = units // (n_t * n_s)
    half = columns // 2

    def kernel(*refs):
        ex, index, outs = refs[:n_s], refs[n_s], refs[n_s + 1 :]
        vectors, qkv, up = outs[0], outs[1 : 1 + layers], outs[1 + layers :]
        for layer in range(layers):
            qkv[layer][...] = jnp.zeros_like(qkv[layer])
        for t in range(n_t):
            rows = slice(t * spare, (t + 1) * spare)
            for k in range(n_s):
                place = (k * n_t + t) * cut
                vectors[:, place : place + cut] = ex[k][0, rows, :cut].astype(f32)
            for head in range(heads):
                blocks = [ex[k][head, rows, half:].astype(f32) for k in range(n_s)]
                blocks = flip_list(blocks, index[:, :half])
                for s in range(n_s):
                    place = t * n_s + s
                    for layer in range(layers):
                        row = blocks[s][layer : layer + 1, :]
                        at = place * small
                        qkv[layer][head, :, at : at + small] = row[:, :small]
                        at += 2 * HD
                        qkv[layer][head, :, at : at + small] = row[:, small : 2 * small]
                        at = place * unit
                        up[layer][head, :, at : at + unit] = row[:, 2 * small : 2 * small + unit]

    block = pl.BlockSpec((heads, n_t * spare, columns), lambda i: (0, part // (n_t * spare), 0))
    shapes = [shape((spare, width), f32)]
    shapes += [shape((heads, 1, 3 * HD), f32)] * layers
    shapes += [shape((heads, 1, units), f32)] * layers

    def whole(dims):
        return pl.BlockSpec(dims, lambda i: (0,) * len(dims))

    out = pl.pallas_call(
        kernel,
        grid=(1,),
        in_specs=[block] * n_s + [whole(turn.shape)],
        out_specs=[whole(item.shape) for item in shapes],
        out_shape=shapes,
        compiler_params=pltpu.CompilerParams(vmem_limit_bytes=VMEM_LIMIT),
    )(*planes, turn)
    return out[0], out[1 : 1 + layers], out[1 + layers :]


def per_device(
    sizes,
    tokens,
    qkv_weight,
    dense_weight,
    up_weight,
    down_weight,
    first_gain,
    first_shift,
    query_bias,
    value_bias,
    dense_bias,
    second_gain,
    second_shift,
    up_bias,
    down_bias,
    cotangent,
):
    n_t, n_s, n_z = sizes
    seq_count, slice_len, width = tokens.shape
    assert seq_count == 1 and n_t == n_z
    d, c, z = (lax.axis_index(name) for name in (DP, SEQ, HEAD))
    rows = slice_len // n_t
    cut = qkv_weight.shape[1]
    part = cut * n_t
    heads = query_bias.shape[1]
    assert heads == n_t
    units = up_bias.shape[2] * n_t * n_s

    def spread_rows(array):
        return exchange(array.reshape(n_t, rows, width), DP)

    def own_rows(blocks):
        return lax.dynamic_index_in_dim(blocks, z, 0, False)

    def send_rows(array):
        return gather(array, DP, n_t)

    def in_halves(blocks):
        return [blocks]

    def send_sums(blocks):
        return deal(blocks, DP, n_t)

    def to_planes_of(array):
        return lax.all_gather(array, HEAD, axis=0, tiled=False)

    def send_output(planes):
        return exchange(planes, DP).reshape(1, slice_len, width)

    def packed_mixed(layer):
        qkv = qkv_weight[layer].reshape(cut, n_t, -1).transpose(1, 0, 2)
        dense = dense_weight[layer].reshape(n_t, -1, cut).transpose(0, 2, 1)
        return jnp.concatenate((qkv, dense), axis=2)

    def packed_feed(layer):
        up = up_weight[layer].reshape(cut, n_t, -1).transpose(1, 0, 2)
        down = down_weight[layer].reshape(n_t, -1, cut).transpose(0, 2, 1)
        return jnp.concatenate((up, down), axis=2)

    def to_planes(blocks):
        return exchange(blocks, DP).reshape(part, -1)

    def join(planes):
        return gather(planes, SEQ, n_s)

    counts = (n_t, n_s)
    turn = jnp.full((1, 128), c, jnp.int32)
    wide = jnp.concatenate(
        (first_gain, first_shift, dense_bias, second_gain, second_shift, down_bias), axis=0
    )
    tall = jnp.concatenate((query_bias, value_bias, up_bias), axis=2).transpose(1, 0, 2)
    columns, spare = 4 * HD, 16
    half = columns // 2
    wide = jnp.pad(wide, ((0, spare - 6 * LAYERS), (0, half - cut)))
    tall = jnp.pad(tall, ((0, 0), (0, spare - LAYERS), (0, half - tall.shape[2])))
    small = jnp.concatenate((jnp.broadcast_to(wide[None], (n_t, spare, half)), tall), axis=2)
    first = jnp.concatenate((packed_mixed(0), small.astype(bf16)), axis=1)
    first = exchange(first, DP)
    first_shard = jnp.concatenate(
        (first[:, :cut].reshape(part, columns), first[:, cut:].reshape(-1, columns)), axis=0
    )
    messages = [to_planes_of(first_shard)]
    hidden, low = first_norm([own_rows(spread_rows(tokens[0]))], turn, counts)
    normed_one = send_rows(low)
    normed_one, pack = meet(normed_one, packed_feed(0))
    messages.append(to_planes_of(to_planes(pack)))
    messages[0], normed_one = meet(messages[0], normed_one)
    mixed = join(messages[0])
    vectors, biases_qkv, biases_up = unpack(mixed, turn, counts, width, LAYERS, spare)
    tall_sizes = (HD, HD, units)

    def vector(kind, layer):
        return kind * LAYERS + layer

    qkv_columns = 3 * HD
    head_ids = jnp.arange(n_z, dtype=jnp.int32) * heads + d
    slopes = 2.0 ** (-8.0 * (head_ids + 1).astype(f32) / H)
    slopes = jnp.broadcast_to(slopes[:, None, None], (n_z, 1, 128))
    block_ids = (d ^ jnp.arange(n_t, dtype=jnp.int32)) * rows
    own_pos = (block_ids[:, None] + jnp.arange(rows, dtype=jnp.int32)[None]).reshape(-1)
    query_pos = (c * slice_len + own_pos).astype(f32)[:, None]
    others = (c ^ jnp.arange(n_s, dtype=jnp.int32)) * slice_len
    key_pos = (others[:, None] + own_pos[None]).astype(f32)[:, None, :]
    cot = cotangent[0]
    records = []
    for layer in range(LAYERS):
        if layer > 0:
            normed_one = send_rows(low)
            normed_one, messages[2 * layer] = meet(normed_one, messages[2 * layer])
            mixed = join(messages[2 * layer])
        affine = (vectors, vector(0, 0), vector(1, 0)) if layer == 0 else ()
        queries, both, normed_one = project(normed_one, mixed, biases_qkv[layer], *affine)
        both = gather(both, SEQ, n_s)
        if layer == 0:
            later = jnp.concatenate((packed_mixed(1), packed_feed(1)), axis=2)
            both, later = meet(both, later)
            later = to_planes(later)
        else:
            both, cot_rows = meet(both, cot_rows)
            cot_rows = send_rows(cot_rows)
        context, logs, out = attend(queries, both, mixed, slopes, key_pos, query_pos, n_t, width)
        if layer == 0:
            out, later = meet(out, later)
        else:
            out, cot_rows = meet(out, cot_rows)
        got = send_sums(out)
        got, messages[2 * layer + 1] = meet(got, messages[2 * layer + 1])
        feed = join(messages[2 * layer + 1])
        if layer == 0:
            got, later = meet(got, later)
            messages.append(to_planes_of(later[:, :columns]))
            messages.append(to_planes_of(later[:, columns:]))
        hidden_mid, low = norm_forward(
            hidden, got, vectors, vector(2, layer), vector(3, layer), vector(4, layer)
        )
        normed_two = send_rows(low)
        if layer == 0:
            normed_two, cot_rows = meet(normed_two, cot)
            cot_rows = spread_rows(cot_rows)
        halves = [feed_forward(part, feed, biases_up[layer]) for part in in_halves(normed_two)]
        pre_up, activation, out = (list(item) for item in zip(*halves))
        out = [block for part in out for block in part]
        got = send_sums(out)
        if layer == 0:
            got, cot_rows = meet(got, turned_sum([own_rows(cot_rows)], turn, counts, True))
        records.append(
            (
                (mixed, feed),
                (hidden, hidden_mid, normed_one, normed_two),
                (queries, both, logs, context, pre_up, activation),
            )
        )
        if layer + 1 < LAYERS:
            hidden, low = norm_forward(
                hidden_mid,
                got,
                vectors,
                vector(5, layer),
                vector(0, layer + 1),
                vector(1, layer + 1),
            )

    last_bias = vector(5, LAYERS - 1)
    output_low = turned_sum([hidden_mid] + list(got) + [vectors], turn, counts, False, last_bias)

    gradient = cot_rows[0]
    grad_low = cot_rows
    down_bias_grad = jnp.sum(gradient, axis=0, keepdims=True, dtype=f32)
    wide_grads = [None] * LAYERS
    tall_grads = [None] * LAYERS

    def core_sum(blocks):
        return sum_blocks(blocks, SEQ, n_s).astype(bf16)

    def head_sum(mine):
        return lax.psum_scatter(mine, HEAD, scatter_dimension=0, tiled=False)

    def send_shares(mine):
        return exchange(mine.reshape(n_t, cut, -1), DP)

    feed_shares = [None] * LAYERS
    mixed_shares = [None] * LAYERS
    feed_sums = [None] * LAYERS
    mixed_sums = [None] * LAYERS
    for layer in reversed(range(LAYERS)):
        (
            (mixed, feed),
            (hidden, hidden_mid, normed_one, normed_two),
            (queries, both, logs, context, pre_up, activation),
        ) = records[layer]
        last = layer == LAYERS - 1
        halves = [
            feed_back(part, feed, kept) for part, kept in zip(in_halves(grad_low), pre_up)
        ]
        pre_grad, up_bias_grad, out = (list(item) for item in zip(*halves))
        got = send_sums([block for part in out for block in part])
        up_bias_grad = functools.reduce(jnp.add, up_bias_grad)
        feed_grad = weight_back(normed_two, pre_grad, grad_low, activation, n_s)
        if last:
            got, feed_grad, output_low = meet(got, feed_grad, output_low)
            output_planes = to_planes_of(output_low)
        else:
            got, feed_grad, mixed_sums[1] = meet(got, feed_grad, mixed_sums[1])
        mid_grad, low, sums_two = norm_back(
            hidden_mid, gradient, got, vectors, vector(3, layer)
        )
        mid_low = send_rows(low)
        if last:
            mid_low, mine = meet(mid_low, core_sum(feed_grad))
        else:
            mid_low, mine, output_planes = meet(mid_low, core_sum(feed_grad), output_planes)
        feed_sums[layer] = head_sum(mine)
        query_grad, both_grads = attend_back(
            mid_low, queries, both, mixed, context, logs, slopes, key_pos, query_pos
        )
        if not last:
            both_grads, output = meet(both_grads, send_output(output_planes))
        got = deal(both_grads, SEQ, n_s)
        joined, qkv_sums, out = project_back(query_grad, got, mixed, n_t, width)
        got = send_sums(out)
        mixed_grad = weight_back(normed_one, [joined], mid_low, [context], n_s)
        if last:
            got, mixed_grad, output_planes = meet(got, mixed_grad, output_planes)
        else:
            got, feed_sums[0] = meet(got, feed_sums[0])
            mixed_sums[layer] = head_sum(core_sum(mixed_grad))
        gradient, low, sums_one = norm_back(
            hidden, mid_grad, got, vectors, vector(0, layer)
        )
        if layer > 0:
            grad_low, mine, feed_sums[layer] = meet(
                send_rows(low), core_sum(mixed_grad), feed_sums[layer]
            )
            mixed_sums[layer] = head_sum(mine)
        wide_grads[layer] = jnp.stack(
            (
                sums_one[0],
                sums_one[1],
                sums_two[2],
                sums_two[0],
                sums_two[1],
                down_bias_grad[0],
            )
        )
        down_bias_grad = sums_one[2:3]
        tall_grads[layer] = jnp.concatenate(
            (qkv_sums[:, 0, :HD], qkv_sums[:, 0, 2 * HD :], up_bias_grad[:, 0]), axis=1
        )

    low_outer = turned_sum([low], turn, counts, False)
    low_outer, mixed_sums[0] = meet(low_outer, mixed_sums[0])
    tokens_planes = to_planes_of(low_outer)
    low_outer, mixed_sums[1], feed_sums[0], feed_sums[1] = meet(
        low_outer, mixed_sums[1], feed_sums[0], feed_sums[1]
    )
    feed_shares[1] = send_shares(feed_sums[1])
    mixed_shares[1] = send_shares(mixed_sums[1])
    feed_shares[0] = send_shares(feed_sums[0])
    mixed_shares[0] = send_shares(mixed_sums[0])
    tokens_grad = send_output(tokens_planes).astype(f32)

    def fold(arrays, name, size):
        total = arrays[0]
        for step in range(1, size):
            total = total + swap(arrays[step], name, size, step)
        return total

    wide = jnp.stack(wide_grads).reshape(LAYERS * 6, n_s, n_t, cut)
    pieces, begin = [], 0
    tall = jnp.stack(tall_grads)
    for size in tall_sizes:
        piece = tall[:, :, begin : begin + size]
        begin += size
        piece = piece.reshape(LAYERS, n_z, n_t, n_s, size // (n_t * n_s))
        pieces.append(flip(flip(piece, c, 3), z, 1))
    tall = jnp.concatenate(
        [piece.transpose(3, 1, 2, 0, 4).reshape(n_s, n_z, n_t, -1) for piece in pieces], axis=3
    )
    wide = wide.transpose(1, 2, 0, 3).reshape(n_s, n_t, -1)
    n_wide = wide.shape[2]
    wide = jnp.broadcast_to(wide[:, None], (n_s, n_z) + wide.shape[1:])
    joint = jnp.concatenate((wide, tall), axis=3)
    joint = fold([joint[step] for step in range(n_s)], SEQ, n_s)
    joint = fold([joint[step] for step in range(n_z)], HEAD, n_z)
    joint = flip(joint, d)
    got = deal([joint[step] for step in range(n_t)], DP, n_t)
    wide = functools.reduce(jnp.add, [item[:n_wide] for item in got])
    wide = wide.reshape(LAYERS, 6, cut)
    tall = flip(jnp.stack([item[n_wide:] for item in got]), d)
    outs, begin = [], 0
    for size in tall_sizes:
        size = size // (n_t * n_s)
        piece = tall[:, begin : begin + LAYERS * size].reshape(n_t, LAYERS, size)
        begin += LAYERS * size
        outs.append(piece.transpose(1, 0, 2))
    query_bias_grad, value_bias_grad, up_bias_grad = outs
    def rows_first(shares, begin, end):
        parts = [share[:, :, begin:end].transpose(1, 0, 2).reshape(cut, -1) for share in shares]
        return jnp.stack(parts).astype(f32)

    def columns_first(shares, begin, end):
        parts = [share[:, :, begin:end].transpose(0, 2, 1).reshape(-1, cut) for share in shares]
        return jnp.stack(parts).astype(f32)

    qkv_grad = rows_first(mixed_shares, 0, qkv_columns)
    dense_grad = columns_first(mixed_shares, qkv_columns, columns)
    up_grad = rows_first(feed_shares, 0, units)
    down_grad = columns_first(feed_shares, units, 2 * units)
    return (
        output,
        tokens_grad,
        qkv_grad,
        dense_grad,
        up_grad,
        down_grad,
        wide[:, 0],
        wide[:, 1],
        query_bias_grad,
        value_bias_grad,
        wide[:, 2],
        wide[:, 3],
        wide[:, 4],
        up_bias_grad,
        wide[:, 5],
    )


def solution(mesh):
    sizes = tuple(mesh.shape[name] for name in (DP, SEQ, HEAD))
    rows = P(DP, SEQ, None)
    tall = P(None, (DP, SEQ), HEAD)
    flat = P(None, HEAD, (DP, SEQ))
    vector = P(None, (DP, SEQ))
    params = (
        tall,
        flat,
        tall,
        flat,
        vector,
        vector,
        flat,
        flat,
        vector,
        vector,
        vector,
        flat,
        vector,
    )
    return jax.shard_map(
        functools.partial(per_device, sizes),
        mesh=mesh,
        in_specs=(rows,) + params + (rows,),
        out_specs=(rows, rows) + params,
        check_vma=False,
    )
```

```python
import functools
import math

import jax
import jax.numpy as jnp
from jax import lax
from jax.experimental import pallas as pl
from jax.experimental.pallas import tpu as pltpu
from jax.sharding import PartitionSpec as P

H = 16
HD = 64
LAYERS = 2
DP, SEQ, HEAD = "dp", "seq", "head"

epsilon = 1e-05
masked_value = -1000000000.0
VMEM_LIMIT = 60 * 1024 * 1024
bf16 = jnp.bfloat16
f32 = jnp.float32


def flip_list(blocks, index):
    bit = 1
    while bit < len(blocks):
        turn = (index & bit) != 0
        blocks = [
            jax.tree.map(lambda x, y: jnp.where(turn, x, y), blocks[j ^ bit], blocks[j])
            for j in range(len(blocks))
        ]
        bit *= 2
    return blocks


def flip(array, index, axis=0):
    blocks = [lax.index_in_dim(array, j, axis, keepdims=True) for j in range(array.shape[axis])]
    return jnp.concatenate(flip_list(blocks, index), axis=axis)


def swap(array, name, size, step):
    return lax.ppermute(array, name, [(i, i ^ step) for i in range(size)])


def gather(array, name, size):
    return [array] + [swap(array, name, size, step) for step in range(1, size)]


def deal(blocks, name, size):
    return [blocks[0]] + [swap(blocks[step], name, size, step) for step in range(1, size)]


def exchange(array, name):
    return lax.all_to_all(array, name, 0, 0, tiled=True)


def meet(*groups):
    return lax.optimization_barrier(groups)


def add_all(blocks):
    return functools.reduce(jnp.add, [block.astype(f32) for block in blocks])


def sum_blocks(blocks, name, size):
    total = blocks[0].astype(f32)
    for step in range(1, size):
        total = total + swap(blocks[step].astype(bf16), name, size, step).astype(f32)
    return total


def after(array, *others):
    return lax.optimization_barrier((array,) + others)[0]


def dot(left, right, left_dim, right_dim):
    dims = (((left_dim,), (right_dim,)), ((), ()))
    return lax.dot_general(left, right, dims, preferred_element_type=f32)


def gelu_tanh(values):
    argument = 0.7978845608028654 * (values + 0.044715 * values * values * values)
    return 0.5 * values * (1.0 + jnp.tanh(argument))


def gelu_slope(values):
    square = values * values
    bent = jnp.tanh(0.7978845608028654 * (values + 0.044715 * values * square))
    inner = 0.7978845608028654 * (1.0 + 3.0 * 0.044715 * square)
    return 0.5 * (1.0 + bent) + 0.5 * values * (1.0 - bent * bent) * inner


def norm_parts(values):
    row_mean = jnp.mean(values, axis=-1, keepdims=True)
    centred = values - row_mean
    scale = lax.rsqrt(jnp.mean(centred * centred, axis=-1, keepdims=True) + epsilon)
    return centred * scale, scale


def run(body, steps, each_in, whole_in, each_out, whole_out, scratch=(), flops=0):
    def each(array):
        zeros = (0,) * (len(array.shape) - 1)
        return pl.BlockSpec((None,) + tuple(array.shape[1:]), lambda z: (z,) + zeros)

    def whole(array):
        zeros = (0,) * len(array.shape)
        return pl.BlockSpec(tuple(array.shape), lambda z: zeros)

    counts = [len(part) for part in (each_in, whole_in, each_out, whole_out)]

    def kernel(*refs):
        parts, begin = [], 0
        for count in counts:
            parts.append(refs[begin : begin + count])
            begin += count
        body(pl.program_id(0), *parts, refs[begin:])

    arrays = list(each_in) + list(whole_in)
    shapes = list(each_out) + list(whole_out)
    moved = sum(math.prod(item.shape) * item.dtype.itemsize for item in arrays + shapes)
    return pl.pallas_call(
        kernel,
        grid=(steps,),
        in_specs=[each(item) for item in each_in] + [whole(item) for item in whole_in],
        out_specs=[each(item) for item in each_out] + [whole(item) for item in whole_out],
        out_shape=shapes,
        scratch_shapes=list(scratch),
        compiler_params=pltpu.CompilerParams(vmem_limit_bytes=VMEM_LIMIT),
        cost_estimate=pl.CostEstimate(flops=flops, bytes_accessed=moved, transcendentals=0),
    )(*arrays)


def shape(dims, kind):
    return jax.ShapeDtypeStruct(tuple(dims), kind)


def lay(target, blocks):
    rows = blocks[0].shape[0]
    for index, block in enumerate(blocks):
        target[index * rows : (index + 1) * rows, :] = block[...]


def spread(blocks, source):
    rows = blocks[0].shape[0]
    for index, block in enumerate(blocks):
        block[...] = source[index * rows : (index + 1) * rows, :].astype(block.dtype)


def times(array, planes, begin, end):
    part = array.shape[1] // len(planes)
    total = None
    for s, plane in enumerate(planes):
        term = dot(array[:, s * part : (s + 1) * part], plane[:part, begin:end], 1, 0)
        total = term if total is None else total + term
    return total


def add_back(acc, array, planes, begin, end):
    part = acc.shape[1] // len(planes)
    for s, plane in enumerate(planes):
        acc[:, s * part : (s + 1) * part] += dot(array, plane[:part, begin:end], 1, 1)


def project(blocks, planes, bias, vectors=None, gain=None, shift=None):
    rows, width = blocks[0].shape
    length = rows * len(blocks)
    heads = planes[0].shape[0]
    n, n_blocks = len(planes), len(blocks)
    vectors = [] if gain is None else [vectors]

    def body(z, each_in, whole_in, each_out, whole_out, scratch):
        wide = scratch[0]

        @pl.when(z == 0)
        def _():
            lay(wide, whole_in[:n_blocks])
            if vectors:
                lines = whole_in[n_blocks]
                normed = wide[...].astype(f32) * lines[gain : gain + 1, :]
                normed = normed + lines[shift : shift + 1, :]
                wide[...] = normed.astype(bf16)
                spread(whole_out, wide)

        got = times(wide, each_in[:n], 0, 3 * HD) + each_in[n][...]
        low = got.astype(bf16)
        each_out[0][...] = low[:, :HD] * jnp.asarray(1.0 / math.sqrt(HD), bf16)
        each_out[1][...] = low[:, HD:]

    out = run(
        body,
        heads,
        list(planes) + [bias],
        list(blocks) + vectors,
        [shape((heads, length, HD), bf16), shape((heads, length, 2 * HD), bf16)],
        [shape((rows, width), bf16)] * n_blocks if vectors else [],
        [pltpu.VMEM((length, width), bf16)],
        2 * heads * length * width * 3 * HD,
    )
    return out[0], out[1], out[2:] or blocks


def masked_scores(queries, both, slope, key_pos, query_pos):
    scores = dot(queries, both[:, :HD], 1, 1) + slope * key_pos
    return jnp.where(key_pos <= query_pos, scores, masked_value)


def attend(queries, both, planes, slopes, key_pos, query_pos, n_t, width):
    heads, length, _ = queries.shape
    n = len(planes)
    rows = length // n_t

    def body(z, each_in, whole_in, each_out, whole_out, scratch):
        kv, weights = each_in[1 : 1 + n], each_in[1 + n : 1 + 2 * n]
        slope = each_in[1 + 2 * n][:, :1]
        acc = scratch[0]

        @pl.when(z == 0)
        def _():
            acc[...] = jnp.zeros_like(acc)

        low_queries = each_in[0][...]
        scores = [
            masked_scores(low_queries, kv[s], slope, whole_in[0][s], whole_in[1][...])
            for s in range(n)
        ]
        top = functools.reduce(jnp.maximum, [jnp.max(x, axis=1, keepdims=True) for x in scores])
        shifted = [jnp.exp(x - top) for x in scores]
        total = sum(jnp.sum(x, axis=1, keepdims=True) for x in shifted)
        context = sum(dot(x.astype(bf16), kv[s][:, HD:], 1, 0) for s, x in enumerate(shifted))
        low = (context / total).astype(bf16)
        each_out[0][...] = low
        each_out[1][...] = top + jnp.log(total)
        add_back(acc, low, weights, 3 * HD, 4 * HD)

        @pl.when(z == heads - 1)
        def _():
            spread(whole_out, acc)

    out = run(
        body,
        heads,
        [queries] + list(both) + list(planes) + [slopes],
        [key_pos, query_pos],
        [shape((heads, length, HD), bf16), shape((heads, length, 1), f32)],
        [shape((rows, width), bf16)] * n_t,
        [pltpu.VMEM((length, width), f32)],
        2 * heads * length * (2 * HD * length * n + HD * width),
    )
    return out[0], out[1], out[2:]


def attend_back(blocks, queries, both, planes, context, logs, slopes, key_pos, query_pos):
    heads, length, _ = queries.shape
    n = len(planes)
    width = blocks[0].shape[1]

    def body(z, each_in, whole_in, each_out, whole_out, scratch):
        @pl.when(z == 0)
        def _():
            lay(scratch[0], whole_in[2:])

        kv, weights = each_in[1 : 1 + n], each_in[1 + n : 1 + 2 * n]
        context_ref, logs_ref, slope_ref = each_in[1 + 2 * n :]
        slope = slope_ref[:, :1]
        low_queries = each_in[0][...]
        grads = times(scratch[0], weights, 3 * HD, 4 * HD).astype(bf16)
        inner = jnp.sum(grads.astype(f32) * context_ref[...].astype(f32), axis=1, keepdims=True)
        query_grad = None
        for s in range(n):
            scores = masked_scores(low_queries, kv[s], slope, whole_in[0][s], whole_in[1][...])
            probs = jnp.exp(scores - logs_ref[...])
            prob_grad = dot(grads, kv[s][:, HD:], 1, 1)
            score_grad = (probs * (prob_grad - inner)).astype(bf16)
            term = dot(score_grad, kv[s][:, :HD], 1, 0)
            query_grad = term if query_grad is None else query_grad + term
            each_out[1 + s][:, :HD] = dot(score_grad, low_queries, 0, 0).astype(bf16)
            each_out[1 + s][:, HD:] = dot(probs.astype(bf16), grads, 0, 0).astype(bf16)
        each_out[0][...] = (query_grad * (1.0 / math.sqrt(HD))).astype(bf16)

    out = run(
        body,
        heads,
        [queries] + list(both) + list(planes) + [context, logs, slopes],
        [key_pos, query_pos] + list(blocks),
        [shape((heads, length, HD), bf16)] + [shape((heads, length, 2 * HD), bf16)] * n,
        [],
        [pltpu.VMEM((length, width), bf16)],
        2 * heads * length * (5 * HD * length * n + HD * width),
    )
    return out[0], out[1:]


def project_back(query_grad, both_grads, planes, n_t, width):
    heads, length, _ = query_grad.shape
    n = len(planes)
    rows = length // n_t

    def body(z, each_in, whole_in, each_out, whole_out, scratch):
        acc = scratch[0]

        @pl.when(z == 0)
        def _():
            acc[...] = jnp.zeros_like(acc)

        low = sum(item[...].astype(f32) for item in each_in[1 : 1 + n]).astype(bf16)
        joined, sums = each_out
        joined[:, :HD] = each_in[0][...]
        joined[:, HD:] = low
        sums[:, :HD] = jnp.sum(each_in[0][...].astype(f32), axis=0, keepdims=True)
        sums[:, HD:] = jnp.sum(low.astype(f32), axis=0, keepdims=True)
        add_back(acc, joined[...], each_in[1 + n :], 0, 3 * HD)

        @pl.when(z == heads - 1)
        def _():
            spread(whole_out, acc)

    out = run(
        body,
        heads,
        [query_grad] + list(both_grads) + list(planes),
        [],
        [shape((heads, length, 3 * HD), bf16), shape((heads, 1, 3 * HD), f32)],
        [shape((rows, width), bf16)] * n_t,
        [pltpu.VMEM((length, width), f32)],
        2 * heads * length * width * 3 * HD,
    )
    return out[0], out[1], out[2:]


def feed_forward(blocks, planes, bias):
    rows, width = blocks[0].shape
    length = rows * len(blocks)
    heads, _, units = bias.shape
    n = len(planes)

    def body(z, each_in, whole_in, each_out, whole_out, scratch):
        wide, acc = scratch

        @pl.when(z == 0)
        def _():
            lay(wide, whole_in)
            acc[...] = jnp.zeros_like(acc)

        pre_up = times(wide, each_in[:n], 0, units) + each_in[n][...]
        each_out[0][...] = pre_up
        low = gelu_tanh(pre_up).astype(bf16)
        each_out[1][...] = low
        add_back(acc, low, each_in[:n], units, 2 * units)

        @pl.when(z == heads - 1)
        def _():
            spread(whole_out, acc)

    out = run(
        body,
        heads,
        list(planes) + [bias],
        blocks,
        [shape((heads, length, units), f32), shape((heads, length, units), bf16)],
        [shape((rows, width), bf16)] * len(blocks),
        [pltpu.VMEM((length, width), bf16), pltpu.VMEM((length, width), f32)],
        4 * heads * length * width * units,
    )
    return out[0], out[1], out[2:]


def feed_back(blocks, planes, pre_up):
    rows, width = blocks[0].shape
    length = rows * len(blocks)
    heads, _, units = pre_up.shape
    n = len(planes)

    def body(z, each_in, whole_in, each_out, whole_out, scratch):
        wide, acc = scratch

        @pl.when(z == 0)
        def _():
            lay(wide, whole_in)
            acc[...] = jnp.zeros_like(acc)

        act_grad = times(wide, each_in[:n], units, 2 * units)
        low = (act_grad * gelu_slope(each_in[n][...])).astype(bf16)
        each_out[0][...] = low
        each_out[1][...] = jnp.sum(low.astype(f32), axis=0, keepdims=True)
        add_back(acc, low, each_in[:n], 0, units)

        @pl.when(z == heads - 1)
        def _():
            spread(whole_out, acc)

    out = run(
        body,
        heads,
        list(planes) + [pre_up],
        blocks,
        [shape((heads, length, units), bf16), shape((heads, 1, units), f32)],
        [shape((rows, width), bf16)] * len(blocks),
        [pltpu.VMEM((length, width), bf16), pltpu.VMEM((length, width), f32)],
        4 * heads * length * width * units,
    )
    return out[0], out[1], out[2:]


def weight_back(one_blocks, one, two_blocks, two, n):
    rows, width = one_blocks[0].shape
    length = rows * len(one_blocks)
    heads, _, first = one[0].shape
    second = two[0].shape[2]
    part = width // n
    half = len(one_blocks)

    def summed(wide, cols, items):
        total, begin = None, 0
        for item in items:
            end = begin + item.shape[0]
            term = dot(wide[begin:end, cols], item[...], 0, 0)
            total = term if total is None else total + term
            begin = end
        return total.astype(bf16)

    def body(z, each_in, whole_in, each_out, whole_out, scratch):
        @pl.when(z == 0)
        def _():
            lay(scratch[0], whole_in[:half])
            lay(scratch[1], whole_in[half:])

        for s in range(n):
            cols = slice(s * part, (s + 1) * part)
            each_out[s][:, :first] = summed(scratch[0], cols, each_in[: len(one)])
            each_out[s][:, first:] = summed(scratch[1], cols, each_in[len(one) :])

    return run(
        body,
        heads,
        list(one) + list(two),
        list(one_blocks) + list(two_blocks),
        [shape((heads, part, first + second), bf16)] * n,
        [],
        [pltpu.VMEM((length, width), bf16)] * 2,
        2 * heads * length * width * (first + second),
    )


def norm_forward(values, got, vectors, bias, gain, shift):
    def body(z, each_in, whole_in, each_out, whole_out, scratch):
        start, rows = whole_in[:2]
        total = start[...] + rows[bias : bias + 1, :]
        for item in whole_in[2:]:
            total = total + item[...].astype(f32)
        whole_out[0][...] = total
        xhat, _ = norm_parts(total)
        normed = xhat * rows[gain : gain + 1, :] + rows[shift : shift + 1, :]
        whole_out[1][...] = normed.astype(bf16)

    shapes = [shape(values.shape, f32), shape(values.shape, bf16)]
    return run(body, 1, [], [values, vectors] + list(got), [], shapes)


def norm_back(values, gradient, got, vectors, gain):
    width = values.shape[1]

    def body(z, each_in, whole_in, each_out, whole_out, scratch):
        e = sum(item[...].astype(f32) for item in whole_in[3:])
        xhat, scale = norm_parts(whole_in[0][...])
        eg = e * whole_in[2][gain : gain + 1, :]
        back = scale * (
            eg
            - jnp.mean(eg, axis=-1, keepdims=True)
            - xhat * jnp.mean(eg * xhat, axis=-1, keepdims=True)
        )
        fresh = whole_in[1][...].astype(f32) + back
        whole_out[0][...] = fresh
        whole_out[1][...] = fresh.astype(bf16)
        whole_out[2][0:1, :] = jnp.sum(e * xhat, axis=0, keepdims=True)
        whole_out[2][1:2, :] = jnp.sum(e, axis=0, keepdims=True)
        whole_out[2][2:3, :] = jnp.sum(fresh, axis=0, keepdims=True)

    shapes = [shape(values.shape, f32), shape(values.shape, bf16), shape((3, width), f32)]
    return run(body, 1, [], [values, gradient, vectors] + list(got), [], shapes)


def turn_columns(array, turn, counts, inward):
    n_t, n_s = counts
    cut = array.shape[1] // (n_t * n_s)
    parts = [array[:, j * cut : (j + 1) * cut] for j in range(n_t * n_s)]
    index = turn[:, :cut]
    if inward:
        groups = flip_list([parts[s::n_s] for s in range(n_s)], index)
        return [part for group in groups for part in group]
    groups = flip_list([parts[k * n_t : (k + 1) * n_t] for k in range(n_s)], index)
    return [groups[s][t] for t in range(n_t) for s in range(n_s)]


def store_columns(target, parts):
    cut = parts[0].shape[1]
    for j, part in enumerate(parts):
        target[:, j * cut : (j + 1) * cut] = part.astype(target.dtype)


def first_norm(items, turn, counts):
    dims = items[0].shape

    def body(z, each_in, whole_in, each_out, whole_out, scratch):
        total = sum(item[...].astype(f32) for item in whole_in[1:])
        store_columns(whole_out[0], turn_columns(total, whole_in[0][...], counts, True))
        whole_out[1][...] = norm_parts(whole_out[0][...])[0].astype(bf16)

    return run(body, 1, [], [turn] + list(items), [], [shape(dims, f32), shape(dims, bf16)])


def turned_sum(items, turn, counts, inward, bias=None):
    dims = items[0].shape

    def body(z, each_in, whole_in, each_out, whole_out, scratch):
        count = len(whole_in) - (0 if bias is None else 1)
        total = sum(item[...].astype(f32) for item in whole_in[1:count])
        if bias is not None:
            total = total + whole_in[count][bias : bias + 1, :]
        store_columns(whole_out[0], turn_columns(total, whole_in[0][...], counts, inward))

    return run(body, 1, [], [turn] + list(items), [], [shape(dims, bf16)])[0]


def unpack(planes, turn, counts, width, layers, spare):
    n_t, n_s = counts
    heads, _, columns = planes[0].shape
    part, cut = width // n_s, width // (n_s * n_t)
    small = HD // (n_t * n_s)
    units = columns
    unit = units // (n_t * n_s)
    half = columns // 2

    def kernel(*refs):
        ex, index, outs = refs[:n_s], refs[n_s], refs[n_s + 1 :]
        vectors, qkv, up = outs[0], outs[1 : 1 + layers], outs[1 + layers :]
        for layer in range(layers):
            qkv[layer][...] = jnp.zeros_like(qkv[layer])
        for t in range(n_t):
            rows = slice(t * spare, (t + 1) * spare)
            for k in range(n_s):
                place = (k * n_t + t) * cut
                vectors[:, place : place + cut] = ex[k][0, rows, :cut].astype(f32)
            for head in range(heads):
                blocks = [ex[k][head, rows, half:].astype(f32) for k in range(n_s)]
                blocks = flip_list(blocks, index[:, :half])
                for s in range(n_s):
                    place = t * n_s + s
                    for layer in range(layers):
                        row = blocks[s][layer : layer + 1, :]
                        at = place * small
                        qkv[layer][head, :, at : at + small] = row[:, :small]
                        at += 2 * HD
                        qkv[layer][head, :, at : at + small] = row[:, small : 2 * small]
                        at = place * unit
                        up[layer][head, :, at : at + unit] = row[:, 2 * small : 2 * small + unit]

    block = pl.BlockSpec((heads, n_t * spare, columns), lambda i: (0, part // (n_t * spare), 0))
    shapes = [shape((spare, width), f32)]
    shapes += [shape((heads, 1, 3 * HD), f32)] * layers
    shapes += [shape((heads, 1, units), f32)] * layers

    def whole(dims):
        return pl.BlockSpec(dims, lambda i: (0,) * len(dims))

    out = pl.pallas_call(
        kernel,
        grid=(1,),
        in_specs=[block] * n_s + [whole(turn.shape)],
        out_specs=[whole(item.shape) for item in shapes],
        out_shape=shapes,
        compiler_params=pltpu.CompilerParams(vmem_limit_bytes=VMEM_LIMIT),
    )(*planes, turn)
    return out[0], out[1 : 1 + layers], out[1 + layers :]


def per_device(
    sizes,
    tokens,
    qkv_weight,
    dense_weight,
    up_weight,
    down_weight,
    first_gain,
    first_shift,
    query_bias,
    value_bias,
    dense_bias,
    second_gain,
    second_shift,
    up_bias,
    down_bias,
    cotangent,
):
    n_t, n_s, n_z = sizes
    seq_count, slice_len, width = tokens.shape
    assert seq_count == 1 and n_t == n_z
    d, c, z = (lax.axis_index(name) for name in (DP, SEQ, HEAD))
    rows = slice_len // n_t
    cut = qkv_weight.shape[1]
    part = cut * n_t
    heads = query_bias.shape[1]
    assert heads == n_t
    units = up_bias.shape[2] * n_t * n_s

    def spread_rows(array):
        return exchange(array.reshape(n_t, rows, width), DP)

    def own_rows(blocks):
        return lax.dynamic_index_in_dim(blocks, z, 0, False)

    def send_rows(array):
        return gather(array, DP, n_t)

    def in_halves(blocks):
        return [blocks]

    def send_sums(blocks):
        return deal(blocks, DP, n_t)

    def to_planes_of(array):
        return lax.all_gather(array, HEAD, axis=0, tiled=False)

    def send_output(planes):
        return exchange(planes, DP).reshape(1, slice_len, width)

    def packed_mixed(layer):
        qkv = qkv_weight[layer].reshape(cut, n_t, -1).transpose(1, 0, 2)
        dense = dense_weight[layer].reshape(n_t, -1, cut).transpose(0, 2, 1)
        return jnp.concatenate((qkv, dense), axis=2)

    def packed_feed(layer):
        up = up_weight[layer].reshape(cut, n_t, -1).transpose(1, 0, 2)
        down = down_weight[layer].reshape(n_t, -1, cut).transpose(0, 2, 1)
        return jnp.concatenate((up, down), axis=2)

    def to_planes(blocks):
        return exchange(blocks, DP).reshape(part, -1)

    def join(planes):
        return gather(planes, SEQ, n_s)

    counts = (n_t, n_s)
    turn = jnp.full((1, 128), c, jnp.int32)
    wide = jnp.concatenate(
        (first_gain, first_shift, dense_bias, second_gain, second_shift, down_bias), axis=0
    )
    tall = jnp.concatenate((query_bias, value_bias, up_bias), axis=2).transpose(1, 0, 2)
    columns, spare = 4 * HD, 16
    half = columns // 2
    wide = jnp.pad(wide, ((0, spare - 6 * LAYERS), (0, half - cut)))
    tall = jnp.pad(tall, ((0, 0), (0, spare - LAYERS), (0, half - tall.shape[2])))
    small = jnp.concatenate((jnp.broadcast_to(wide[None], (n_t, spare, half)), tall), axis=2)
    first = jnp.concatenate((packed_mixed(0), small.astype(bf16)), axis=1)
    feed_rows = jnp.pad(packed_feed(0), ((0, 0), (0, spare), (0, 0)))
    first = exchange(jnp.concatenate((first, feed_rows), axis=2), DP)
    second_shard = first[:, :cut, columns:].reshape(part, -1)
    first = first[:, :, :columns]
    first_shard = jnp.concatenate(
        (first[:, :cut].reshape(part, columns), first[:, cut:].reshape(-1, columns)), axis=0
    )
    messages = [to_planes_of(first_shard)]
    hidden, low = first_norm([own_rows(spread_rows(tokens[0]))], turn, counts)
    normed_one = send_rows(low)
    normed_one, second_shard = meet(normed_one, second_shard)
    messages.append(to_planes_of(second_shard))
    messages[0], normed_one = meet(messages[0], normed_one)
    mixed = join(messages[0])
    vectors, biases_qkv, biases_up = unpack(mixed, turn, counts, width, LAYERS, spare)
    tall_sizes = (HD, HD, units)

    def vector(kind, layer):
        return kind * LAYERS + layer

    qkv_columns = 3 * HD
    head_ids = jnp.arange(n_z, dtype=jnp.int32) * heads + d
    slopes = 2.0 ** (-8.0 * (head_ids + 1).astype(f32) / H)
    slopes = jnp.broadcast_to(slopes[:, None, None], (n_z, 1, 128))
    block_ids = (d ^ jnp.arange(n_t, dtype=jnp.int32)) * rows
    own_pos = (block_ids[:, None] + jnp.arange(rows, dtype=jnp.int32)[None]).reshape(-1)
    query_pos = (c * slice_len + own_pos).astype(f32)[:, None]
    others = (c ^ jnp.arange(n_s, dtype=jnp.int32)) * slice_len
    key_pos = (others[:, None] + own_pos[None]).astype(f32)[:, None, :]
    cot = cotangent[0]
    records = []
    for layer in range(LAYERS):
        if layer > 0:
            normed_one = send_rows(low)
            normed_one, messages[2 * layer] = meet(normed_one, messages[2 * layer])
            mixed = join(messages[2 * layer])
        affine = (vectors, vector(0, 0), vector(1, 0)) if layer == 0 else ()
        queries, both, normed_one = project(normed_one, mixed, biases_qkv[layer], *affine)
        both = gather(both, SEQ, n_s)
        if layer == 0:
            later = jnp.concatenate((packed_mixed(1), packed_feed(1)), axis=2)
            both, later = meet(both, later)
            later = to_planes(later)
        else:
            both, cot_rows = meet(both, cot_rows)
            cot_rows = send_rows(cot_rows)
        context, logs, out = attend(queries, both, mixed, slopes, key_pos, query_pos, n_t, width)
        if layer == 0:
            out, later = meet(out, later)
        else:
            out, cot_rows = meet(out, cot_rows)
        got = send_sums(out)
        got, messages[2 * layer + 1] = meet(got, messages[2 * layer + 1])
        feed = join(messages[2 * layer + 1])
        if layer == 0:
            got, later = meet(got, later)
            messages.append(to_planes_of(later[:, :columns]))
            messages.append(to_planes_of(later[:, columns:]))
        hidden_mid, low = norm_forward(
            hidden, got, vectors, vector(2, layer), vector(3, layer), vector(4, layer)
        )
        normed_two = send_rows(low)
        if layer == 0:
            normed_two, cot_rows = meet(normed_two, cot)
            cot_rows = spread_rows(cot_rows)
        halves = [feed_forward(part, feed, biases_up[layer]) for part in in_halves(normed_two)]
        pre_up, activation, out = (list(item) for item in zip(*halves))
        out = [block for part in out for block in part]
        got = send_sums(out)
        if layer == 0:
            got, cot_rows = meet(got, turned_sum([own_rows(cot_rows)], turn, counts, True))
        records.append(
            (
                (mixed, feed),
                (hidden, hidden_mid, normed_one, normed_two),
                (queries, both, logs, context, pre_up, activation),
            )
        )
        if layer + 1 < LAYERS:
            hidden, low = norm_forward(
                hidden_mid,
                got,
                vectors,
                vector(5, layer),
                vector(0, layer + 1),
                vector(1, layer + 1),
            )

    last_bias = vector(5, LAYERS - 1)
    output_low = turned_sum([hidden_mid] + list(got) + [vectors], turn, counts, False, last_bias)

    gradient = cot_rows[0]
    grad_low = cot_rows
    down_bias_grad = jnp.sum(gradient, axis=0, keepdims=True, dtype=f32)
    wide_grads = [None] * LAYERS
    tall_grads = [None] * LAYERS

    def core_sum(blocks):
        return sum_blocks(blocks, SEQ, n_s).astype(bf16)

    def head_sum(mine):
        return lax.psum_scatter(mine, HEAD, scatter_dimension=0, tiled=False)

    def send_shares(mine):
        return exchange(mine.reshape(n_t, cut, -1), DP)

    feed_shares = [None] * LAYERS
    mixed_shares = [None] * LAYERS
    feed_sums = [None] * LAYERS
    mixed_sums = [None] * LAYERS
    for layer in reversed(range(LAYERS)):
        (
            (mixed, feed),
            (hidden, hidden_mid, normed_one, normed_two),
            (queries, both, logs, context, pre_up, activation),
        ) = records[layer]
        last = layer == LAYERS - 1
        halves = [
            feed_back(part, feed, kept) for part, kept in zip(in_halves(grad_low), pre_up)
        ]
        pre_grad, up_bias_grad, out = (list(item) for item in zip(*halves))
        got = send_sums([block for part in out for block in part])
        up_bias_grad = functools.reduce(jnp.add, up_bias_grad)
        feed_grad = weight_back(normed_two, pre_grad, grad_low, activation, n_s)
        if last:
            got, feed_grad, output_low = meet(got, feed_grad, output_low)
            output_planes = to_planes_of(output_low)
        else:
            got, feed_grad, mixed_sums[1] = meet(got, feed_grad, mixed_sums[1])
        mid_grad, low, sums_two = norm_back(
            hidden_mid, gradient, got, vectors, vector(3, layer)
        )
        mid_low = send_rows(low)
        if last:
            mid_low, mine = meet(mid_low, core_sum(feed_grad))
        else:
            mid_low, mine, output_planes = meet(mid_low, core_sum(feed_grad), output_planes)
        feed_sums[layer] = head_sum(mine)
        query_grad, both_grads = attend_back(
            mid_low, queries, both, mixed, context, logs, slopes, key_pos, query_pos
        )
        if not last:
            both_grads, output = meet(both_grads, send_output(output_planes))
        got = deal(both_grads, SEQ, n_s)
        joined, qkv_sums, out = project_back(query_grad, got, mixed, n_t, width)
        got = send_sums(out)
        mixed_grad = weight_back(normed_one, [joined], mid_low, [context], n_s)
        if last:
            got, mixed_grad, output_planes = meet(got, mixed_grad, output_planes)
        else:
            got, feed_sums[0] = meet(got, feed_sums[0])
            mixed_sums[layer] = head_sum(core_sum(mixed_grad))
        gradient, low, sums_one = norm_back(
            hidden, mid_grad, got, vectors, vector(0, layer)
        )
        if layer > 0:
            grad_low, mine, feed_sums[layer] = meet(
                send_rows(low), core_sum(mixed_grad), feed_sums[layer]
            )
            mixed_sums[layer] = head_sum(mine)
        wide_grads[layer] = jnp.stack(
            (
                sums_one[0],
                sums_one[1],
                sums_two[2],
                sums_two[0],
                sums_two[1],
                down_bias_grad[0],
            )
        )
        down_bias_grad = sums_one[2:3]
        tall_grads[layer] = jnp.concatenate(
            (qkv_sums[:, 0, :HD], qkv_sums[:, 0, 2 * HD :], up_bias_grad[:, 0]), axis=1
        )

    low_outer = turned_sum([low], turn, counts, False)
    low_outer, mixed_sums[1], feed_sums[1] = meet(low_outer, mixed_sums[1], feed_sums[1])
    feed_shares[1] = send_shares(feed_sums[1])
    mixed_shares[1] = send_shares(mixed_sums[1])
    low_outer, mixed_sums[0], feed_shares[1], mixed_shares[1] = meet(
        low_outer, mixed_sums[0], feed_shares[1], mixed_shares[1]
    )
    tokens_planes = to_planes_of(low_outer)
    mixed_sums[0], feed_sums[0] = meet(mixed_sums[0], feed_sums[0])
    feed_shares[0] = send_shares(feed_sums[0])
    mixed_shares[0] = send_shares(mixed_sums[0])
    tokens_planes, feed_shares[0], mixed_shares[0] = meet(
        tokens_planes, feed_shares[0], mixed_shares[0]
    )
    tokens_grad = send_output(tokens_planes).astype(f32)

    def fold(arrays, name, size):
        total = arrays[0]
        for step in range(1, size):
            total = total + swap(arrays[step], name, size, step)
        return total

    wide = jnp.stack(wide_grads).reshape(LAYERS * 6, n_s, n_t, cut)
    pieces, begin = [], 0
    tall = jnp.stack(tall_grads)
    for size in tall_sizes:
        piece = tall[:, :, begin : begin + size]
        begin += size
        piece = piece.reshape(LAYERS, n_z, n_t, n_s, size // (n_t * n_s))
        pieces.append(flip(flip(piece, c, 3), z, 1))
    tall = jnp.concatenate(
        [piece.transpose(3, 1, 2, 0, 4).reshape(n_s, n_z, n_t, -1) for piece in pieces], axis=3
    )
    wide = wide.transpose(1, 2, 0, 3).reshape(n_s, n_t, -1)
    n_wide = wide.shape[2]
    wide = jnp.broadcast_to(wide[:, None], (n_s, n_z) + wide.shape[1:])
    joint = jnp.concatenate((wide, tall), axis=3)
    joint = fold([joint[step] for step in range(n_s)], SEQ, n_s)
    joint = fold([joint[step] for step in range(n_z)], HEAD, n_z)
    joint = flip(joint, d)
    got = deal([joint[step] for step in range(n_t)], DP, n_t)
    wide = functools.reduce(jnp.add, [item[:n_wide] for item in got])
    wide = wide.reshape(LAYERS, 6, cut)
    tall = flip(jnp.stack([item[n_wide:] for item in got]), d)
    outs, begin = [], 0
    for size in tall_sizes:
        size = size // (n_t * n_s)
        piece = tall[:, begin : begin + LAYERS * size].reshape(n_t, LAYERS, size)
        begin += LAYERS * size
        outs.append(piece.transpose(1, 0, 2))
    query_bias_grad, value_bias_grad, up_bias_grad = outs
    def rows_first(shares, begin, end):
        parts = [share[:, :, begin:end].transpose(1, 0, 2).reshape(cut, -1) for share in shares]
        return jnp.stack(parts).astype(f32)

    def columns_first(shares, begin, end):
        parts = [share[:, :, begin:end].transpose(0, 2, 1).reshape(-1, cut) for share in shares]
        return jnp.stack(parts).astype(f32)

    qkv_grad = rows_first(mixed_shares, 0, qkv_columns)
    dense_grad = columns_first(mixed_shares, qkv_columns, columns)
    up_grad = rows_first(feed_shares, 0, units)
    down_grad = columns_first(feed_shares, units, 2 * units)
    return (
        output,
        tokens_grad,
        qkv_grad,
        dense_grad,
        up_grad,
        down_grad,
        wide[:, 0],
        wide[:, 1],
        query_bias_grad,
        value_bias_grad,
        wide[:, 2],
        wide[:, 3],
        wide[:, 4],
        up_bias_grad,
        wide[:, 5],
    )


def solution(mesh):
    sizes = tuple(mesh.shape[name] for name in (DP, SEQ, HEAD))
    rows = P(DP, SEQ, None)
    tall = P(None, (DP, SEQ), HEAD)
    flat = P(None, HEAD, (DP, SEQ))
    vector = P(None, (DP, SEQ))
    params = (
        tall,
        flat,
        tall,
        flat,
        vector,
        vector,
        flat,
        flat,
        vector,
        vector,
        vector,
        flat,
        vector,
    )
    return jax.shard_map(
        functools.partial(per_device, sizes),
        mesh=mesh,
        in_specs=(rows,) + params + (rows,),
        out_specs=(rows, rows) + params,
        check_vma=False,
    )
```

```python
import functools
import math

import jax
import jax.numpy as jnp
from jax import lax
from jax.experimental import pallas as pl
from jax.experimental.pallas import tpu as pltpu
from jax.sharding import PartitionSpec as P

H = 16
HD = 64
LAYERS = 2
DP, SEQ, HEAD = "dp", "seq", "head"

epsilon = 1e-05
masked_value = -1000000000.0
VMEM_LIMIT = 60 * 1024 * 1024
SMALL_LIMIT = 16 * 1024 * 1024
bf16 = jnp.bfloat16
f32 = jnp.float32


def flip_list(blocks, index):
    bit = 1
    while bit < len(blocks):
        turn = (index & bit) != 0
        blocks = [
            jax.tree.map(lambda x, y: jnp.where(turn, x, y), blocks[j ^ bit], blocks[j])
            for j in range(len(blocks))
        ]
        bit *= 2
    return blocks


def flip(array, index, axis=0):
    blocks = [lax.index_in_dim(array, j, axis, keepdims=True) for j in range(array.shape[axis])]
    return jnp.concatenate(flip_list(blocks, index), axis=axis)


def swap(array, name, size, step):
    return lax.ppermute(array, name, [(i, i ^ step) for i in range(size)])


def gather(array, name, size):
    return [array] + [swap(array, name, size, step) for step in range(1, size)]


def deal(blocks, name, size):
    return [blocks[0]] + [swap(blocks[step], name, size, step) for step in range(1, size)]


def exchange(array, name):
    return lax.all_to_all(array, name, 0, 0, tiled=True)


def meet(*groups):
    return lax.optimization_barrier(groups)


def add_all(blocks):
    return functools.reduce(jnp.add, [block.astype(f32) for block in blocks])


def sum_blocks(blocks, name, size):
    total = blocks[0].astype(f32)
    for step in range(1, size):
        total = total + swap(blocks[step].astype(bf16), name, size, step).astype(f32)
    return total


def after(array, *others):
    return lax.optimization_barrier((array,) + others)[0]


def dot(left, right, left_dim, right_dim):
    dims = (((left_dim,), (right_dim,)), ((), ()))
    return lax.dot_general(left, right, dims, preferred_element_type=f32)


def gelu_tanh(values):
    argument = 0.7978845608028654 * (values + 0.044715 * values * values * values)
    return 0.5 * values * (1.0 + jnp.tanh(argument))


def gelu_slope(values):
    square = values * values
    bent = jnp.tanh(0.7978845608028654 * (values + 0.044715 * values * square))
    inner = 0.7978845608028654 * (1.0 + 3.0 * 0.044715 * square)
    return 0.5 * (1.0 + bent) + 0.5 * values * (1.0 - bent * bent) * inner


def norm_parts(values):
    row_mean = jnp.mean(values, axis=-1, keepdims=True)
    centred = values - row_mean
    scale = lax.rsqrt(jnp.mean(centred * centred, axis=-1, keepdims=True) + epsilon)
    return centred * scale, scale


def run(body, steps, each_in, whole_in, each_out, whole_out, scratch=(), flops=0):
    def each(array):
        zeros = (0,) * (len(array.shape) - 1)
        return pl.BlockSpec((None,) + tuple(array.shape[1:]), lambda z: (z,) + zeros)

    def whole(array):
        zeros = (0,) * len(array.shape)
        return pl.BlockSpec(tuple(array.shape), lambda z: zeros)

    counts = [len(part) for part in (each_in, whole_in, each_out, whole_out)]

    def kernel(*refs):
        parts, begin = [], 0
        for count in counts:
            parts.append(refs[begin : begin + count])
            begin += count
        body(pl.program_id(0), *parts, refs[begin:])

    arrays = list(each_in) + list(whole_in)
    shapes = list(each_out) + list(whole_out)
    moved = sum(math.prod(item.shape) * item.dtype.itemsize for item in arrays + shapes)
    return pl.pallas_call(
        kernel,
        grid=(steps,),
        in_specs=[each(item) for item in each_in] + [whole(item) for item in whole_in],
        out_specs=[each(item) for item in each_out] + [whole(item) for item in whole_out],
        out_shape=shapes,
        scratch_shapes=list(scratch),
        compiler_params=pltpu.CompilerParams(vmem_limit_bytes=VMEM_LIMIT if steps > 1 else SMALL_LIMIT),
        cost_estimate=pl.CostEstimate(flops=flops, bytes_accessed=moved, transcendentals=0),
    )(*arrays)


def shape(dims, kind):
    return jax.ShapeDtypeStruct(tuple(dims), kind)


def lay(target, blocks):
    rows = blocks[0].shape[0]
    for index, block in enumerate(blocks):
        target[index * rows : (index + 1) * rows, :] = block[...]


def spread(blocks, source):
    rows = blocks[0].shape[0]
    for index, block in enumerate(blocks):
        block[...] = source[index * rows : (index + 1) * rows, :].astype(block.dtype)


def times(array, planes, begin, end):
    part = array.shape[1] // len(planes)
    total = None
    for s, plane in enumerate(planes):
        term = dot(array[:, s * part : (s + 1) * part], plane[:part, begin:end], 1, 0)
        total = term if total is None else total + term
    return total


def add_back(acc, array, planes, begin, end):
    part = acc.shape[1] // len(planes)
    for s, plane in enumerate(planes):
        acc[:, s * part : (s + 1) * part] += dot(array, plane[:part, begin:end], 1, 1)


def project(blocks, planes, bias, vectors=None, gain=None, shift=None):
    rows, width = blocks[0].shape
    length = rows * len(blocks)
    heads = planes[0].shape[0]
    n, n_blocks = len(planes), len(blocks)
    vectors = [] if gain is None else [vectors]

    def body(z, each_in, whole_in, each_out, whole_out, scratch):
        wide = scratch[0]

        @pl.when(z == 0)
        def _():
            lay(wide, whole_in[:n_blocks])
            if vectors:
                lines = whole_in[n_blocks]
                normed = wide[...].astype(f32) * lines[gain : gain + 1, :]
                normed = normed + lines[shift : shift + 1, :]
                wide[...] = normed.astype(bf16)
                spread(whole_out, wide)

        got = times(wide, each_in[:n], 0, 3 * HD) + each_in[n][...]
        low = got.astype(bf16)
        each_out[0][...] = low[:, :HD] * jnp.asarray(1.0 / math.sqrt(HD), bf16)
        each_out[1][...] = low[:, HD:]

    out = run(
        body,
        heads,
        list(planes) + [bias],
        list(blocks) + vectors,
        [shape((heads, length, HD), bf16), shape((heads, length, 2 * HD), bf16)],
        [shape((rows, width), bf16)] * n_blocks if vectors else [],
        [pltpu.VMEM((length, width), bf16)],
        2 * heads * length * width * 3 * HD,
    )
    return out[0], out[1], out[2:] or blocks


def masked_scores(queries, both, slope, key_pos, query_pos):
    scores = dot(queries, both[:, :HD], 1, 1) + slope * key_pos
    return jnp.where(key_pos <= query_pos, scores, masked_value)


def attend(queries, both, planes, slopes, key_pos, query_pos, n_t, width):
    heads, length, _ = queries.shape
    n = len(planes)
    rows = length // n_t

    def body(z, each_in, whole_in, each_out, whole_out, scratch):
        kv, weights = each_in[1 : 1 + n], each_in[1 + n : 1 + 2 * n]
        slope = each_in[1 + 2 * n][:, :1]
        acc = scratch[0]

        @pl.when(z == 0)
        def _():
            acc[...] = jnp.zeros_like(acc)

        low_queries = each_in[0][...]
        scores = [
            masked_scores(low_queries, kv[s], slope, whole_in[0][s], whole_in[1][...])
            for s in range(n)
        ]
        top = functools.reduce(jnp.maximum, [jnp.max(x, axis=1, keepdims=True) for x in scores])
        shifted = [jnp.exp(x - top) for x in scores]
        total = sum(jnp.sum(x, axis=1, keepdims=True) for x in shifted)
        context = sum(dot(x.astype(bf16), kv[s][:, HD:], 1, 0) for s, x in enumerate(shifted))
        low = (context / total).astype(bf16)
        each_out[0][...] = low
        each_out[1][...] = top + jnp.log(total)
        add_back(acc, low, weights, 3 * HD, 4 * HD)

        @pl.when(z == heads - 1)
        def _():
            spread(whole_out, acc)

    out = run(
        body,
        heads,
        [queries] + list(both) + list(planes) + [slopes],
        [key_pos, query_pos],
        [shape((heads, length, HD), bf16), shape((heads, length, 1), f32)],
        [shape((rows, width), bf16)] * n_t,
        [pltpu.VMEM((length, width), f32)],
        2 * heads * length * (2 * HD * length * n + HD * width),
    )
    return out[0], out[1], out[2:]


def attend_back(blocks, queries, both, planes, context, logs, slopes, key_pos, query_pos):
    heads, length, _ = queries.shape
    n = len(planes)
    width = blocks[0].shape[1]

    def body(z, each_in, whole_in, each_out, whole_out, scratch):
        @pl.when(z == 0)
        def _():
            lay(scratch[0], whole_in[2:])

        kv, weights = each_in[1 : 1 + n], each_in[1 + n : 1 + 2 * n]
        context_ref, logs_ref, slope_ref = each_in[1 + 2 * n :]
        slope = slope_ref[:, :1]
        low_queries = each_in[0][...]
        grads = times(scratch[0], weights, 3 * HD, 4 * HD).astype(bf16)
        inner = jnp.sum(grads.astype(f32) * context_ref[...].astype(f32), axis=1, keepdims=True)
        query_grad = None
        for s in range(n):
            scores = masked_scores(low_queries, kv[s], slope, whole_in[0][s], whole_in[1][...])
            probs = jnp.exp(scores - logs_ref[...])
            prob_grad = dot(grads, kv[s][:, HD:], 1, 1)
            score_grad = (probs * (prob_grad - inner)).astype(bf16)
            term = dot(score_grad, kv[s][:, :HD], 1, 0)
            query_grad = term if query_grad is None else query_grad + term
            each_out[1 + s][:, :HD] = dot(score_grad, low_queries, 0, 0).astype(bf16)
            each_out[1 + s][:, HD:] = dot(probs.astype(bf16), grads, 0, 0).astype(bf16)
        each_out[0][...] = (query_grad * (1.0 / math.sqrt(HD))).astype(bf16)

    out = run(
        body,
        heads,
        [queries] + list(both) + list(planes) + [context, logs, slopes],
        [key_pos, query_pos] + list(blocks),
        [shape((heads, length, HD), bf16)] + [shape((heads, length, 2 * HD), bf16)] * n,
        [],
        [pltpu.VMEM((length, width), bf16)],
        2 * heads * length * (5 * HD * length * n + HD * width),
    )
    return out[0], out[1:]


def project_back(query_grad, both_grads, planes, n_t, width):
    heads, length, _ = query_grad.shape
    n = len(planes)
    rows = length // n_t

    def body(z, each_in, whole_in, each_out, whole_out, scratch):
        acc = scratch[0]

        @pl.when(z == 0)
        def _():
            acc[...] = jnp.zeros_like(acc)

        low = sum(item[...].astype(f32) for item in each_in[1 : 1 + n]).astype(bf16)
        joined, sums = each_out
        joined[:, :HD] = each_in[0][...]
        joined[:, HD:] = low
        sums[:, :HD] = jnp.sum(each_in[0][...].astype(f32), axis=0, keepdims=True)
        sums[:, HD:] = jnp.sum(low.astype(f32), axis=0, keepdims=True)
        add_back(acc, joined[...], each_in[1 + n :], 0, 3 * HD)

        @pl.when(z == heads - 1)
        def _():
            spread(whole_out, acc)

    out = run(
        body,
        heads,
        [query_grad] + list(both_grads) + list(planes),
        [],
        [shape((heads, length, 3 * HD), bf16), shape((heads, 1, 3 * HD), f32)],
        [shape((rows, width), bf16)] * n_t,
        [pltpu.VMEM((length, width), f32)],
        2 * heads * length * width * 3 * HD,
    )
    return out[0], out[1], out[2:]


def feed_forward(blocks, planes, bias):
    rows, width = blocks[0].shape
    length = rows * len(blocks)
    heads, _, units = bias.shape
    n = len(planes)

    def body(z, each_in, whole_in, each_out, whole_out, scratch):
        wide, acc = scratch

        @pl.when(z == 0)
        def _():
            lay(wide, whole_in)
            acc[...] = jnp.zeros_like(acc)

        pre_up = times(wide, each_in[:n], 0, units) + each_in[n][...]
        each_out[0][...] = pre_up
        low = gelu_tanh(pre_up).astype(bf16)
        each_out[1][...] = low
        add_back(acc, low, each_in[:n], units, 2 * units)

        @pl.when(z == heads - 1)
        def _():
            spread(whole_out, acc)

    out = run(
        body,
        heads,
        list(planes) + [bias],
        blocks,
        [shape((heads, length, units), f32), shape((heads, length, units), bf16)],
        [shape((rows, width), bf16)] * len(blocks),
        [pltpu.VMEM((length, width), bf16), pltpu.VMEM((length, width), f32)],
        4 * heads * length * width * units,
    )
    return out[0], out[1], out[2:]


def feed_back(blocks, planes, pre_up):
    rows, width = blocks[0].shape
    length = rows * len(blocks)
    heads, _, units = pre_up.shape
    n = len(planes)

    def body(z, each_in, whole_in, each_out, whole_out, scratch):
        wide, acc = scratch

        @pl.when(z == 0)
        def _():
            lay(wide, whole_in)
            acc[...] = jnp.zeros_like(acc)

        act_grad = times(wide, each_in[:n], units, 2 * units)
        low = (act_grad * gelu_slope(each_in[n][...])).astype(bf16)
        each_out[0][...] = low
        each_out[1][...] = jnp.sum(low.astype(f32), axis=0, keepdims=True)
        add_back(acc, low, each_in[:n], 0, units)

        @pl.when(z == heads - 1)
        def _():
            spread(whole_out, acc)

    out = run(
        body,
        heads,
        list(planes) + [pre_up],
        blocks,
        [shape((heads, length, units), bf16), shape((heads, 1, units), f32)],
        [shape((rows, width), bf16)] * len(blocks),
        [pltpu.VMEM((length, width), bf16), pltpu.VMEM((length, width), f32)],
        4 * heads * length * width * units,
    )
    return out[0], out[1], out[2:]


def weight_back(one_blocks, one, two_blocks, two, n):
    rows, width = one_blocks[0].shape
    length = rows * len(one_blocks)
    heads, _, first = one[0].shape
    second = two[0].shape[2]
    part = width // n
    half = len(one_blocks)

    def summed(wide, cols, items):
        total, begin = None, 0
        for item in items:
            end = begin + item.shape[0]
            term = dot(wide[begin:end, cols], item[...], 0, 0)
            total = term if total is None else total + term
            begin = end
        return total.astype(bf16)

    def body(z, each_in, whole_in, each_out, whole_out, scratch):
        @pl.when(z == 0)
        def _():
            lay(scratch[0], whole_in[:half])
            lay(scratch[1], whole_in[half:])

        for s in range(n):
            cols = slice(s * part, (s + 1) * part)
            each_out[s][:, :first] = summed(scratch[0], cols, each_in[: len(one)])
            each_out[s][:, first:] = summed(scratch[1], cols, each_in[len(one) :])

    return run(
        body,
        heads,
        list(one) + list(two),
        list(one_blocks) + list(two_blocks),
        [shape((heads, part, first + second), bf16)] * n,
        [],
        [pltpu.VMEM((length, width), bf16)] * 2,
        2 * heads * length * width * (first + second),
    )


def norm_forward(values, got, vectors, bias, gain, shift):
    def body(z, each_in, whole_in, each_out, whole_out, scratch):
        start, rows = whole_in[:2]
        total = start[...] + rows[bias : bias + 1, :]
        for item in whole_in[2:]:
            total = total + item[...].astype(f32)
        whole_out[0][...] = total
        xhat, _ = norm_parts(total)
        normed = xhat * rows[gain : gain + 1, :] + rows[shift : shift + 1, :]
        whole_out[1][...] = normed.astype(bf16)

    shapes = [shape(values.shape, f32), shape(values.shape, bf16)]
    return run(body, 1, [], [values, vectors] + list(got), [], shapes)


def norm_back(values, gradient, got, vectors, gain):
    width = values.shape[1]

    def body(z, each_in, whole_in, each_out, whole_out, scratch):
        e = sum(item[...].astype(f32) for item in whole_in[3:])
        xhat, scale = norm_parts(whole_in[0][...])
        eg = e * whole_in[2][gain : gain + 1, :]
        back = scale * (
            eg
            - jnp.mean(eg, axis=-1, keepdims=True)
            - xhat * jnp.mean(eg * xhat, axis=-1, keepdims=True)
        )
        fresh = whole_in[1][...].astype(f32) + back
        whole_out[0][...] = fresh
        whole_out[1][...] = fresh.astype(bf16)
        whole_out[2][0:1, :] = jnp.sum(e * xhat, axis=0, keepdims=True)
        whole_out[2][1:2, :] = jnp.sum(e, axis=0, keepdims=True)
        whole_out[2][2:3, :] = jnp.sum(fresh, axis=0, keepdims=True)

    shapes = [shape(values.shape, f32), shape(values.shape, bf16), shape((3, width), f32)]
    return run(body, 1, [], [values, gradient, vectors] + list(got), [], shapes)


def turn_columns(array, turn, counts, inward):
    n_t, n_s = counts
    cut = array.shape[1] // (n_t * n_s)
    parts = [array[:, j * cut : (j + 1) * cut] for j in range(n_t * n_s)]
    index = turn[:, :cut]
    if inward:
        groups = flip_list([parts[s::n_s] for s in range(n_s)], index)
        return [part for group in groups for part in group]
    groups = flip_list([parts[k * n_t : (k + 1) * n_t] for k in range(n_s)], index)
    return [groups[s][t] for t in range(n_t) for s in range(n_s)]


def store_columns(target, parts):
    cut = parts[0].shape[1]
    for j, part in enumerate(parts):
        target[:, j * cut : (j + 1) * cut] = part.astype(target.dtype)


def first_norm(items, turn, counts):
    dims = items[0].shape

    def body(z, each_in, whole_in, each_out, whole_out, scratch):
        total = sum(item[...].astype(f32) for item in whole_in[1:])
        store_columns(whole_out[0], turn_columns(total, whole_in[0][...], counts, True))
        whole_out[1][...] = norm_parts(whole_out[0][...])[0].astype(bf16)

    return run(body, 1, [], [turn] + list(items), [], [shape(dims, f32), shape(dims, bf16)])


def turned_sum(items, turn, counts, inward, bias=None):
    dims = items[0].shape

    def body(z, each_in, whole_in, each_out, whole_out, scratch):
        count = len(whole_in) - (0 if bias is None else 1)
        total = sum(item[...].astype(f32) for item in whole_in[1:count])
        if bias is not None:
            total = total + whole_in[count][bias : bias + 1, :]
        store_columns(whole_out[0], turn_columns(total, whole_in[0][...], counts, inward))

    return run(body, 1, [], [turn] + list(items), [], [shape(dims, bf16)])[0]


def unpack(planes, turn, counts, width, layers, spare):
    n_t, n_s = counts
    heads, _, columns = planes[0].shape
    part, cut = width // n_s, width // (n_s * n_t)
    small = HD // (n_t * n_s)
    units = columns
    unit = units // (n_t * n_s)
    half = columns // 2

    def kernel(*refs):
        ex, index, outs = refs[:n_s], refs[n_s], refs[n_s + 1 :]
        vectors, qkv, up = outs[0], outs[1 : 1 + layers], outs[1 + layers :]
        for layer in range(layers):
            qkv[layer][...] = jnp.zeros_like(qkv[layer])
        for t in range(n_t):
            rows = slice(t * spare, (t + 1) * spare)
            for k in range(n_s):
                place = (k * n_t + t) * cut
                vectors[:, place : place + cut] = ex[k][0, rows, :cut].astype(f32)
            for head in range(heads):
                blocks = [ex[k][head, rows, half:].astype(f32) for k in range(n_s)]
                blocks = flip_list(blocks, index[:, :half])
                for s in range(n_s):
                    place = t * n_s + s
                    for layer in range(layers):
                        row = blocks[s][layer : layer + 1, :]
                        at = place * small
                        qkv[layer][head, :, at : at + small] = row[:, :small]
                        at += 2 * HD
                        qkv[layer][head, :, at : at + small] = row[:, small : 2 * small]
                        at = place * unit
                        up[layer][head, :, at : at + unit] = row[:, 2 * small : 2 * small + unit]

    block = pl.BlockSpec((heads, n_t * spare, columns), lambda i: (0, part // (n_t * spare), 0))
    shapes = [shape((spare, width), f32)]
    shapes += [shape((heads, 1, 3 * HD), f32)] * layers
    shapes += [shape((heads, 1, units), f32)] * layers

    def whole(dims):
        return pl.BlockSpec(dims, lambda i: (0,) * len(dims))

    out = pl.pallas_call(
        kernel,
        grid=(1,),
        in_specs=[block] * n_s + [whole(turn.shape)],
        out_specs=[whole(item.shape) for item in shapes],
        out_shape=shapes,
        compiler_params=pltpu.CompilerParams(vmem_limit_bytes=VMEM_LIMIT),
    )(*planes, turn)
    return out[0], out[1 : 1 + layers], out[1 + layers :]


def per_device(
    sizes,
    tokens,
    qkv_weight,
    dense_weight,
    up_weight,
    down_weight,
    first_gain,
    first_shift,
    query_bias,
    value_bias,
    dense_bias,
    second_gain,
    second_shift,
    up_bias,
    down_bias,
    cotangent,
):
    n_t, n_s, n_z = sizes
    seq_count, slice_len, width = tokens.shape
    assert seq_count == 1 and n_t == n_z
    d, c, z = (lax.axis_index(name) for name in (DP, SEQ, HEAD))
    rows = slice_len // n_t
    cut = qkv_weight.shape[1]
    part = cut * n_t
    heads = query_bias.shape[1]
    assert heads == n_t
    units = up_bias.shape[2] * n_t * n_s

    def spread_rows(array):
        return exchange(array.reshape(n_t, rows, width), DP)

    def own_rows(blocks):
        return lax.dynamic_index_in_dim(blocks, z, 0, False)

    def send_rows(array):
        return gather(array, DP, n_t)

    def in_halves(blocks):
        return [blocks]

    def send_sums(blocks):
        return deal(blocks, DP, n_t)

    def to_planes_of(array):
        return lax.all_gather(array, HEAD, axis=0, tiled=False)

    def send_output(planes):
        return exchange(planes, DP).reshape(1, slice_len, width)

    def packed_mixed(layer):
        qkv = qkv_weight[layer].reshape(cut, n_t, -1).transpose(1, 0, 2)
        dense = dense_weight[layer].reshape(n_t, -1, cut).transpose(0, 2, 1)
        return jnp.concatenate((qkv, dense), axis=2)

    def packed_feed(layer):
        up = up_weight[layer].reshape(cut, n_t, -1).transpose(1, 0, 2)
        down = down_weight[layer].reshape(n_t, -1, cut).transpose(0, 2, 1)
        return jnp.concatenate((up, down), axis=2)

    def to_planes(blocks):
        return exchange(blocks, DP).reshape(part, -1)

    def join(planes):
        return gather(planes, SEQ, n_s)

    counts = (n_t, n_s)
    turn = jnp.full((1, 128), c, jnp.int32)
    wide = jnp.concatenate(
        (first_gain, first_shift, dense_bias, second_gain, second_shift, down_bias), axis=0
    )
    tall = jnp.concatenate((query_bias, value_bias, up_bias), axis=2).transpose(1, 0, 2)
    columns, spare = 4 * HD, 16
    half = columns // 2
    wide = jnp.pad(wide, ((0, spare - 6 * LAYERS), (0, half - cut)))
    tall = jnp.pad(tall, ((0, 0), (0, spare - LAYERS), (0, half - tall.shape[2])))
    small = jnp.concatenate((jnp.broadcast_to(wide[None], (n_t, spare, half)), tall), axis=2)
    first = jnp.concatenate((packed_mixed(0), small.astype(bf16)), axis=1)
    feed_rows = jnp.pad(packed_feed(0), ((0, 0), (0, spare), (0, 0)))
    first = exchange(jnp.concatenate((first, feed_rows), axis=2), DP)
    second_shard = first[:, :cut, columns:].reshape(part, -1)
    first = first[:, :, :columns]
    first_shard = jnp.concatenate(
        (first[:, :cut].reshape(part, columns), first[:, cut:].reshape(-1, columns)), axis=0
    )
    messages = [to_planes_of(first_shard)]
    hidden, low = first_norm([own_rows(spread_rows(tokens[0]))], turn, counts)
    normed_one = send_rows(low)
    normed_one, second_shard = meet(normed_one, second_shard)
    messages.append(to_planes_of(second_shard))
    messages[0], normed_one = meet(messages[0], normed_one)
    mixed = join(messages[0])
    vectors, biases_qkv, biases_up = unpack(mixed, turn, counts, width, LAYERS, spare)
    tall_sizes = (HD, HD, units)

    def vector(kind, layer):
        return kind * LAYERS + layer

    qkv_columns = 3 * HD
    head_ids = jnp.arange(n_z, dtype=jnp.int32) * heads + d
    slopes = 2.0 ** (-8.0 * (head_ids + 1).astype(f32) / H)
    slopes = jnp.broadcast_to(slopes[:, None, None], (n_z, 1, 128))
    block_ids = (d ^ jnp.arange(n_t, dtype=jnp.int32)) * rows
    own_pos = (block_ids[:, None] + jnp.arange(rows, dtype=jnp.int32)[None]).reshape(-1)
    query_pos = (c * slice_len + own_pos).astype(f32)[:, None]
    others = (c ^ jnp.arange(n_s, dtype=jnp.int32)) * slice_len
    key_pos = (others[:, None] + own_pos[None]).astype(f32)[:, None, :]
    cot = cotangent[0]
    records = []
    for layer in range(LAYERS):
        if layer > 0:
            normed_one = send_rows(low)
            normed_one, messages[2 * layer] = meet(normed_one, messages[2 * layer])
            mixed = join(messages[2 * layer])
        affine = (vectors, vector(0, 0), vector(1, 0)) if layer == 0 else ()
        queries, both, normed_one = project(normed_one, mixed, biases_qkv[layer], *affine)
        both = gather(both, SEQ, n_s)
        if layer == 0:
            later = jnp.concatenate((packed_mixed(1), packed_feed(1)), axis=2)
            both, later = meet(both, later)
            later = to_planes(later)
        else:
            both, cot_rows = meet(both, cot_rows)
            cot_rows = send_rows(cot_rows)
        context, logs, out = attend(queries, both, mixed, slopes, key_pos, query_pos, n_t, width)
        if layer == 0:
            out, later = meet(out, later)
        else:
            out, cot_rows = meet(out, cot_rows)
        got = send_sums(out)
        got, messages[2 * layer + 1] = meet(got, messages[2 * layer + 1])
        feed = join(messages[2 * layer + 1])
        if layer == 0:
            got, later = meet(got, later)
            messages.append(to_planes_of(later[:, :columns]))
            messages.append(to_planes_of(later[:, columns:]))
        hidden_mid, low = norm_forward(
            hidden, got, vectors, vector(2, layer), vector(3, layer), vector(4, layer)
        )
        normed_two = send_rows(low)
        if layer == 0:
            normed_two, cot_rows = meet(normed_two, cot)
            cot_rows = spread_rows(cot_rows)
        halves = [feed_forward(part, feed, biases_up[layer]) for part in in_halves(normed_two)]
        pre_up, activation, out = (list(item) for item in zip(*halves))
        out = [block for part in out for block in part]
        got = send_sums(out)
        if layer == 0:
            got, cot_rows = meet(got, turned_sum([own_rows(cot_rows)], turn, counts, True))
        records.append(
            (
                (mixed, feed),
                (hidden, hidden_mid, normed_one, normed_two),
                (queries, both, logs, context, pre_up, activation),
            )
        )
        if layer + 1 < LAYERS:
            hidden, low = norm_forward(
                hidden_mid,
                got,
                vectors,
                vector(5, layer),
                vector(0, layer + 1),
                vector(1, layer + 1),
            )

    last_bias = vector(5, LAYERS - 1)
    output_low = turned_sum([hidden_mid] + list(got) + [vectors], turn, counts, False, last_bias)

    gradient = cot_rows[0]
    grad_low = cot_rows
    down_bias_grad = jnp.sum(gradient, axis=0, keepdims=True, dtype=f32)
    wide_grads = [None] * LAYERS
    tall_grads = [None] * LAYERS

    def core_sum(blocks):
        return sum_blocks(blocks, SEQ, n_s).astype(bf16)

    def head_sum(mine):
        return lax.psum_scatter(mine, HEAD, scatter_dimension=0, tiled=False)

    def send_shares(mine):
        return exchange(mine.reshape(n_t, cut, -1), DP)

    feed_shares = [None] * LAYERS
    mixed_shares = [None] * LAYERS
    feed_sums = [None] * LAYERS
    mixed_sums = [None] * LAYERS
    for layer in reversed(range(LAYERS)):
        (
            (mixed, feed),
            (hidden, hidden_mid, normed_one, normed_two),
            (queries, both, logs, context, pre_up, activation),
        ) = records[layer]
        last = layer == LAYERS - 1
        halves = [
            feed_back(part, feed, kept) for part, kept in zip(in_halves(grad_low), pre_up)
        ]
        pre_grad, up_bias_grad, out = (list(item) for item in zip(*halves))
        got = send_sums([block for part in out for block in part])
        up_bias_grad = functools.reduce(jnp.add, up_bias_grad)
        feed_grad = weight_back(normed_two, pre_grad, grad_low, activation, n_s)
        if last:
            got, feed_grad, output_low = meet(got, feed_grad, output_low)
            output_planes = to_planes_of(output_low)
        else:
            got, feed_grad, mixed_sums[1] = meet(got, feed_grad, mixed_sums[1])
        mid_grad, low, sums_two = norm_back(
            hidden_mid, gradient, got, vectors, vector(3, layer)
        )
        mid_low = send_rows(low)
        if last:
            mid_low, mine = meet(mid_low, core_sum(feed_grad))
        else:
            mid_low, mine, output_planes = meet(mid_low, core_sum(feed_grad), output_planes)
        feed_sums[layer] = head_sum(mine)
        query_grad, both_grads = attend_back(
            mid_low, queries, both, mixed, context, logs, slopes, key_pos, query_pos
        )
        if not last:
            both_grads, output = meet(both_grads, send_output(output_planes))
        got = deal(both_grads, SEQ, n_s)
        joined, qkv_sums, out = project_back(query_grad, got, mixed, n_t, width)
        got = send_sums(out)
        mixed_grad = weight_back(normed_one, [joined], mid_low, [context], n_s)
        if last:
            got, mixed_grad, output_planes = meet(got, mixed_grad, output_planes)
        else:
            got, feed_sums[0] = meet(got, feed_sums[0])
            mixed_sums[layer] = head_sum(core_sum(mixed_grad))
        gradient, low, sums_one = norm_back(
            hidden, mid_grad, got, vectors, vector(0, layer)
        )
        if layer > 0:
            grad_low, mine, feed_sums[layer] = meet(
                send_rows(low), core_sum(mixed_grad), feed_sums[layer]
            )
            mixed_sums[layer] = head_sum(mine)
        wide_grads[layer] = jnp.stack(
            (
                sums_one[0],
                sums_one[1],
                sums_two[2],
                sums_two[0],
                sums_two[1],
                down_bias_grad[0],
            )
        )
        down_bias_grad = sums_one[2:3]
        tall_grads[layer] = jnp.concatenate(
            (qkv_sums[:, 0, :HD], qkv_sums[:, 0, 2 * HD :], up_bias_grad[:, 0]), axis=1
        )

    low_outer = turned_sum([low], turn, counts, False)
    low_outer, mixed_sums[1], feed_sums[1] = meet(low_outer, mixed_sums[1], feed_sums[1])
    feed_shares[1] = send_shares(feed_sums[1])
    mixed_shares[1] = send_shares(mixed_sums[1])
    low_outer, mixed_sums[0], feed_shares[1], mixed_shares[1] = meet(
        low_outer, mixed_sums[0], feed_shares[1], mixed_shares[1]
    )
    tokens_planes = to_planes_of(low_outer)
    mixed_sums[0], feed_sums[0] = meet(mixed_sums[0], feed_sums[0])
    feed_shares[0] = send_shares(feed_sums[0])
    mixed_shares[0] = send_shares(mixed_sums[0])
    tokens_planes, feed_shares[0], mixed_shares[0] = meet(
        tokens_planes, feed_shares[0], mixed_shares[0]
    )
    tokens_grad = send_output(tokens_planes).astype(f32)

    def fold(arrays, name, size):
        total = arrays[0]
        for step in range(1, size):
            total = total + swap(arrays[step], name, size, step)
        return total

    wide = jnp.stack(wide_grads).reshape(LAYERS * 6, n_s, n_t, cut)
    pieces, begin = [], 0
    tall = jnp.stack(tall_grads)
    for size in tall_sizes:
        piece = tall[:, :, begin : begin + size]
        begin += size
        piece = piece.reshape(LAYERS, n_z, n_t, n_s, size // (n_t * n_s))
        pieces.append(flip(flip(piece, c, 3), z, 1))
    tall = jnp.concatenate(
        [piece.transpose(3, 1, 2, 0, 4).reshape(n_s, n_z, n_t, -1) for piece in pieces], axis=3
    )
    wide = wide.transpose(1, 2, 0, 3).reshape(n_s, n_t, -1)
    n_wide = wide.shape[2]
    wide = jnp.broadcast_to(wide[:, None], (n_s, n_z) + wide.shape[1:])
    joint = jnp.concatenate((wide, tall), axis=3)
    joint = fold([joint[step] for step in range(n_s)], SEQ, n_s)
    joint = fold([joint[step] for step in range(n_z)], HEAD, n_z)
    joint = flip(joint, d)
    got = deal([joint[step] for step in range(n_t)], DP, n_t)
    wide = functools.reduce(jnp.add, [item[:n_wide] for item in got])
    wide = wide.reshape(LAYERS, 6, cut)
    tall = flip(jnp.stack([item[n_wide:] for item in got]), d)
    outs, begin = [], 0
    for size in tall_sizes:
        size = size // (n_t * n_s)
        piece = tall[:, begin : begin + LAYERS * size].reshape(n_t, LAYERS, size)
        begin += LAYERS * size
        outs.append(piece.transpose(1, 0, 2))
    query_bias_grad, value_bias_grad, up_bias_grad = outs
    def rows_first(shares, begin, end):
        parts = [share[:, :, begin:end].transpose(1, 0, 2).reshape(cut, -1) for share in shares]
        return jnp.stack(parts).astype(f32)

    def columns_first(shares, begin, end):
        parts = [share[:, :, begin:end].transpose(0, 2, 1).reshape(-1, cut) for share in shares]
        return jnp.stack(parts).astype(f32)

    qkv_grad = rows_first(mixed_shares, 0, qkv_columns)
    dense_grad = columns_first(mixed_shares, qkv_columns, columns)
    up_grad = rows_first(feed_shares, 0, units)
    down_grad = columns_first(feed_shares, units, 2 * units)
    return (
        output,
        tokens_grad,
        qkv_grad,
        dense_grad,
        up_grad,
        down_grad,
        wide[:, 0],
        wide[:, 1],
        query_bias_grad,
        value_bias_grad,
        wide[:, 2],
        wide[:, 3],
        wide[:, 4],
        up_bias_grad,
        wide[:, 5],
    )


def solution(mesh):
    sizes = tuple(mesh.shape[name] for name in (DP, SEQ, HEAD))
    rows = P(DP, SEQ, None)
    tall = P(None, (DP, SEQ), HEAD)
    flat = P(None, HEAD, (DP, SEQ))
    vector = P(None, (DP, SEQ))
    params = (
        tall,
        flat,
        tall,
        flat,
        vector,
        vector,
        flat,
        flat,
        vector,
        vector,
        vector,
        flat,
        vector,
    )
    return jax.shard_map(
        functools.partial(per_device, sizes),
        mesh=mesh,
        in_specs=(rows,) + params + (rows,),
        out_specs=(rows, rows) + params,
        check_vma=False,
    )
```

```python
import functools
import math

import jax
import jax.numpy as jnp
from jax import lax
from jax.experimental import pallas as pl
from jax.experimental.pallas import tpu as pltpu
from jax.sharding import PartitionSpec as P

H = 16
HD = 64
LAYERS = 2
DP, SEQ, HEAD = "dp", "seq", "head"

epsilon = 1e-05
masked_value = -1000000000.0
VMEM_LIMIT = 60 * 1024 * 1024
SMALL_LIMIT = 16 * 1024 * 1024
bf16 = jnp.bfloat16
f32 = jnp.float32


def flip_list(blocks, index):
    bit = 1
    while bit < len(blocks):
        turn = (index & bit) != 0
        blocks = [
            jax.tree.map(lambda x, y: jnp.where(turn, x, y), blocks[j ^ bit], blocks[j])
            for j in range(len(blocks))
        ]
        bit *= 2
    return blocks


def flip(array, index, axis=0):
    blocks = [lax.index_in_dim(array, j, axis, keepdims=True) for j in range(array.shape[axis])]
    return jnp.concatenate(flip_list(blocks, index), axis=axis)


def swap(array, name, size, step):
    return lax.ppermute(array, name, [(i, i ^ step) for i in range(size)])


def gather(array, name, size):
    return [array] + [swap(array, name, size, step) for step in range(1, size)]


def deal(blocks, name, size):
    return [blocks[0]] + [swap(blocks[step], name, size, step) for step in range(1, size)]


def exchange(array, name):
    return lax.all_to_all(array, name, 0, 0, tiled=True)


def meet(*groups):
    return lax.optimization_barrier(groups)


def add_all(blocks):
    return functools.reduce(jnp.add, [block.astype(f32) for block in blocks])


def sum_blocks(blocks, name, size):
    total = blocks[0].astype(f32)
    for step in range(1, size):
        total = total + swap(blocks[step].astype(bf16), name, size, step).astype(f32)
    return total


def after(array, *others):
    return lax.optimization_barrier((array,) + others)[0]


def dot(left, right, left_dim, right_dim):
    dims = (((left_dim,), (right_dim,)), ((), ()))
    return lax.dot_general(left, right, dims, preferred_element_type=f32)


def gelu_tanh(values):
    argument = 0.7978845608028654 * (values + 0.044715 * values * values * values)
    return 0.5 * values * (1.0 + jnp.tanh(argument))


def gelu_slope(values):
    square = values * values
    bent = jnp.tanh(0.7978845608028654 * (values + 0.044715 * values * square))
    inner = 0.7978845608028654 * (1.0 + 3.0 * 0.044715 * square)
    return 0.5 * (1.0 + bent) + 0.5 * values * (1.0 - bent * bent) * inner


def norm_parts(values):
    row_mean = jnp.mean(values, axis=-1, keepdims=True)
    centred = values - row_mean
    scale = lax.rsqrt(jnp.mean(centred * centred, axis=-1, keepdims=True) + epsilon)
    return centred * scale, scale


def run(body, steps, each_in, whole_in, each_out, whole_out, scratch=(), flops=0):
    def each(array):
        zeros = (0,) * (len(array.shape) - 1)
        return pl.BlockSpec((None,) + tuple(array.shape[1:]), lambda z: (z,) + zeros)

    def whole(array):
        zeros = (0,) * len(array.shape)
        return pl.BlockSpec(tuple(array.shape), lambda z: zeros)

    counts = [len(part) for part in (each_in, whole_in, each_out, whole_out)]

    def kernel(*refs):
        parts, begin = [], 0
        for count in counts:
            parts.append(refs[begin : begin + count])
            begin += count
        body(pl.program_id(0), *parts, refs[begin:])

    arrays = list(each_in) + list(whole_in)
    shapes = list(each_out) + list(whole_out)
    moved = sum(math.prod(item.shape) * item.dtype.itemsize for item in arrays + shapes)
    return pl.pallas_call(
        kernel,
        grid=(steps,),
        in_specs=[each(item) for item in each_in] + [whole(item) for item in whole_in],
        out_specs=[each(item) for item in each_out] + [whole(item) for item in whole_out],
        out_shape=shapes,
        scratch_shapes=list(scratch),
        compiler_params=pltpu.CompilerParams(vmem_limit_bytes=VMEM_LIMIT if steps > 1 else SMALL_LIMIT),
        cost_estimate=pl.CostEstimate(flops=flops, bytes_accessed=moved, transcendentals=0),
    )(*arrays)


def shape(dims, kind):
    return jax.ShapeDtypeStruct(tuple(dims), kind)


def lay(target, blocks):
    rows = blocks[0].shape[0]
    for index, block in enumerate(blocks):
        target[index * rows : (index + 1) * rows, :] = block[...]


def spread(blocks, source):
    rows = blocks[0].shape[0]
    for index, block in enumerate(blocks):
        block[...] = source[index * rows : (index + 1) * rows, :].astype(block.dtype)


def times(array, planes, begin, end):
    part = array.shape[1] // len(planes)
    total = None
    for s, plane in enumerate(planes):
        term = dot(array[:, s * part : (s + 1) * part], plane[:part, begin:end], 1, 0)
        total = term if total is None else total + term
    return total


def add_back(acc, array, planes, begin, end):
    part = acc.shape[1] // len(planes)
    for s, plane in enumerate(planes):
        acc[:, s * part : (s + 1) * part] += dot(array, plane[:part, begin:end], 1, 1)


def project(blocks, planes, bias, vectors=None, gain=None, shift=None):
    rows, width = blocks[0].shape
    length = rows * len(blocks)
    heads = planes[0].shape[0]
    n, n_blocks = len(planes), len(blocks)
    vectors = [] if gain is None else [vectors]

    def body(z, each_in, whole_in, each_out, whole_out, scratch):
        wide = scratch[0]

        @pl.when(z == 0)
        def _():
            lay(wide, whole_in[:n_blocks])
            if vectors:
                lines = whole_in[n_blocks]
                normed = wide[...].astype(f32) * lines[gain : gain + 1, :]
                normed = normed + lines[shift : shift + 1, :]
                wide[...] = normed.astype(bf16)
                spread(whole_out, wide)

        got = times(wide, each_in[:n], 0, 3 * HD) + each_in[n][...]
        low = got.astype(bf16)
        each_out[0][...] = low[:, :HD] * jnp.asarray(1.0 / math.sqrt(HD), bf16)
        each_out[1][...] = low[:, HD:]

    out = run(
        body,
        heads,
        list(planes) + [bias],
        list(blocks) + vectors,
        [shape((heads, length, HD), bf16), shape((heads, length, 2 * HD), bf16)],
        [shape((rows, width), bf16)] * n_blocks if vectors else [],
        [pltpu.VMEM((length, width), bf16)],
        2 * heads * length * width * 3 * HD,
    )
    return out[0], out[1], out[2:] or blocks


def masked_scores(queries, both, slope, key_pos, query_pos):
    scores = dot(queries, both[:, :HD], 1, 1) + slope * key_pos
    return jnp.where(key_pos <= query_pos, scores, masked_value)


def attend(queries, both, planes, slopes, key_pos, query_pos, n_t, width):
    heads, length, _ = queries.shape
    n = len(planes)
    rows = length // n_t

    def body(z, each_in, whole_in, each_out, whole_out, scratch):
        kv, weights = each_in[1 : 1 + n], each_in[1 + n : 1 + 2 * n]
        slope = each_in[1 + 2 * n][:, :1]
        acc = scratch[0]

        @pl.when(z == 0)
        def _():
            acc[...] = jnp.zeros_like(acc)

        low_queries = each_in[0][...]
        scores = [
            masked_scores(low_queries, kv[s], slope, whole_in[0][s], whole_in[1][...])
            for s in range(n)
        ]
        top = functools.reduce(jnp.maximum, [jnp.max(x, axis=1, keepdims=True) for x in scores])
        shifted = [jnp.exp(x - top) for x in scores]
        total = sum(jnp.sum(x, axis=1, keepdims=True) for x in shifted)
        context = sum(dot(x.astype(bf16), kv[s][:, HD:], 1, 0) for s, x in enumerate(shifted))
        low = (context / total).astype(bf16)
        each_out[0][...] = low
        each_out[1][...] = top + jnp.log(total)
        add_back(acc, low, weights, 3 * HD, 4 * HD)

        @pl.when(z == heads - 1)
        def _():
            spread(whole_out, acc)

    out = run(
        body,
        heads,
        [queries] + list(both) + list(planes) + [slopes],
        [key_pos, query_pos],
        [shape((heads, length, HD), bf16), shape((heads, length, 1), f32)],
        [shape((rows, width), bf16)] * n_t,
        [pltpu.VMEM((length, width), f32)],
        2 * heads * length * (2 * HD * length * n + HD * width),
    )
    return out[0], out[1], out[2:]


def attend_back(blocks, queries, both, planes, context, logs, slopes, key_pos, query_pos):
    heads, length, _ = queries.shape
    n = len(planes)
    width = blocks[0].shape[1]

    def body(z, each_in, whole_in, each_out, whole_out, scratch):
        @pl.when(z == 0)
        def _():
            lay(scratch[0], whole_in[2:])

        kv, weights = each_in[1 : 1 + n], each_in[1 + n : 1 + 2 * n]
        context_ref, logs_ref, slope_ref = each_in[1 + 2 * n :]
        slope = slope_ref[:, :1]
        low_queries = each_in[0][...]
        grads = times(scratch[0], weights, 3 * HD, 4 * HD).astype(bf16)
        inner = jnp.sum(grads.astype(f32) * context_ref[...].astype(f32), axis=1, keepdims=True)
        query_grad = None
        for s in range(n):
            scores = masked_scores(low_queries, kv[s], slope, whole_in[0][s], whole_in[1][...])
            probs = jnp.exp(scores - logs_ref[...])
            prob_grad = dot(grads, kv[s][:, HD:], 1, 1)
            score_grad = (probs * (prob_grad - inner)).astype(bf16)
            term = dot(score_grad, kv[s][:, :HD], 1, 0)
            query_grad = term if query_grad is None else query_grad + term
            each_out[1 + s][:, :HD] = dot(score_grad, low_queries, 0, 0).astype(bf16)
            each_out[1 + s][:, HD:] = dot(probs.astype(bf16), grads, 0, 0).astype(bf16)
        each_out[0][...] = (query_grad * (1.0 / math.sqrt(HD))).astype(bf16)

    out = run(
        body,
        heads,
        [queries] + list(both) + list(planes) + [context, logs, slopes],
        [key_pos, query_pos] + list(blocks),
        [shape((heads, length, HD), bf16)] + [shape((heads, length, 2 * HD), bf16)] * n,
        [],
        [pltpu.VMEM((length, width), bf16)],
        2 * heads * length * (5 * HD * length * n + HD * width),
    )
    return out[0], out[1:]


def project_back(query_grad, both_grads, planes, n_t, width):
    heads, length, _ = query_grad.shape
    n = len(planes)
    rows = length // n_t

    def body(z, each_in, whole_in, each_out, whole_out, scratch):
        acc = scratch[0]

        @pl.when(z == 0)
        def _():
            acc[...] = jnp.zeros_like(acc)

        low = sum(item[...].astype(f32) for item in each_in[1 : 1 + n]).astype(bf16)
        joined, sums = each_out
        joined[:, :HD] = each_in[0][...]
        joined[:, HD:] = low
        sums[:, :HD] = jnp.sum(each_in[0][...].astype(f32), axis=0, keepdims=True)
        sums[:, HD:] = jnp.sum(low.astype(f32), axis=0, keepdims=True)
        add_back(acc, joined[...], each_in[1 + n :], 0, 3 * HD)

        @pl.when(z == heads - 1)
        def _():
            spread(whole_out, acc)

    out = run(
        body,
        heads,
        [query_grad] + list(both_grads) + list(planes),
        [],
        [shape((heads, length, 3 * HD), bf16), shape((heads, 1, 3 * HD), f32)],
        [shape((rows, width), bf16)] * n_t,
        [pltpu.VMEM((length, width), f32)],
        2 * heads * length * width * 3 * HD,
    )
    return out[0], out[1], out[2:]


def feed_forward(blocks, planes, bias):
    rows, width = blocks[0].shape
    length = rows * len(blocks)
    heads, _, units = bias.shape
    n = len(planes)

    def body(z, each_in, whole_in, each_out, whole_out, scratch):
        wide, acc = scratch

        @pl.when(z == 0)
        def _():
            lay(wide, whole_in)
            acc[...] = jnp.zeros_like(acc)

        pre_up = times(wide, each_in[:n], 0, units) + each_in[n][...]
        each_out[0][...] = pre_up
        low = gelu_tanh(pre_up).astype(bf16)
        each_out[1][...] = low
        add_back(acc, low, each_in[:n], units, 2 * units)

        @pl.when(z == heads - 1)
        def _():
            spread(whole_out, acc)

    out = run(
        body,
        heads,
        list(planes) + [bias],
        blocks,
        [shape((heads, length, units), f32), shape((heads, length, units), bf16)],
        [shape((rows, width), bf16)] * len(blocks),
        [pltpu.VMEM((length, width), bf16), pltpu.VMEM((length, width), f32)],
        4 * heads * length * width * units,
    )
    return out[0], out[1], out[2:]


def feed_back(blocks, planes, pre_up):
    rows, width = blocks[0].shape
    length = rows * len(blocks)
    heads, _, units = pre_up.shape
    n = len(planes)

    def body(z, each_in, whole_in, each_out, whole_out, scratch):
        wide, acc = scratch

        @pl.when(z == 0)
        def _():
            lay(wide, whole_in)
            acc[...] = jnp.zeros_like(acc)

        act_grad = times(wide, each_in[:n], units, 2 * units)
        low = (act_grad * gelu_slope(each_in[n][...])).astype(bf16)
        each_out[0][...] = low
        each_out[1][...] = jnp.sum(low.astype(f32), axis=0, keepdims=True)
        add_back(acc, low, each_in[:n], 0, units)

        @pl.when(z == heads - 1)
        def _():
            spread(whole_out, acc)

    out = run(
        body,
        heads,
        list(planes) + [pre_up],
        blocks,
        [shape((heads, length, units), bf16), shape((heads, 1, units), f32)],
        [shape((rows, width), bf16)] * len(blocks),
        [pltpu.VMEM((length, width), bf16), pltpu.VMEM((length, width), f32)],
        4 * heads * length * width * units,
    )
    return out[0], out[1], out[2:]


def weight_back(one_blocks, one, two_blocks, two, n):
    rows, width = one_blocks[0].shape
    length = rows * len(one_blocks)
    heads, _, first = one[0].shape
    second = two[0].shape[2]
    part = width // n
    half = len(one_blocks)

    def summed(wide, cols, items):
        total, begin = None, 0
        for item in items:
            end = begin + item.shape[0]
            term = dot(wide[begin:end, cols], item[...], 0, 0)
            total = term if total is None else total + term
            begin = end
        return total.astype(bf16)

    def body(z, each_in, whole_in, each_out, whole_out, scratch):
        @pl.when(z == 0)
        def _():
            lay(scratch[0], whole_in[:half])
            lay(scratch[1], whole_in[half:])

        for s in range(n):
            cols = slice(s * part, (s + 1) * part)
            each_out[s][:, :first] = summed(scratch[0], cols, each_in[: len(one)])
            each_out[s][:, first:] = summed(scratch[1], cols, each_in[len(one) :])

    return run(
        body,
        heads,
        list(one) + list(two),
        list(one_blocks) + list(two_blocks),
        [shape((heads, part, first + second), bf16)] * n,
        [],
        [pltpu.VMEM((length, width), bf16)] * 2,
        2 * heads * length * width * (first + second),
    )


def norm_forward(values, got, vectors, bias, gain, shift):
    def body(z, each_in, whole_in, each_out, whole_out, scratch):
        start, rows = whole_in[:2]
        total = start[...] + rows[bias : bias + 1, :]
        for item in whole_in[2:]:
            total = total + item[...].astype(f32)
        whole_out[0][...] = total
        xhat, _ = norm_parts(total)
        normed = xhat * rows[gain : gain + 1, :] + rows[shift : shift + 1, :]
        whole_out[1][...] = normed.astype(bf16)

    shapes = [shape(values.shape, f32), shape(values.shape, bf16)]
    return run(body, 1, [], [values, vectors] + list(got), [], shapes)


def norm_back(values, gradient, got, vectors, gain):
    width = values.shape[1]

    def body(z, each_in, whole_in, each_out, whole_out, scratch):
        e = sum(item[...].astype(f32) for item in whole_in[3:])
        xhat, scale = norm_parts(whole_in[0][...])
        eg = e * whole_in[2][gain : gain + 1, :]
        back = scale * (
            eg
            - jnp.mean(eg, axis=-1, keepdims=True)
            - xhat * jnp.mean(eg * xhat, axis=-1, keepdims=True)
        )
        fresh = whole_in[1][...].astype(f32) + back
        whole_out[0][...] = fresh
        whole_out[1][...] = fresh.astype(bf16)
        whole_out[2][0:1, :] = jnp.sum(e * xhat, axis=0, keepdims=True)
        whole_out[2][1:2, :] = jnp.sum(e, axis=0, keepdims=True)
        whole_out[2][2:3, :] = jnp.sum(fresh, axis=0, keepdims=True)

    shapes = [shape(values.shape, f32), shape(values.shape, bf16), shape((3, width), f32)]
    return run(body, 1, [], [values, gradient, vectors] + list(got), [], shapes)


def turn_columns(array, turn, counts, inward):
    n_t, n_s = counts
    cut = array.shape[1] // (n_t * n_s)
    parts = [array[:, j * cut : (j + 1) * cut] for j in range(n_t * n_s)]
    index = turn[:, :cut]
    if inward:
        groups = flip_list([parts[s::n_s] for s in range(n_s)], index)
        return [part for group in groups for part in group]
    groups = flip_list([parts[k * n_t : (k + 1) * n_t] for k in range(n_s)], index)
    return [groups[s][t] for t in range(n_t) for s in range(n_s)]


def store_columns(target, parts):
    cut = parts[0].shape[1]
    for j, part in enumerate(parts):
        target[:, j * cut : (j + 1) * cut] = part.astype(target.dtype)


def first_norm(items, turn, counts):
    dims = items[0].shape

    def body(z, each_in, whole_in, each_out, whole_out, scratch):
        total = sum(item[...].astype(f32) for item in whole_in[1:])
        store_columns(whole_out[0], turn_columns(total, whole_in[0][...], counts, True))
        whole_out[1][...] = norm_parts(whole_out[0][...])[0].astype(bf16)

    return run(body, 1, [], [turn] + list(items), [], [shape(dims, f32), shape(dims, bf16)])


def turned_sum(items, turn, counts, inward, bias=None):
    dims = items[0].shape

    def body(z, each_in, whole_in, each_out, whole_out, scratch):
        count = len(whole_in) - (0 if bias is None else 1)
        total = sum(item[...].astype(f32) for item in whole_in[1:count])
        if bias is not None:
            total = total + whole_in[count][bias : bias + 1, :]
        store_columns(whole_out[0], turn_columns(total, whole_in[0][...], counts, inward))

    return run(body, 1, [], [turn] + list(items), [], [shape(dims, bf16)])[0]


def unpack(planes, turn, counts, width, layers, spare):
    n_t, n_s = counts
    heads, _, columns = planes[0].shape
    part, cut = width // n_s, width // (n_s * n_t)
    small = HD // (n_t * n_s)
    units = columns
    unit = units // (n_t * n_s)
    half = columns // 2

    def kernel(*refs):
        ex, index, outs = refs[:n_s], refs[n_s], refs[n_s + 1 :]
        vectors, qkv, up = outs[0], outs[1 : 1 + layers], outs[1 + layers :]
        for layer in range(layers):
            qkv[layer][...] = jnp.zeros_like(qkv[layer])
        for t in range(n_t):
            rows = slice(t * spare, (t + 1) * spare)
            for k in range(n_s):
                place = (k * n_t + t) * cut
                vectors[:, place : place + cut] = ex[k][0, rows, :cut].astype(f32)
            for head in range(heads):
                blocks = [ex[k][head, rows, half:].astype(f32) for k in range(n_s)]
                blocks = flip_list(blocks, index[:, :half])
                for s in range(n_s):
                    place = t * n_s + s
                    for layer in range(layers):
                        row = blocks[s][layer : layer + 1, :]
                        at = place * small
                        qkv[layer][head, :, at : at + small] = row[:, :small]
                        at += 2 * HD
                        qkv[layer][head, :, at : at + small] = row[:, small : 2 * small]
                        at = place * unit
                        up[layer][head, :, at : at + unit] = row[:, 2 * small : 2 * small + unit]

    block = pl.BlockSpec((heads, n_t * spare, columns), lambda i: (0, part // (n_t * spare), 0))
    shapes = [shape((spare, width), f32)]
    shapes += [shape((heads, 1, 3 * HD), f32)] * layers
    shapes += [shape((heads, 1, units), f32)] * layers

    def whole(dims):
        return pl.BlockSpec(dims, lambda i: (0,) * len(dims))

    out = pl.pallas_call(
        kernel,
        grid=(1,),
        in_specs=[block] * n_s + [whole(turn.shape)],
        out_specs=[whole(item.shape) for item in shapes],
        out_shape=shapes,
        compiler_params=pltpu.CompilerParams(vmem_limit_bytes=SMALL_LIMIT),
    )(*planes, turn)
    return out[0], out[1 : 1 + layers], out[1 + layers :]


def per_device(
    sizes,
    tokens,
    qkv_weight,
    dense_weight,
    up_weight,
    down_weight,
    first_gain,
    first_shift,
    query_bias,
    value_bias,
    dense_bias,
    second_gain,
    second_shift,
    up_bias,
    down_bias,
    cotangent,
):
    n_t, n_s, n_z = sizes
    seq_count, slice_len, width = tokens.shape
    assert seq_count == 1 and n_t == n_z
    d, c, z = (lax.axis_index(name) for name in (DP, SEQ, HEAD))
    rows = slice_len // n_t
    cut = qkv_weight.shape[1]
    part = cut * n_t
    heads = query_bias.shape[1]
    assert heads == n_t
    units = up_bias.shape[2] * n_t * n_s

    def spread_rows(array):
        return exchange(array.reshape(n_t, rows, width), DP)

    def own_rows(blocks):
        return lax.dynamic_index_in_dim(blocks, z, 0, False)

    def send_rows(array):
        return gather(array, DP, n_t)

    def in_halves(blocks):
        return [blocks]

    def send_sums(blocks):
        return deal(blocks, DP, n_t)

    def to_planes_of(array):
        return lax.all_gather(array, HEAD, axis=0, tiled=False)

    def send_output(planes):
        return exchange(planes, DP).reshape(1, slice_len, width)

    def packed_mixed(layer):
        qkv = qkv_weight[layer].reshape(cut, n_t, -1).transpose(1, 0, 2)
        dense = dense_weight[layer].reshape(n_t, -1, cut).transpose(0, 2, 1)
        return jnp.concatenate((qkv, dense), axis=2)

    def packed_feed(layer):
        up = up_weight[layer].reshape(cut, n_t, -1).transpose(1, 0, 2)
        down = down_weight[layer].reshape(n_t, -1, cut).transpose(0, 2, 1)
        return jnp.concatenate((up, down), axis=2)

    def to_planes(blocks):
        return exchange(blocks, DP).reshape(part, -1)

    def join(planes):
        return gather(planes, SEQ, n_s)

    counts = (n_t, n_s)
    turn = jnp.full((1, 128), c, jnp.int32)
    wide = jnp.concatenate(
        (first_gain, first_shift, dense_bias, second_gain, second_shift, down_bias), axis=0
    )
    tall = jnp.concatenate((query_bias, value_bias, up_bias), axis=2).transpose(1, 0, 2)
    columns, spare = 4 * HD, 16
    half = columns // 2
    wide = jnp.pad(wide, ((0, spare - 6 * LAYERS), (0, half - cut)))
    tall = jnp.pad(tall, ((0, 0), (0, spare - LAYERS), (0, half - tall.shape[2])))
    small = jnp.concatenate((jnp.broadcast_to(wide[None], (n_t, spare, half)), tall), axis=2)
    first = jnp.concatenate((packed_mixed(0), small.astype(bf16)), axis=1)
    feed_rows = jnp.pad(packed_feed(0), ((0, 0), (0, spare), (0, 0)))
    first = exchange(jnp.concatenate((first, feed_rows), axis=2), DP)
    second_shard = first[:, :cut, columns:].reshape(part, -1)
    first = first[:, :, :columns]
    first_shard = jnp.concatenate(
        (first[:, :cut].reshape(part, columns), first[:, cut:].reshape(-1, columns)), axis=0
    )
    messages = [to_planes_of(first_shard)]
    hidden, low = first_norm([own_rows(spread_rows(tokens[0]))], turn, counts)
    normed_one = send_rows(low)
    normed_one, second_shard = meet(normed_one, second_shard)
    messages.append(to_planes_of(second_shard))
    messages[0], normed_one = meet(messages[0], normed_one)
    mixed = join(messages[0])
    vectors, biases_qkv, biases_up = unpack(mixed, turn, counts, width, LAYERS, spare)
    tall_sizes = (HD, HD, units)

    def vector(kind, layer):
        return kind * LAYERS + layer

    qkv_columns = 3 * HD
    head_ids = jnp.arange(n_z, dtype=jnp.int32) * heads + d
    slopes = 2.0 ** (-8.0 * (head_ids + 1).astype(f32) / H)
    slopes = jnp.broadcast_to(slopes[:, None, None], (n_z, 1, 128))
    block_ids = (d ^ jnp.arange(n_t, dtype=jnp.int32)) * rows
    own_pos = (block_ids[:, None] + jnp.arange(rows, dtype=jnp.int32)[None]).reshape(-1)
    query_pos = (c * slice_len + own_pos).astype(f32)[:, None]
    others = (c ^ jnp.arange(n_s, dtype=jnp.int32)) * slice_len
    key_pos = (others[:, None] + own_pos[None]).astype(f32)[:, None, :]
    cot = cotangent[0]
    records = []
    for layer in range(LAYERS):
        if layer > 0:
            normed_one = send_rows(low)
            normed_one, messages[2 * layer] = meet(normed_one, messages[2 * layer])
            mixed = join(messages[2 * layer])
        affine = (vectors, vector(0, 0), vector(1, 0)) if layer == 0 else ()
        queries, both, normed_one = project(normed_one, mixed, biases_qkv[layer], *affine)
        both = gather(both, SEQ, n_s)
        if layer == 0:
            later = jnp.concatenate((packed_mixed(1), packed_feed(1)), axis=2)
            both, later = meet(both, later)
            later = to_planes(later)
        else:
            both, cot_rows = meet(both, cot_rows)
            cot_rows = send_rows(cot_rows)
        context, logs, out = attend(queries, both, mixed, slopes, key_pos, query_pos, n_t, width)
        if layer == 0:
            out, later = meet(out, later)
        else:
            out, cot_rows = meet(out, cot_rows)
        got = send_sums(out)
        got, messages[2 * layer + 1] = meet(got, messages[2 * layer + 1])
        feed = join(messages[2 * layer + 1])
        if layer == 0:
            got, later = meet(got, later)
            messages.append(to_planes_of(later[:, :columns]))
            messages.append(to_planes_of(later[:, columns:]))
        hidden_mid, low = norm_forward(
            hidden, got, vectors, vector(2, layer), vector(3, layer), vector(4, layer)
        )
        normed_two = send_rows(low)
        if layer == 0:
            normed_two, cot_rows = meet(normed_two, cot)
            cot_rows = spread_rows(cot_rows)
        halves = [feed_forward(part, feed, biases_up[layer]) for part in in_halves(normed_two)]
        pre_up, activation, out = (list(item) for item in zip(*halves))
        out = [block for part in out for block in part]
        got = send_sums(out)
        if layer == 0:
            got, cot_rows = meet(got, turned_sum([own_rows(cot_rows)], turn, counts, True))
        records.append(
            (
                (mixed, feed),
                (hidden, hidden_mid, normed_one, normed_two),
                (queries, both, logs, context, pre_up, activation),
            )
        )
        if layer + 1 < LAYERS:
            hidden, low = norm_forward(
                hidden_mid,
                got,
                vectors,
                vector(5, layer),
                vector(0, layer + 1),
                vector(1, layer + 1),
            )

    last_bias = vector(5, LAYERS - 1)
    output_low = turned_sum([hidden_mid] + list(got) + [vectors], turn, counts, False, last_bias)

    gradient = cot_rows[0]
    grad_low = cot_rows
    down_bias_grad = jnp.sum(gradient, axis=0, keepdims=True, dtype=f32)
    wide_grads = [None] * LAYERS
    tall_grads = [None] * LAYERS

    def core_sum(blocks):
        return sum_blocks(blocks, SEQ, n_s).astype(bf16)

    def head_sum(mine):
        return lax.psum_scatter(mine, HEAD, scatter_dimension=0, tiled=False)

    def send_shares(mine):
        return exchange(mine.reshape(n_t, cut, -1), DP)

    feed_shares = [None] * LAYERS
    mixed_shares = [None] * LAYERS
    feed_sums = [None] * LAYERS
    mixed_sums = [None] * LAYERS
    for layer in reversed(range(LAYERS)):
        (
            (mixed, feed),
            (hidden, hidden_mid, normed_one, normed_two),
            (queries, both, logs, context, pre_up, activation),
        ) = records[layer]
        last = layer == LAYERS - 1
        halves = [
            feed_back(part, feed, kept) for part, kept in zip(in_halves(grad_low), pre_up)
        ]
        pre_grad, up_bias_grad, out = (list(item) for item in zip(*halves))
        got = send_sums([block for part in out for block in part])
        up_bias_grad = functools.reduce(jnp.add, up_bias_grad)
        feed_grad = weight_back(normed_two, pre_grad, grad_low, activation, n_s)
        if last:
            got, feed_grad, output_low = meet(got, feed_grad, output_low)
            output_planes = to_planes_of(output_low)
        else:
            got, feed_grad, mixed_sums[1] = meet(got, feed_grad, mixed_sums[1])
        mid_grad, low, sums_two = norm_back(
            hidden_mid, gradient, got, vectors, vector(3, layer)
        )
        mid_low = send_rows(low)
        if last:
            mid_low, mine = meet(mid_low, core_sum(feed_grad))
        else:
            mid_low, mine, output_planes = meet(mid_low, core_sum(feed_grad), output_planes)
        feed_sums[layer] = head_sum(mine)
        query_grad, both_grads = attend_back(
            mid_low, queries, both, mixed, context, logs, slopes, key_pos, query_pos
        )
        if not last:
            both_grads, output = meet(both_grads, send_output(output_planes))
        got = deal(both_grads, SEQ, n_s)
        joined, qkv_sums, out = project_back(query_grad, got, mixed, n_t, width)
        got = send_sums(out)
        mixed_grad = weight_back(normed_one, [joined], mid_low, [context], n_s)
        if last:
            got, mixed_grad, output_planes = meet(got, mixed_grad, output_planes)
        else:
            got, feed_sums[0] = meet(got, feed_sums[0])
            mixed_sums[layer] = head_sum(core_sum(mixed_grad))
        gradient, low, sums_one = norm_back(
            hidden, mid_grad, got, vectors, vector(0, layer)
        )
        if layer > 0:
            grad_low, mine, feed_sums[layer] = meet(
                send_rows(low), core_sum(mixed_grad), feed_sums[layer]
            )
            mixed_sums[layer] = head_sum(mine)
        wide_grads[layer] = jnp.stack(
            (
                sums_one[0],
                sums_one[1],
                sums_two[2],
                sums_two[0],
                sums_two[1],
                down_bias_grad[0],
            )
        )
        down_bias_grad = sums_one[2:3]
        tall_grads[layer] = jnp.concatenate(
            (qkv_sums[:, 0, :HD], qkv_sums[:, 0, 2 * HD :], up_bias_grad[:, 0]), axis=1
        )

    low_outer = turned_sum([low], turn, counts, False)
    low_outer, mixed_sums[1], feed_sums[1] = meet(low_outer, mixed_sums[1], feed_sums[1])
    feed_shares[1] = send_shares(feed_sums[1])
    mixed_shares[1] = send_shares(mixed_sums[1])
    low_outer, mixed_sums[0], feed_shares[1], mixed_shares[1] = meet(
        low_outer, mixed_sums[0], feed_shares[1], mixed_shares[1]
    )
    tokens_planes = to_planes_of(low_outer)
    mixed_sums[0], feed_sums[0] = meet(mixed_sums[0], feed_sums[0])
    feed_shares[0] = send_shares(feed_sums[0])
    mixed_shares[0] = send_shares(mixed_sums[0])
    tokens_planes, feed_shares[0], mixed_shares[0] = meet(
        tokens_planes, feed_shares[0], mixed_shares[0]
    )
    tokens_grad = send_output(tokens_planes).astype(f32)

    def fold(arrays, name, size):
        total = arrays[0]
        for step in range(1, size):
            total = total + swap(arrays[step], name, size, step)
        return total

    wide = jnp.stack(wide_grads).reshape(LAYERS * 6, n_s, n_t, cut)
    pieces, begin = [], 0
    tall = jnp.stack(tall_grads)
    for size in tall_sizes:
        piece = tall[:, :, begin : begin + size]
        begin += size
        piece = piece.reshape(LAYERS, n_z, n_t, n_s, size // (n_t * n_s))
        pieces.append(flip(flip(piece, c, 3), z, 1))
    tall = jnp.concatenate(
        [piece.transpose(3, 1, 2, 0, 4).reshape(n_s, n_z, n_t, -1) for piece in pieces], axis=3
    )
    wide = wide.transpose(1, 2, 0, 3).reshape(n_s, n_t, -1)
    n_wide = wide.shape[2]
    wide = jnp.broadcast_to(wide[:, None], (n_s, n_z) + wide.shape[1:])
    joint = jnp.concatenate((wide, tall), axis=3)
    joint = fold([joint[step] for step in range(n_s)], SEQ, n_s)
    joint = fold([joint[step] for step in range(n_z)], HEAD, n_z)
    joint = flip(joint, d)
    got = deal([joint[step] for step in range(n_t)], DP, n_t)
    wide = functools.reduce(jnp.add, [item[:n_wide] for item in got])
    wide = wide.reshape(LAYERS, 6, cut)
    tall = flip(jnp.stack([item[n_wide:] for item in got]), d)
    outs, begin = [], 0
    for size in tall_sizes:
        size = size // (n_t * n_s)
        piece = tall[:, begin : begin + LAYERS * size].reshape(n_t, LAYERS, size)
        begin += LAYERS * size
        outs.append(piece.transpose(1, 0, 2))
    query_bias_grad, value_bias_grad, up_bias_grad = outs
    def rows_first(shares, begin, end):
        parts = [share[:, :, begin:end].transpose(1, 0, 2).reshape(cut, -1) for share in shares]
        return jnp.stack(parts).astype(f32)

    def columns_first(shares, begin, end):
        parts = [share[:, :, begin:end].transpose(0, 2, 1).reshape(-1, cut) for share in shares]
        return jnp.stack(parts).astype(f32)

    qkv_grad = rows_first(mixed_shares, 0, qkv_columns)
    dense_grad = columns_first(mixed_shares, qkv_columns, columns)
    up_grad = rows_first(feed_shares, 0, units)
    down_grad = columns_first(feed_shares, units, 2 * units)
    return (
        output,
        tokens_grad,
        qkv_grad,
        dense_grad,
        up_grad,
        down_grad,
        wide[:, 0],
        wide[:, 1],
        query_bias_grad,
        value_bias_grad,
        wide[:, 2],
        wide[:, 3],
        wide[:, 4],
        up_bias_grad,
        wide[:, 5],
    )


def solution(mesh):
    sizes = tuple(mesh.shape[name] for name in (DP, SEQ, HEAD))
    rows = P(DP, SEQ, None)
    tall = P(None, (DP, SEQ), HEAD)
    flat = P(None, HEAD, (DP, SEQ))
    vector = P(None, (DP, SEQ))
    params = (
        tall,
        flat,
        tall,
        flat,
        vector,
        vector,
        flat,
        flat,
        vector,
        vector,
        vector,
        flat,
        vector,
    )
    return jax.shard_map(
        functools.partial(per_device, sizes),
        mesh=mesh,
        in_specs=(rows,) + params + (rows,),
        out_specs=(rows, rows) + params,
        check_vma=False,
    )
```
